128 devices in a mesh: gx: 16 (over y, x), gy: 8 (over z, core).
Axes of the slice: x: 4, y: 4, z: 4, core: 2. Of those that a mesh axis runs over, the one named last changes fastest.
Arguments:
- nodes: bfloat16 [262144, 256], P(('gx', 'gy')), may hold values from -6 to 6
- boundary_rows: int32 [16384], P(('gx', 'gy')), may hold values from 0 to 2047
- edge_source: int32 [4096, 128], P(('gx', 'gy')), may hold values from 0 to 2559
- edge_target: int32 [4096, 128], P(('gx', 'gy')), may hold values from 0 to 2047
- edge_mask: int32 [4096, 128], P(('gx', 'gy')), may hold values 0 or 1
- segment_ids: int32 [262144], P(('gx', 'gy')), may hold values from 0 to 511
- w_first: bfloat16 [512, 512], replicated, may hold values from -0.25 to 0.25
- b_first: float32 [512], replicated, may hold values from -3 to 3
- w_second: bfloat16 [512, 256], replicated, may hold values from -0.25 to 0.25
- cotangent: bfloat16 [4096, 256], P(('gx', 'gy')), may hold values from -6 to 6
Outputs:
- pooled: bfloat16 [4096, 256], P(('gx', 'gy'))
- grad_nodes: bfloat16 [262144, 256], P(('gx', 'gy'))
- grad_first: float32 [512, 512], replicated
- grad_bias: float32 [512], replicated
- grad_second: float32 [512, 256], replicated
The draws below stay inside these ranges and needn't reach their ends.
All inputs are finite; a program needn't handle non-finite values. No bound on the sum of `edge_mask` on one device may be relied on, other than what follows from the above.
Results may differ from the reference program's by a relative error of at most 0.0043.
Values may be sent and summed in bfloat16 or wider, within the bound.
A program may use at most 128 MiB of HBM per device.

```python
import jax
import jax.numpy as jnp
from jax import lax

F = 256
HID = 512
EDGE_BLOCK = 128
SEGROWS = 32
NODE_DEV = 2048
BND = 128
EB = 32
NODES = 262144
BOUNDARY = 16384
BLOCKS = 4096
EDGES = 524288
SEGS = 4096
N_GX = 16
N_GY = 8


def plant(entries, own_key, low, high):
    spot = [jax.random.randint(jax.random.fold_in(own_key, axis), (), 0, length) for axis, length in enumerate(entries.shape)]
    main_axis = entries.shape.index(max(entries.shape))
    neighbour = spot[:main_axis] + [(spot[main_axis] + 1) % entries.shape[main_axis]] + spot[main_axis + 1:]
    return entries.at[tuple(spot)].set(low).at[tuple(neighbour)].set(high)


def level_of(rng, dims, split, smallest, largest):
    gain = 1.0
    for position, shards_of in split:
        draws = jax.random.uniform(jax.random.fold_in(jax.random.fold_in(rng, 6), position), (shards_of,), jnp.float32, smallest / len(split), largest / len(split))
        gain = gain * jnp.repeat(jnp.exp(draws), dims[position] // shards_of).reshape((-1,) + (1,) * (len(dims) - 1 - position))
    return gain


def normal_values(own_key, extent, width, bound, pieces=(), kind=jnp.bfloat16):
    gain = level_of(own_key, extent, pieces, -0.22, 0.18) if pieces else 1.0
    entries = jax.random.normal(own_key, extent, jnp.float32) * width * gain
    return jnp.minimum(jnp.maximum(entries, -bound), bound).astype(kind)


def setup_inputs(seed: int = 0) -> dict:
    seeds = jax.random.split(jax.random.key(seed), 11)
    nodes = normal_values(seeds[0], (NODES, F), 1.0, 6.0, ((0, 128),))
    boundary_rows = plant(jax.random.randint(seeds[1], (BOUNDARY,), 0, NODE_DEV), jax.random.fold_in(seeds[1], 1), 0, NODE_DEV - 1).astype(jnp.int32)
    edge_source = plant(jax.random.randint(seeds[2], (BLOCKS, EDGE_BLOCK), 0, NODE_DEV + 4 * BND), jax.random.fold_in(seeds[2], 1), 0, (NODE_DEV + 4 * BND) - 1).astype(jnp.int32)
    edge_target = plant(jax.random.randint(seeds[3], (BLOCKS, EDGE_BLOCK), 0, NODE_DEV), jax.random.fold_in(seeds[3], 1), 0, NODE_DEV - 1).astype(jnp.int32)
    edge_mask = plant((jax.random.randint(seeds[4], (BLOCKS, EDGE_BLOCK), 0, 4) < 3).astype(jnp.int32), jax.random.fold_in(seeds[4], 1), 0, 1)
    segment_ids = plant(jax.random.randint(seeds[5], (NODES,), 0, N_GX * SEGROWS), jax.random.fold_in(seeds[5], 1), 0, (N_GX * SEGROWS) - 1).astype(jnp.int32)
    w_first = normal_values(seeds[6], (2 * F, HID), (2 * F) ** -0.5, 0.25)
    b_first = normal_values(seeds[7], (HID,), 0.5, 3.0, (), jnp.float32)
    w_second = normal_values(seeds[8], (HID, F), HID ** -0.5, 0.25)
    cotangent = normal_values(seeds[9], (SEGS, F), 1.0, 6.0, ((0, 128),))
    return dict(nodes=nodes, boundary_rows=boundary_rows, edge_source=edge_source, edge_target=edge_target, edge_mask=edge_mask, segment_ids=segment_ids, w_first=w_first, b_first=b_first, w_second=w_second, cotangent=cotangent)


def reference(nodes, boundary_rows, edge_source, edge_target, edge_mask, segment_ids, w_first, b_first, w_second, cotangent):
    features = nodes.shape[1]
    devices = N_GX * N_GY
    table_rows = NODE_DEV + 4 * BND
    local_rows = nodes.reshape(N_GX, N_GY, NODE_DEV, features)
    picks_all = boundary_rows.reshape(N_GX, N_GY, BND)
    boundary = jax.vmap(jax.vmap(lambda brick_rows, picked: brick_rows[picked]))(local_rows, picks_all)
    zero_x = jnp.zeros_like(boundary[:1])
    zero_y = jnp.zeros_like(boundary[:, :1])
    lower_x = jnp.concatenate([zero_x, boundary[:-1]], 0)
    upper_x = jnp.concatenate([boundary[1:], zero_x], 0)
    lower_y = jnp.concatenate([zero_y, boundary[:, :-1]], 1)
    upper_y = jnp.concatenate([boundary[:, 1:], zero_y], 1)
    row_table = jnp.concatenate([local_rows, lower_x, upper_x, lower_y, upper_y], 2).reshape(devices, table_rows, features)
    sources = edge_source.reshape(devices, EB * EDGE_BLOCK)
    targets = edge_target.reshape(devices, EB * EDGE_BLOCK)
    lives = edge_mask.reshape(devices, EB * EDGE_BLOCK)

    def edge_forward(table_one, source_ids, target_ids, live_mask):
        inputs = jnp.concatenate([table_one[source_ids], table_one[target_ids]], 1)
        preact = jnp.dot(inputs, w_first, preferred_element_type=jnp.float32) + b_first
        hidden = jax.nn.gelu(preact).astype(jnp.bfloat16)
        message = (jnp.dot(hidden, w_second, preferred_element_type=jnp.float32) * live_mask[:, None].astype(jnp.float32)).astype(jnp.bfloat16)
        return (inputs, preact, hidden, message)

    def forward_one(packed):
        table_one, source_ids, target_ids, live_mask, own_rows = packed
        inputs, preact, hidden, message = edge_forward(table_one, source_ids, target_ids, live_mask)
        incoming = jax.ops.segment_sum(message.astype(jnp.float32), target_ids, NODE_DEV)
        return (own_rows.astype(jnp.float32) + incoming).astype(jnp.bfloat16)
    updated = lax.map(forward_one, (row_table, sources, targets, lives, local_rows.reshape(devices, NODE_DEV, features)))
    seg_grid = segment_ids.reshape(N_GX, N_GY, NODE_DEV)
    offsets = (jnp.arange(N_GY, dtype=jnp.int32) * (N_GX * SEGROWS))[None, :, None]
    global_ids = (seg_grid + offsets).astype(jnp.int32).reshape(-1)
    sums = jax.ops.segment_sum(updated.reshape(-1, features).astype(jnp.float32), global_ids, N_GY * N_GX * SEGROWS)
    pooled = sums.reshape(N_GY, N_GX, SEGROWS, features).transpose(1, 0, 2, 3).reshape(-1, features).astype(jnp.bfloat16)
    line_rows = cotangent.reshape(N_GX, N_GY, SEGROWS, features).transpose(1, 0, 2, 3).reshape(-1, features)
    grad_updated = line_rows[global_ids].astype(jnp.float32).reshape(devices, NODE_DEV, features)

    def backward_one(packed):
        table_one, source_ids, target_ids, live_mask, grad_rows = packed
        inputs, preact, hidden, message = edge_forward(table_one, source_ids, target_ids, live_mask)
        grad_message = (grad_rows[target_ids] * live_mask[:, None].astype(jnp.float32)).astype(jnp.bfloat16)
        grad_second = jnp.dot(hidden.T, grad_message, preferred_element_type=jnp.float32)
        grad_hidden = jnp.dot(grad_message, w_second.T, preferred_element_type=jnp.float32)
        unused, pull_back = jax.vjp(jax.nn.gelu, preact)
        grad_pre = pull_back(grad_hidden)[0].astype(jnp.bfloat16)
        grad_bias = lax.optimization_barrier(jnp.sum(grad_pre.astype(jnp.float32), 0))
        grad_first = jnp.dot(inputs.T, grad_pre, preferred_element_type=jnp.float32)
        grad_inputs = jnp.dot(grad_pre, w_first.T, preferred_element_type=jnp.float32).astype(jnp.bfloat16).astype(jnp.float32)
        grad_table = jax.ops.segment_sum(grad_inputs[:, :features], source_ids, table_rows) + jax.ops.segment_sum(grad_inputs[:, features:], target_ids, table_rows)
        return (grad_table, grad_first, grad_bias, grad_second)
    grad_table, first_terms, bias_terms, second_terms = lax.map(backward_one, (row_table, sources, targets, lives, grad_updated))
    grad_grid = grad_table.reshape(N_GX, N_GY, table_rows, features)
    own_part = grad_grid[:, :, :NODE_DEV]

    def slot_of(number):
        return grad_grid[:, :, NODE_DEV + number * BND:NODE_DEV + (number + 1) * BND]
    gzero_x = jnp.zeros_like(slot_of(0)[:1])
    gzero_y = jnp.zeros_like(slot_of(0)[:, :1])
    to_boundary = jnp.concatenate([slot_of(0)[1:], gzero_x], 0) + jnp.concatenate([gzero_x, slot_of(1)[:-1]], 0)
    to_boundary = to_boundary + jnp.concatenate([slot_of(2)[:, 1:], gzero_y], 1) + jnp.concatenate([gzero_y, slot_of(3)[:, :-1]], 1)
    returned = jax.vmap(jax.vmap(lambda values, picked: jax.ops.segment_sum(values, picked, NODE_DEV)))(to_boundary, picks_all)
    grad_nodes = (grad_updated.reshape(N_GX, N_GY, NODE_DEV, features) + own_part + returned).reshape(-1, features).astype(jnp.bfloat16)
    edge_scale = 1.0 / jnp.sqrt(jnp.float32(EDGES))
    return (pooled, grad_nodes, lax.optimization_barrier(jnp.sum(first_terms, 0)) * edge_scale, lax.optimization_barrier(jnp.sum(bias_terms, 0)) * edge_scale, lax.optimization_barrier(jnp.sum(second_terms, 0)) * edge_scale)
```

```python
import functools

import jax
import jax.numpy as jnp
from jax import lax
from jax.experimental import pallas as pl
from jax.experimental.pallas import tpu as pltpu
from jax.sharding import PartitionSpec as P

MESH = pl.DeviceIdType.MESH
BF = jnp.bfloat16
F32 = jnp.float32
N = 2048
NB = 128
HALO = 4 * NB
F = 256
H = 512
E = 4096
SEG = 512
SR = 32
GX = 16
GY = 8
W = 1024
CH = 48
PW = 784
HW = H // 2
NT = (((1,), (1,)), ((), ()))


def dot(a, b):
    return jnp.dot(a, b, preferred_element_type=F32)


def dnt(a, b):
    return lax.dot_general(a, b, NT, preferred_element_type=F32)


def one_hot(row, first, count):
    rows = lax.broadcasted_iota(jnp.int32, (count, row.shape[1]), 0)
    return jnp.where(rows == row - first, 1.0, 0.0).astype(BF)


def id_row(ref, first, count):
    return jnp.concatenate([ref[pl.ds(first + i, 1), :] for i in range(count)], axis=1)


def eye(size):
    a = lax.broadcasted_iota(jnp.int32, (size, size), 0)
    b = lax.broadcasted_iota(jnp.int32, (size, size), 1)
    return jnp.where(a == b, 1.0, 0.0).astype(BF)


def split(value):
    high = value.astype(BF)
    return high, (value - high.astype(F32)).astype(BF)


def kernel(
    nodes,
    brows,
    src,
    tgt,
    mask,
    segs,
    w1,
    b1,
    w2,
    cot,
    pooled,
    gnodes,
    gw,
    tt,
    w1t,
    bcol,
    bnd,
    hrecv,
    line,
    line_t,
    xt,
    mseg,
    hid,
    gp,
    gi,
    pwf,
    pws,
    cbuf,
    csum,
    rsb,
    rsbias,
    zb,
    zbias,
    ag,
    psend,
    precv,
    gslot,
    gret,
    acc,
    h_s,
    h_r,
    c_s,
    c_r,
    p_s,
    p_r,
    g_s,
    g_r,
    core_s,
    core_r,
    rs_s,
    rs_r,
    rb_s,
    rb_r,
    z_s,
    z_r,
    zb_s,
    zb_r,
    ag_s,
    ag_r,
    agb_s,
    agb_r,
    fw_s,
    fw_r,
):
    me = lax.axis_index("gx")
    my = lax.axis_index("gy")
    core = lax.rem(my, 2)
    z = lax.div(my, 2)
    sib = my + 1 - 2 * core

    barrier = pltpu.get_barrier_semaphore()
    for d in range(1, GX):
        pl.semaphore_signal(
            barrier, inc=1, device_id={"gx": lax.rem(me + d, GX)}, device_id_type=MESH
        )
    for d in range(1, GY):
        pl.semaphore_signal(
            barrier, inc=1, device_id={"gy": lax.rem(my + d, GY)}, device_id_type=MESH
        )

    def remote(source, target, send, receive, device):
        return pltpu.make_async_remote_copy(
            src_ref=source,
            dst_ref=target,
            send_sem=send,
            recv_sem=receive,
            device_id=device,
            device_id_type=MESH,
        )

    unit = eye(F)
    tt[:, :N] = dnt(unit, nodes[...]).astype(BF)
    bnd[...] = dot(tt[:, :N], one_hot(brows[...], 0, N)).astype(BF)
    line[pl.ds(me, 1)] = cot[...][None]

    pl.semaphore_wait(barrier, GX - 1 + GY - 1)

    there = (me > 0, me < GX - 1, my > 0, my < GY - 1)
    halo = (
        remote(bnd, hrecv.at[1], h_s.at[1], h_r.at[1], {"gx": lax.rem(me + GX - 1, GX)}),
        remote(bnd, hrecv.at[0], h_s.at[0], h_r.at[0], {"gx": lax.rem(me + 1, GX)}),
        remote(bnd, hrecv.at[3], h_s.at[3], h_r.at[3], {"gy": lax.rem(my + GY - 1, GY)}),
        remote(bnd, hrecv.at[2], h_s.at[2], h_r.at[2], {"gy": lax.rem(my + 1, GY)}),
    )
    for k in range(4):
        pl.when(there[k])(halo[k].start)
    cots = [
        remote(
            cot,
            line.at[me],
            c_s.at[d],
            c_r.at[d],
            {"gx": lax.rem(me + d, GX)},
        )
        for d in range(1, GX)
    ]
    for copy in cots:
        copy.start()

    for i in range(2):
        for j in range(2):
            w1t[j * F : (j + 1) * F, i * F : (i + 1) * F] = dnt(
                unit, w1[i * F : (i + 1) * F, j * F : (j + 1) * F]
            ).astype(BF)
    bcol[...] = jnp.broadcast_to(
        jnp.transpose(jnp.broadcast_to(b1[...], (8, H)))[:, :1], (H, 128)
    )
    xt[2 * F :, :] = jnp.ones((16, E), BF)
    seg_ids = segs[...]
    seg_parts = jnp.concatenate(
        [
            jnp.bitwise_and(seg_ids, 255).astype(F32).astype(BF),
            jnp.right_shift(seg_ids, 8).astype(F32).astype(BF),
        ],
        axis=0,
    )

    def block(b, width=W):
        return pl.ds(pl.multiple_of(b * width, width), width)

    def gather(b, carry):
        targets = id_row(tgt, b * 8, 8)
        sources = id_row(src, b * 8, 8)
        live = id_row(mask, b * 8, 8)
        low = one_hot(jnp.bitwise_and(targets, 127), 0, 128)
        found = dot(seg_parts, low)
        found = found[:16] + 256.0 * found[16:]
        high = lax.broadcasted_iota(jnp.int32, (16, W), 0) == jnp.right_shift(targets, 7)
        segment = jnp.sum(jnp.where(high, found, 0.0), axis=0, keepdims=True)
        segment = jnp.where(live > 0, segment, -1.0).astype(jnp.int32)
        mseg[:, block(b)] = jnp.broadcast_to(segment, (8, W))
        xt[F : 2 * F, block(b)] = dot(tt[:, :N], one_hot(targets, 0, N)).astype(BF)
        xt[:F, block(b)] = dot(tt[:, :N], one_hot(sources, 0, N)).astype(BF)
        return carry

    lax.fori_loop(0, E // W, gather, 0)

    for k, coming in enumerate((halo[1], halo[0], halo[3], halo[2])):
        pl.when(there[k])(coming.wait_recv)

        @pl.when(jnp.logical_not(there[k]))
        def _(k=k):
            hrecv[k] = jnp.zeros((F, NB), BF)

        tt[:, N + k * NB : N + (k + 1) * NB] = hrecv[k]
    for copy in cots:
        copy.wait_recv()
    lines = jnp.concatenate([line[g] for g in range(GX)], axis=0)
    line_t[...] = dnt(unit, lines).astype(BF)

    def edges(b, carry):
        sources = id_row(src, b * 8, 8)
        xt[:F, block(b)] = (
            xt[:F, block(b)].astype(F32) + dot(tt[:, N:], one_hot(sources, N, HALO))
        ).astype(BF)
        chosen = one_hot(mseg[:1, block(b)], 0, SEG)
        gm = dot(line_t[...], chosen).astype(BF)
        bias = jnp.concatenate([bcol[...]] * (W // 128), axis=1)
        x = dot(w1t[...], xt[: 2 * F, block(b)]) + bias
        gh = dot(w2[...], gm)
        square = x * x
        t = jnp.tanh(x * (0.7978845608028654 + 0.035677408136300125 * square))
        half = 0.5 + 0.5 * t
        hid[:, block(b)] = (x * half).astype(BF)
        slope = half + (0.5 * x) * (1.0 - t * t) * (
            0.7978845608028654 + 0.10703222440890037 * square
        )
        gp[:, block(b)] = (gh * slope).astype(BF)
        return carry

    lax.fori_loop(0, E // W, edges, 0)

    w2v = w2[...]

    def segment_sums(b, carry):
        first = b * 256
        edge_hot = one_hot(mseg[:1, :], first, 256)
        high, low = split(dnt(edge_hot, hid[...]))
        node_hot = one_hot(id_row(segs, 0, N // 128), first, 256)
        part = dot(high, w2v) + dot(low, w2v) + dot(node_hot, nodes[...])
        for i in range(8):
            psend[b * 8 + i] = part[i * SR : (i + 1) * SR]
        lines_t = line_t[:, block(b, 256)]
        add = dot(lines_t, high) + dot(lines_t, low)
        for c in range(2):
            pwf[c, 512:768, :] = pwf[c, 512:768, :] + add[:, c * HW : (c + 1) * HW]
        return carry

    pwf[:, 512:768, :] = jnp.zeros((2, 256, HW), F32)
    lax.fori_loop(0, SEG // 256, segment_sums, 0)
    pools = [
        remote(
            psend.at[lax.rem(me + d, GX)],
            precv.at[d],
            p_s.at[d],
            p_r.at[d],
            {"gx": lax.rem(me + d, GX)},
        )
        for d in range(1, GX)
    ]
    for copy in pools:
        copy.start()

    for c in range(2):
        first = dnt(xt[...], gp[c * HW : (c + 1) * HW, :])
        pwf[c, 0:512, :] = first[:512]
        pwf[c, 768:784, :] = first[512:]
    for c in range(2):
        pws[c] = pwf[c].astype(BF)
    pair = remote(pws.at[1 - core], cbuf, core_s, core_r, {"gy": sib})
    pair.start()

    def input_grads(b, carry):
        gi[:, block(b)] = dot(w1[...], gp[:, block(b)]).astype(BF)
        return carry

    lax.fori_loop(0, E // W, input_grads, 0)

    pair.wait_recv()
    csum[...] = (pwf[core] + cbuf[...].astype(F32)).astype(BF)

    def rows_of(member):
        return pl.ds(pl.multiple_of(member * CH, 16), CH)

    scatter = []
    for d in range(1, GX):
        to = lax.rem(me + d, GX)
        scatter.append(
            remote(csum.at[rows_of(to)], rsb.at[d], rs_s.at[d], rs_r.at[d], {"gx": to})
        )
        scatter[-1].start()
    bias_rows = csum.at[pl.ds(768, 16)]
    bias_scatter = [
        remote(bias_rows, rsbias.at[d], rb_s.at[d], rb_r.at[d], {"gx": lax.rem(me + d, GX)})
        for d in range(1, GX)
    ]
    for d in range(1, GX):
        pl.when(me + d == GX)(bias_scatter[d - 1].start)

    all_src = id_row(src, 0, 32)
    slots = dnt(one_hot(all_src, N, HALO), gi[:F, :])
    for k in range(4):
        gslot[k] = slots[k * NB : (k + 1) * NB].astype(BF)
    back = (
        remote(gslot.at[0], gret.at[0], g_s.at[0], g_r.at[0], {"gx": lax.rem(me + GX - 1, GX)}),
        remote(gslot.at[1], gret.at[1], g_s.at[1], g_r.at[1], {"gx": lax.rem(me + 1, GX)}),
        remote(gslot.at[2], gret.at[2], g_s.at[2], g_r.at[2], {"gy": lax.rem(my + GY - 1, GY)}),
        remote(gslot.at[3], gret.at[3], g_s.at[3], g_r.at[3], {"gy": lax.rem(my + 1, GY)}),
    )
    for k in range(4):
        pl.when(there[k])(back[k].start)

    seg_cols = jnp.transpose(segs[...].astype(F32)).astype(jnp.int32)

    def own(b, carry):
        first = b * 512
        s = dnt(one_hot(id_row(src, 0, 32), first, 512), gi[:F, :])
        t = dnt(one_hot(id_row(tgt, 0, 32), first, 512), gi[F:, :])
        acc[block(b, 512), :] = s + t
        return carry

    lax.fori_loop(0, 2, own, 0)

    for copy in scatter:
        copy.wait_recv()
    total = csum[rows_of(me), :].astype(F32)
    for d in range(1, GX):
        total = total + rsb[d].astype(F32)
    zb[pl.ds(z, 1)] = total[None]
    over_z = []
    for d in range(1, 4):
        over_z.append(
            remote(
                zb.at[z], zb.at[z], z_s.at[d], z_r.at[d], {"gy": lax.rem(my + 2 * d, GY)}
            )
        )
        over_z[-1].start()
    bias_z = [
        remote(zbias.at[z], zbias.at[z], zb_s.at[d], zb_r.at[d], {"gy": lax.rem(my + 2 * d, GY)})
        for d in range(1, 4)
    ]

    @pl.when(me == 0)
    def _():
        for copy in bias_scatter:
            copy.wait_recv()
        sums = csum[768:784, :].astype(F32)
        for d in range(1, GX):
            sums = sums + rsbias[d].astype(F32)
        zbias[pl.ds(z, 1)] = sums[None]
        for copy in bias_z:
            copy.start()

    lax.fori_loop(2, 3, own, 0)

    for copy in over_z:
        copy.wait_recv()
    total = (zb[0] + zb[1]) + (zb[2] + zb[3])
    ag[pl.ds(core, 1), rows_of(me), :] = total.astype(BF)[None]
    gathers = []
    for d in range(1, GX):
        to = lax.rem(me + d, GX)
        place = ag.at[core, rows_of(me)]
        gathers.append(remote(place, place, ag_s.at[d], ag_r.at[d], {"gx": to}))
        gathers[-1].start()
    place = ag.at[core, rows_of(me)]
    forwards = [remote(place, place, fw_s.at[0], fw_r.at[0], {"gy": sib})]
    forwards[0].start()
    bias_place = ag.at[core, pl.ds(768, 16)]
    bias_gathers = [
        remote(
            bias_place, bias_place, agb_s.at[d], agb_r.at[d], {"gx": lax.rem(me + d, GX)}
        )
        for d in range(1, GX)
    ]

    @pl.when(me == 0)
    def _():
        for copy in bias_z:
            copy.wait_recv()
        sums = (zbias[0] + zbias[1]) + (zbias[2] + zbias[3])
        ag[pl.ds(core, 1), 768:784, :] = sums.astype(BF)[None]
        for copy in bias_gathers:
            copy.start()

    lax.fori_loop(3, 4, own, 0)

    ret = jnp.zeros((NB, F), F32)
    for k, here in enumerate((there[1], there[0], there[3], there[2])):
        pl.when(here)(back[k].wait_recv)

        @pl.when(jnp.logical_not(here))
        def _(k=k):
            gret[k] = jnp.zeros((NB, F), BF)

        ret = ret + gret[k].astype(F32)
    ret_parts = jnp.concatenate(split(ret), axis=0)
    lines = jnp.concatenate([line[g] for g in range(GX)], axis=0)
    for r in range(N // 128):
        rows = slice(r * 128, (r + 1) * 128)
        seg_hot = jnp.where(
            lax.broadcasted_iota(jnp.int32, (128, SEG), 1) == seg_cols[:, r : r + 1], 1.0, 0.0
        ).astype(BF)
        place_hot = one_hot(brows[...], r * 128, 128)
        place_hot = jnp.concatenate([place_hot, place_hot], axis=1)
        gnodes[rows, :] = (acc[rows, :] + dot(seg_hot, lines) + dot(place_hot, ret_parts)).astype(
            BF
        )

    for copy in pools:
        copy.wait_recv()
    sums = psend[me]
    for d in range(1, GX):
        sums = sums + precv[d]
    pooled[...] = sums.astype(BF)

    for d in range(1, GX):
        gathers[d - 1].wait_recv()
        place = ag.at[core, rows_of(lax.rem(me + GX - d, GX))]
        forwards.append(remote(place, place, fw_s.at[d], fw_r.at[d], {"gy": sib}))
        forwards[-1].start()

    @pl.when(me > 0)
    def _():
        for d in range(1, GX):
            pl.when(me == d)(bias_gathers[d - 1].wait_recv)

    forwards.append(remote(bias_place, bias_place, fw_s.at[GX], fw_r.at[GX], {"gy": sib}))
    forwards[-1].start()
    for copy in forwards:
        copy.wait_recv()
    gw[...] = ag[...]

    for k in range(4):
        pl.when(there[k])(halo[k].wait_send)
        pl.when(there[k])(back[k].wait_send)
    for group in (cots, pools, scatter, over_z, gathers, forwards, [pair]):
        for copy in group:
            copy.wait_send()
    for d in range(1, GX):
        pl.when(me + d == GX)(bias_scatter[d - 1].wait_send)

    @pl.when(me == 0)
    def _():
        for copy in bias_z:
            copy.wait_send()
        for copy in bias_gathers:
            copy.wait_send()


def local(nodes, brows, src, tgt, mask, segs, w1, b1, w2, cot):
    dma = pltpu.SemaphoreType.DMA
    scratch = [
        pltpu.VMEM((F, N + HALO), BF),
        pltpu.VMEM((H, 2 * F), BF),
        pltpu.VMEM((H, 128), F32),
        pltpu.VMEM((F, NB), BF),
        pltpu.VMEM((4, F, NB), BF),
        pltpu.VMEM((GX, SR, F), BF),
        pltpu.VMEM((F, SEG), BF),
        pltpu.VMEM((2 * F + 16, E), BF),
        pltpu.VMEM((8, E), jnp.int32),
        pltpu.VMEM((H, E), BF),
        pltpu.VMEM((H, E), BF),
        pltpu.VMEM((2 * F, E), BF),
        pltpu.VMEM((2, PW, HW), F32),
        pltpu.VMEM((2, PW, HW), BF),
        pltpu.VMEM((PW, HW), BF),
        pltpu.VMEM((PW, HW), BF),
        pltpu.VMEM((GX, CH, HW), BF),
        pltpu.VMEM((GX, 16, HW), BF),
        pltpu.VMEM((4, CH, HW), F32),
        pltpu.VMEM((4, 16, HW), F32),
        pltpu.VMEM((2, PW, HW), BF),
        pltpu.VMEM((GX, SR, F), F32),
        pltpu.VMEM((GX, SR, F), F32),
        pltpu.VMEM((4, NB, F), BF),
        pltpu.VMEM((4, NB, F), BF),
        pltpu.VMEM((N, F), F32),
        dma((4,)),
        dma((4,)),
        dma((GX,)),
        dma((GX,)),
        dma((GX,)),
        dma((GX,)),
        dma((4,)),
        dma((4,)),
        dma,
        dma,
        dma((GX,)),
        dma((GX,)),
        dma((GX,)),
        dma((GX,)),
        dma((4,)),
        dma((4,)),
        dma((4,)),
        dma((4,)),
        dma((GX,)),
        dma((GX,)),
        dma((GX,)),
        dma((GX,)),
        dma((GX + 1,)),
        dma((GX + 1,)),
    ]
    vmem = pl.BlockSpec(memory_space=pltpu.VMEM)
    pooled, gnodes, gw = pl.pallas_call(
        kernel,
        out_shape=(
            jax.ShapeDtypeStruct((SR, F), BF),
            jax.ShapeDtypeStruct((N, F), BF),
            jax.ShapeDtypeStruct((2, PW, HW), BF),
        ),
        in_specs=[vmem] * 10,
        out_specs=(vmem,) * 3,
        scratch_shapes=scratch,
        compiler_params=pltpu.CompilerParams(
            collective_id=0, has_side_effects=True, vmem_limit_bytes=60 * 2**20
        ),
    )(
        nodes,
        brows.reshape(1, NB),
        src,
        tgt,
        mask,
        segs.reshape(N // 128, 128),
        w1,
        b1.reshape(1, H),
        w2,
        cot,
    )
    scale = 1.0 / jnp.sqrt(jnp.float32(E * GX * GY))
    both = jnp.concatenate([gw[0], gw[1]], axis=1).astype(F32) * scale
    return pooled, gnodes, both[:512], both[768], both[512:768].T


def solution(mesh):
    in_specs = (
        P(("gx", "gy"), None),
        P(("gx", "gy")),
        P(("gx", "gy"), None),
        P(("gx", "gy"), None),
        P(("gx", "gy"), None),
        P(("gx", "gy")),
        P(),
        P(),
        P(),
        P(("gx", "gy"), None),
    )
    out_specs = (P(("gx", "gy"), None), P(("gx", "gy"), None), P(), P(), P())
    return jax.shard_map(local, mesh=mesh, in_specs=in_specs, out_specs=out_specs, check_vma=False)
```

```python
import functools

import jax
import jax.numpy as jnp
from jax import lax
from jax.experimental import pallas as pl
from jax.experimental.pallas import tpu as pltpu
from jax.sharding import PartitionSpec as P

MESH = pl.DeviceIdType.MESH
BF = jnp.bfloat16
F32 = jnp.float32
N = 2048
NB = 128
HALO = 4 * NB
F = 256
H = 512
E = 4096
SEG = 512
SR = 32
GX = 16
GY = 8
W = 1024
PW = 784
HW = H // 2
NT = (((1,), (1,)), ((), ()))


def dot(a, b):
    return jnp.dot(a, b, preferred_element_type=F32)


def dnt(a, b):
    return lax.dot_general(a, b, NT, preferred_element_type=F32)


def one_hot(row, first, count):
    rows = lax.broadcasted_iota(jnp.int32, (count, row.shape[1]), 0)
    return jnp.where(rows == row - first, 1.0, 0.0).astype(BF)


def id_row(ref, first, count):
    return jnp.concatenate([ref[pl.ds(first + i, 1), :] for i in range(count)], axis=1)


def eye(size):
    a = lax.broadcasted_iota(jnp.int32, (size, size), 0)
    b = lax.broadcasted_iota(jnp.int32, (size, size), 1)
    return jnp.where(a == b, 1.0, 0.0).astype(BF)


def split(value):
    high = value.astype(BF)
    return high, (value - high.astype(F32)).astype(BF)


def kernel(
    nodes_h,
    brows_h,
    src_h,
    tgt_h,
    mask_h,
    segs_h,
    w1_h,
    b1_h,
    w2_h,
    cot_h,
    pooled_h,
    gnodes_h,
    gw_h,
    nodes,
    brows,
    src,
    tgt,
    mask,
    segs,
    w1,
    b1,
    w2,
    cot,
    pooled,
    gnodes,
    tt,
    w1t,
    bcol,
    bnd,
    hrecv,
    line,
    line_t,
    xt,
    mseg,
    hid,
    gp,
    gi,
    pwf,
    pws,
    cbuf,
    csum,
    rsb_a,
    rsb_b,
    rsbias,
    zb_a,
    zb_b,
    zbias,
    ag,
    psend,
    precv,
    gslot,
    gret,
    acc,
    in_s,
    out_s,
    h_s,
    h_r,
    c_s,
    c_r,
    p_s,
    p_r,
    g_s,
    g_r,
    core_s,
    core_r,
    rs_s,
    rs_r,
    rb_s,
    rb_r,
    z_s,
    z_r,
    zb_s,
    zb_r,
    ag_s,
    ag_r,
    agb_s,
    agb_r,
    fw_s,
    fw_r,
):
    me = lax.axis_index("gx")
    my = lax.axis_index("gy")
    core = lax.rem(my, 2)
    z = lax.div(my, 2)
    sib = my + 1 - 2 * core

    barrier = pltpu.get_barrier_semaphore()
    for d in range(1, GX):
        pl.semaphore_signal(
            barrier, inc=1, device_id={"gx": lax.rem(me + d, GX)}, device_id_type=MESH
        )
    for d in range(1, GY):
        pl.semaphore_signal(
            barrier, inc=1, device_id={"gy": lax.rem(my + d, GY)}, device_id_type=MESH
        )

    def remote(source, target, send, receive, device):
        return pltpu.make_async_remote_copy(
            src_ref=source,
            dst_ref=target,
            send_sem=send,
            recv_sem=receive,
            device_id=device,
            device_id_type=MESH,
        )

    pairs = (
        (nodes_h, nodes),
        (brows_h, brows),
        (cot_h, cot),
        (w1_h, w1),
        (b1_h, b1),
        (segs_h, segs),
        (tgt_h, tgt),
        (src_h, src),
        (mask_h, mask),
        (w2_h, w2),
    )
    loads = [pltpu.make_async_copy(a, b, in_s.at[i]) for i, (a, b) in enumerate(pairs)]
    for copy in loads:
        copy.start()

    unit = eye(F)
    for copy in loads[:3]:
        copy.wait()
    tt[:, :N] = dnt(unit, nodes[...]).astype(BF)
    bnd[...] = dot(tt[:, :N], one_hot(brows[...], 0, N)).astype(BF)
    line[pl.ds(me, 1)] = cot[...][None]

    pl.semaphore_wait(barrier, GX - 1 + GY - 1)

    there = (me > 0, me < GX - 1, my > 0, my < GY - 1)
    halo = (
        remote(bnd, hrecv.at[1], h_s.at[1], h_r.at[1], {"gx": lax.rem(me + GX - 1, GX)}),
        remote(bnd, hrecv.at[0], h_s.at[0], h_r.at[0], {"gx": lax.rem(me + 1, GX)}),
        remote(bnd, hrecv.at[3], h_s.at[3], h_r.at[3], {"gy": lax.rem(my + GY - 1, GY)}),
        remote(bnd, hrecv.at[2], h_s.at[2], h_r.at[2], {"gy": lax.rem(my + 1, GY)}),
    )
    for k in range(4):
        pl.when(there[k])(halo[k].start)
    cots = [
        remote(
            cot,
            line.at[me],
            c_s.at[d],
            c_r.at[d],
            {"gx": lax.rem(me + d, GX)},
        )
        for d in range(1, GX)
    ]
    for copy in cots:
        copy.start()
    for copy in loads[3:]:
        copy.wait()

    for i in range(2):
        for j in range(2):
            w1t[j * F : (j + 1) * F, i * F : (i + 1) * F] = dnt(
                unit, w1[i * F : (i + 1) * F, j * F : (j + 1) * F]
            ).astype(BF)
    bcol[...] = jnp.broadcast_to(
        jnp.transpose(jnp.broadcast_to(b1[...], (8, H)))[:, :1], (H, 128)
    )
    xt[2 * F :, :] = jnp.ones((16, E), BF)
    seg_ids = segs[...]
    seg_parts = jnp.concatenate(
        [
            jnp.bitwise_and(seg_ids, 255).astype(F32).astype(BF),
            jnp.right_shift(seg_ids, 8).astype(F32).astype(BF),
        ],
        axis=0,
    )

    def block(b, width=W):
        return pl.ds(pl.multiple_of(b * width, width), width)

    def gather(b, carry):
        targets = id_row(tgt, b * 8, 8)
        sources = id_row(src, b * 8, 8)
        live = id_row(mask, b * 8, 8)
        low = one_hot(jnp.bitwise_and(targets, 127), 0, 128)
        found = dot(seg_parts, low)
        found = found[:16] + 256.0 * found[16:]
        high = lax.broadcasted_iota(jnp.int32, (16, W), 0) == jnp.right_shift(targets, 7)
        segment = jnp.sum(jnp.where(high, found, 0.0), axis=0, keepdims=True)
        segment = jnp.where(live > 0, segment, -1.0).astype(jnp.int32)
        mseg[:, block(b)] = jnp.broadcast_to(segment, (8, W))
        xt[F : 2 * F, block(b)] = dot(tt[:, :N], one_hot(targets, 0, N)).astype(BF)
        xt[:F, block(b)] = dot(tt[:, :N], one_hot(sources, 0, N)).astype(BF)
        return carry

    lax.fori_loop(0, E // W, gather, 0)

    for k, coming in enumerate((halo[1], halo[0], halo[3], halo[2])):
        pl.when(there[k])(coming.wait_recv)

        @pl.when(jnp.logical_not(there[k]))
        def _(k=k):
            hrecv[k] = jnp.zeros((F, NB), BF)

        tt[:, N + k * NB : N + (k + 1) * NB] = hrecv[k]
    for copy in cots:
        copy.wait_recv()
    lines = jnp.concatenate([line[g] for g in range(GX)], axis=0)
    line_t[...] = dnt(unit, lines).astype(BF)

    def edges(b, carry):
        sources = id_row(src, b * 8, 8)
        xt[:F, block(b)] = (
            xt[:F, block(b)].astype(F32) + dot(tt[:, N:], one_hot(sources, N, HALO))
        ).astype(BF)
        chosen = one_hot(mseg[:1, block(b)], 0, SEG)
        gm = dot(line_t[...], chosen).astype(BF)
        bias = jnp.concatenate([bcol[...]] * (W // 128), axis=1)
        x = dot(w1t[...], xt[: 2 * F, block(b)]) + bias
        gh = dot(w2[...], gm)
        square = x * x
        t = jnp.tanh(x * (0.7978845608028654 + 0.035677408136300125 * square))
        half = 0.5 + 0.5 * t
        hid[:, block(b)] = (x * half).astype(BF)
        slope = half + (0.5 * x) * (1.0 - t * t) * (
            0.7978845608028654 + 0.10703222440890037 * square
        )
        gp[:, block(b)] = (gh * slope).astype(BF)
        return carry

    lax.fori_loop(0, E // W, edges, 0)

    firsts, counts = (0, 528), (528, 256)
    shares = (32, 16)
    arrived = (rsb_a, rsb_b)
    by_z = (zb_a, zb_b)

    def rows_of(part, member):
        return pl.ds(pl.multiple_of(firsts[part] + member * shares[part], 16), shares[part])

    def whole(part):
        return pl.ds(firsts[part], counts[part])

    peers = [lax.rem(me + d, GX) for d in range(GX)]
    pair, scatter, over_z, gathers, forwards = [], [], [], [], []
    for part in range(2):
        pair.append(
            remote(
                pws.at[1 - core, whole(part)],
                cbuf.at[whole(part)],
                core_s.at[part],
                core_r.at[part],
                {"gy": sib},
            )
        )
        scatter.append(
            [
                remote(
                    csum.at[rows_of(part, peers[d])],
                    arrived[part].at[d],
                    rs_s.at[part, d],
                    rs_r.at[part, d],
                    {"gx": peers[d]},
                )
                for d in range(1, GX)
            ]
        )
        over_z.append(
            [
                remote(
                    by_z[part].at[z],
                    by_z[part].at[z],
                    z_s.at[part, d],
                    z_r.at[part, d],
                    {"gy": lax.rem(my + 2 * d, GY)},
                )
                for d in range(1, 4)
            ]
        )
        place = ag.at[core, rows_of(part, me)]
        gathers.append(
            [
                remote(place, place, ag_s.at[part, d], ag_r.at[part, d], {"gx": peers[d]})
                for d in range(1, GX)
            ]
        )
        ways = []
        for d in range(GX):
            place = ag.at[core, rows_of(part, lax.rem(me + GX - d, GX))]
            ways.append(remote(place, place, fw_s.at[part, d], fw_r.at[part, d], {"gy": sib}))
        forwards.append(ways)
    bias_rows = csum.at[pl.ds(512, 16)]
    bias_scatter = [
        remote(bias_rows, rsbias.at[d], rb_s.at[d], rb_r.at[d], {"gx": peers[d]})
        for d in range(1, GX)
    ]
    bias_z = [
        remote(zbias.at[z], zbias.at[z], zb_s.at[d], zb_r.at[d], {"gy": lax.rem(my + 2 * d, GY)})
        for d in range(1, 4)
    ]
    bias_place = ag.at[core, pl.ds(512, 16)]
    bias_gathers = [
        remote(bias_place, bias_place, agb_s.at[d], agb_r.at[d], {"gx": peers[d]})
        for d in range(1, GX)
    ]
    bias_forward = remote(bias_place, bias_place, fw_s.at[0, GX], fw_r.at[0, GX], {"gy": sib})

    def to_pair(part):
        pws[:, whole(part), :] = pwf[:, whole(part), :].astype(BF)
        pair[part].start()

    def to_members(part):
        pair[part].wait_recv()
        csum[whole(part), :] = (
            pwf[core, whole(part), :] + cbuf[whole(part), :].astype(F32)
        ).astype(BF)
        for copy in scatter[part]:
            copy.start()
        if part == 0:
            for d in range(1, GX):
                pl.when(me + d == GX)(bias_scatter[d - 1].start)

    def to_z(part):
        for copy in scatter[part]:
            copy.wait_recv()
        total = csum[rows_of(part, me), :].astype(F32)
        for d in range(1, GX):
            total = total + arrived[part][d].astype(F32)
        by_z[part][pl.ds(z, 1)] = total[None]
        for copy in over_z[part]:
            copy.start()
        if part == 0:

            @pl.when(me == 0)
            def _():
                for copy in bias_scatter:
                    copy.wait_recv()
                sums = csum[512:528, :].astype(F32)
                for d in range(1, GX):
                    sums = sums + rsbias[d].astype(F32)
                zbias[pl.ds(z, 1)] = sums[None]
                for copy in bias_z:
                    copy.start()

    def to_all(part):
        for copy in over_z[part]:
            copy.wait_recv()
        sums = by_z[part]
        total = (sums[0] + sums[1]) + (sums[2] + sums[3])
        ag[pl.ds(core, 1), rows_of(part, me), :] = total.astype(BF)[None]
        for copy in gathers[part]:
            copy.start()
        forwards[part][0].start()
        if part == 0:

            @pl.when(me == 0)
            def _():
                for copy in bias_z:
                    copy.wait_recv()
                sums = (zbias[0] + zbias[1]) + (zbias[2] + zbias[3])
                ag[pl.ds(core, 1), 512:528, :] = sums.astype(BF)[None]
                for copy in bias_gathers:
                    copy.start()

    def to_other_core(part):
        for d in range(1, GX):
            gathers[part][d - 1].wait_recv()
            forwards[part][d].start()
        if part == 0:
            for d in range(1, GX):
                pl.when(me == d)(bias_gathers[d - 1].wait_recv)
            bias_forward.start()

    for c in range(2):
        first = dnt(xt[...], gp[c * HW : (c + 1) * HW, :])
        pwf[c, 0:528, :] = first
    to_pair(0)

    w2v = w2[...]

    def segment_sums(b, carry):
        first = b * 256
        edge_hot = one_hot(mseg[:1, :], first, 256)
        high, low = split(dnt(edge_hot, hid[...]))
        node_hot = one_hot(id_row(segs, 0, N // 128), first, 256)
        part = dot(high, w2v) + dot(low, w2v) + dot(node_hot, nodes[...])
        for i in range(8):
            psend[b * 8 + i] = part[i * SR : (i + 1) * SR]
        lines_t = line_t[:, block(b, 256)]
        add = dot(lines_t, high) + dot(lines_t, low)
        for c in range(2):
            pwf[c, 528:784, :] = pwf[c, 528:784, :] + add[:, c * HW : (c + 1) * HW]
        pl.when(b == 0)(functools.partial(to_members, 0))
        return carry

    pwf[:, 528:784, :] = jnp.zeros((2, 256, HW), F32)
    lax.fori_loop(0, SEG // 256, segment_sums, 0)
    to_pair(1)
    pools = [
        remote(
            psend.at[peers[d]],
            precv.at[d],
            p_s.at[d],
            p_r.at[d],
            {"gx": peers[d]},
        )
        for d in range(1, GX)
    ]
    for copy in pools:
        copy.start()

    def input_grads(b, carry):
        gi[:, block(b)] = dot(w1[...], gp[:, block(b)]).astype(BF)
        return carry

    lax.fori_loop(0, E // W, input_grads, 0)
    to_members(1)
    to_z(0)

    all_src = id_row(src, 0, 32)
    slots = dnt(one_hot(all_src, N, HALO), gi[:F, :])
    for k in range(4):
        gslot[k] = slots[k * NB : (k + 1) * NB].astype(BF)
    back = (
        remote(gslot.at[0], gret.at[0], g_s.at[0], g_r.at[0], {"gx": lax.rem(me + GX - 1, GX)}),
        remote(gslot.at[1], gret.at[1], g_s.at[1], g_r.at[1], {"gx": lax.rem(me + 1, GX)}),
        remote(gslot.at[2], gret.at[2], g_s.at[2], g_r.at[2], {"gy": lax.rem(my + GY - 1, GY)}),
        remote(gslot.at[3], gret.at[3], g_s.at[3], g_r.at[3], {"gy": lax.rem(my + 1, GY)}),
    )
    for k in range(4):
        pl.when(there[k])(back[k].start)

    def own(b, carry):
        first = b * 512
        s = dnt(one_hot(id_row(src, 0, 32), first, 512), gi[:F, :])
        t = dnt(one_hot(id_row(tgt, 0, 32), first, 512), gi[F:, :])
        acc[block(b, 512), :] = s + t

        @pl.when(b == 0)
        def _():
            to_z(1)
            to_all(0)

        pl.when(b == 1)(functools.partial(to_all, 1))
        pl.when(b == 2)(functools.partial(to_other_core, 0))
        pl.when(b == 3)(functools.partial(to_other_core, 1))
        return carry

    lax.fori_loop(0, N // 512, own, 0)

    ret = jnp.zeros((NB, F), F32)
    for k, here in enumerate((there[1], there[0], there[3], there[2])):
        pl.when(here)(back[k].wait_recv)

        @pl.when(jnp.logical_not(here))
        def _(k=k):
            gret[k] = jnp.zeros((NB, F), BF)

        ret = ret + gret[k].astype(F32)
    ret_parts = jnp.concatenate(split(ret), axis=0)
    lines = jnp.concatenate([line[g] for g in range(GX)], axis=0)
    seg_cols = jnp.transpose(segs[...].astype(F32)).astype(jnp.int32)
    stores = []
    for r in range(N // 128):
        rows = slice(r * 128, (r + 1) * 128)
        seg_hot = jnp.where(
            lax.broadcasted_iota(jnp.int32, (128, SEG), 1) == seg_cols[:, r : r + 1], 1.0, 0.0
        ).astype(BF)
        place_hot = one_hot(brows[...], r * 128, 128)
        place_hot = jnp.concatenate([place_hot, place_hot], axis=1)
        gnodes[rows, :] = (acc[rows, :] + dot(seg_hot, lines) + dot(place_hot, ret_parts)).astype(
            BF
        )
        if r % 4 == 3:
            done = pl.ds((r - 3) * 128, 512)
            stores.append(
                pltpu.make_async_copy(gnodes.at[done], gnodes_h.at[done], out_s.at[r // 4])
            )
            stores[-1].start()

    for copy in pools:
        copy.wait_recv()
    sums = psend[me]
    for d in range(1, GX):
        sums = sums + precv[d]
    pooled[...] = sums.astype(BF)
    stores.append(pltpu.make_async_copy(pooled, pooled_h, out_s.at[4]))
    stores[-1].start()

    for part in range(2):
        for copy in forwards[part]:
            copy.wait_recv()
    bias_forward.wait_recv()
    stores.append(pltpu.make_async_copy(ag, gw_h, out_s.at[5]))
    stores[-1].start()

    for k in range(4):
        pl.when(there[k])(halo[k].wait_send)
        pl.when(there[k])(back[k].wait_send)
    for group in (cots, pools, pair, [bias_forward], *scatter, *over_z, *gathers, *forwards):
        for copy in group:
            copy.wait_send()
    for d in range(1, GX):
        pl.when(me + d == GX)(bias_scatter[d - 1].wait_send)

    @pl.when(me == 0)
    def _():
        for copy in bias_z:
            copy.wait_send()
        for copy in bias_gathers:
            copy.wait_send()

    for copy in stores:
        copy.wait()


def finish(scale, pooled, gnodes, gw, pooled_o, gnodes_o, first_o, bias_o, second_o, buf, sems):
    moves = [
        pltpu.make_async_copy(gw, buf, sems.at[0]),
        pltpu.make_async_copy(gnodes, gnodes_o, sems.at[1]),
        pltpu.make_async_copy(pooled, pooled_o, sems.at[2]),
    ]
    for copy in moves:
        copy.start()
    moves[0].wait()
    unit = eye(HW)
    for c in range(2):
        half = slice(c * HW, (c + 1) * HW)
        first_o[:, half] = buf[c, 0:512, :].astype(F32) * scale
        bias_o[:, half] = buf[c, 512:528, :].astype(F32)[:1] * scale
        second_o[half, :] = dnt(unit, buf[c, 528:784, :]) * scale
    moves[1].wait()
    moves[2].wait()


def local(nodes, brows, src, tgt, mask, segs, w1, b1, w2, cot):
    dma = pltpu.SemaphoreType.DMA
    int32 = jnp.int32
    arguments = (
        nodes,
        brows.reshape(1, NB),
        src,
        tgt,
        mask,
        segs.reshape(N // 128, 128),
        w1,
        b1.reshape(1, H),
        w2,
        cot,
    )
    scratch = [pltpu.VMEM(a.shape, a.dtype) for a in arguments]
    scratch += [
        pltpu.VMEM((SR, F), BF),
        pltpu.VMEM((N, F), BF),
        pltpu.VMEM((F, N + HALO), BF),
        pltpu.VMEM((H, 2 * F), BF),
        pltpu.VMEM((H, 128), F32),
        pltpu.VMEM((F, NB), BF),
        pltpu.VMEM((4, F, NB), BF),
        pltpu.VMEM((GX, SR, F), BF),
        pltpu.VMEM((F, SEG), BF),
        pltpu.VMEM((2 * F + 16, E), BF),
        pltpu.VMEM((8, E), int32),
        pltpu.VMEM((H, E), BF),
        pltpu.VMEM((H, E), BF),
        pltpu.VMEM((2 * F, E), BF),
        pltpu.VMEM((2, PW, HW), F32),
        pltpu.VMEM((2, PW, HW), BF),
        pltpu.VMEM((PW, HW), BF),
        pltpu.VMEM((PW, HW), BF),
        pltpu.VMEM((GX, 32, HW), BF),
        pltpu.VMEM((GX, 16, HW), BF),
        pltpu.VMEM((GX, 16, HW), BF),
        pltpu.VMEM((4, 32, HW), F32),
        pltpu.VMEM((4, 16, HW), F32),
        pltpu.VMEM((4, 16, HW), F32),
        pltpu.VMEM((2, PW, HW), BF),
        pltpu.VMEM((GX, SR, F), F32),
        pltpu.VMEM((GX, SR, F), F32),
        pltpu.VMEM((4, NB, F), BF),
        pltpu.VMEM((4, NB, F), BF),
        pltpu.VMEM((N, F), F32),
        dma((10,)),
        dma((6,)),
    ]
    for shape in (
        (4,),
        (GX,),
        (GX,),
        (4,),
        (2,),
        (2, GX),
        (GX,),
        (2, 4),
        (4,),
        (2, GX),
        (GX,),
        (2, GX + 1),
    ):
        scratch += [dma(shape), dma(shape)]
    anywhere = pl.BlockSpec(memory_space=pl.ANY)
    vmem = pl.BlockSpec(memory_space=pltpu.VMEM)
    outs = (
        jax.ShapeDtypeStruct((SR, F), BF),
        jax.ShapeDtypeStruct((N, F), BF),
    )
    pooled, gnodes, gw = pl.pallas_call(
        kernel,
        out_shape=(*outs, jax.ShapeDtypeStruct((2, PW, HW), BF)),
        in_specs=[anywhere] * 10,
        out_specs=(anywhere,) * 3,
        scratch_shapes=scratch,
        compiler_params=pltpu.CompilerParams(
            collective_id=0, has_side_effects=True, vmem_limit_bytes=60 * 2**20
        ),
    )(*arguments)
    pooled, gnodes, first, bias, second = pl.pallas_call(
        functools.partial(finish, float((E * GX * GY) ** -0.5)),
        out_shape=(
            *outs,
            jax.ShapeDtypeStruct((H, H), F32),
            jax.ShapeDtypeStruct((1, H), F32),
            jax.ShapeDtypeStruct((H, F), F32),
        ),
        in_specs=[anywhere] * 3,
        out_specs=(anywhere, anywhere, vmem, vmem, vmem),
        scratch_shapes=[pltpu.VMEM((2, PW, HW), BF), dma((3,))],
        compiler_params=pltpu.CompilerParams(vmem_limit_bytes=16 * 2**20),
    )(pooled, gnodes, gw)
    return pooled, gnodes, first, bias.reshape(H), second


def solution(mesh):
    in_specs = (
        P(("gx", "gy"), None),
        P(("gx", "gy")),
        P(("gx", "gy"), None),
        P(("gx", "gy"), None),
        P(("gx", "gy"), None),
        P(("gx", "gy")),
        P(),
        P(),
        P(),
        P(("gx", "gy"), None),
    )
    out_specs = (P(("gx", "gy"), None), P(("gx", "gy"), None), P(), P(), P())
    return jax.shard_map(local, mesh=mesh, in_specs=in_specs, out_specs=out_specs, check_vma=False)
```

```python
import functools

import jax
import jax.numpy as jnp
from jax import lax
from jax.experimental import pallas as pl
from jax.experimental.pallas import tpu as pltpu
from jax.sharding import PartitionSpec as P

MESH = pl.DeviceIdType.MESH
BF = jnp.bfloat16
F32 = jnp.float32
N = 2048
NB = 128
HALO = 4 * NB
F = 256
H = 512
E = 4096
SEG = 512
SR = 32
GX = 16
GY = 8
W = 1024
PW = 784
HW = H // 2
NT = (((1,), (1,)), ((), ()))


def dot(a, b):
    return jnp.dot(a, b, preferred_element_type=F32)


def dnt(a, b):
    return lax.dot_general(a, b, NT, preferred_element_type=F32)


def one_hot(row, first, count):
    rows = lax.broadcasted_iota(jnp.int32, (count, row.shape[1]), 0)
    return jnp.where(rows == row - first, 1.0, 0.0).astype(BF)


def id_row(ref, first, count):
    return jnp.concatenate([ref[pl.ds(first + i, 1), :] for i in range(count)], axis=1)


def eye(size):
    a = lax.broadcasted_iota(jnp.int32, (size, size), 0)
    b = lax.broadcasted_iota(jnp.int32, (size, size), 1)
    return jnp.where(a == b, 1.0, 0.0).astype(BF)


def split(value):
    high = value.astype(BF)
    return high, (value - high.astype(F32)).astype(BF)


def kernel(
    nodes_h,
    brows_h,
    src_h,
    tgt_h,
    mask_h,
    segs_h,
    w1_h,
    b1_h,
    w2_h,
    cot_h,
    pooled_h,
    gnodes_h,
    gw_h,
    nodes,
    brows,
    src,
    tgt,
    mask,
    segs,
    w1,
    b1,
    w2,
    cot,
    pooled,
    gnodes,
    tt,
    w1t,
    bcol,
    bnd,
    hrecv,
    line,
    line_t,
    xt,
    mseg,
    hid,
    gp,
    gi,
    pwf,
    pws,
    cbuf,
    csum,
    rsb_a,
    rsb_b,
    rsbias,
    zb_a,
    zb_b,
    zbias,
    ag,
    psend,
    precv,
    gslot,
    gret,
    acc,
    in_s,
    out_s,
    h_s,
    h_r,
    c_s,
    c_r,
    p_s,
    p_r,
    g_s,
    g_r,
    core_s,
    core_r,
    rs_s,
    rs_r,
    rb_s,
    rb_r,
    z_s,
    z_r,
    zb_s,
    zb_r,
    ag_s,
    ag_r,
    agb_s,
    agb_r,
    fw_s,
    fw_r,
):
    me = lax.axis_index("gx")
    my = lax.axis_index("gy")
    core = lax.rem(my, 2)
    z = lax.div(my, 2)
    sib = my + 1 - 2 * core

    barrier = pltpu.get_barrier_semaphore()
    for d in range(1, GX):
        pl.semaphore_signal(
            barrier, inc=1, device_id={"gx": lax.rem(me + d, GX)}, device_id_type=MESH
        )
    for d in range(1, GY):
        pl.semaphore_signal(
            barrier, inc=1, device_id={"gy": lax.rem(my + d, GY)}, device_id_type=MESH
        )

    def remote(source, target, send, receive, device):
        return pltpu.make_async_remote_copy(
            src_ref=source,
            dst_ref=target,
            send_sem=send,
            recv_sem=receive,
            device_id=device,
            device_id_type=MESH,
        )

    pairs = (
        (nodes_h, nodes),
        (brows_h, brows),
        (cot_h, cot),
        (w1_h, w1),
        (b1_h, b1),
        (segs_h, segs),
        (tgt_h, tgt),
        (src_h, src),
        (mask_h, mask),
        (w2_h, w2),
    )
    loads = [pltpu.make_async_copy(a, b, in_s.at[i]) for i, (a, b) in enumerate(pairs)]
    for copy in loads:
        copy.start()

    unit = eye(F)
    for copy in loads[:3]:
        copy.wait()
    tt[:, :N] = dnt(unit, nodes[...]).astype(BF)
    bnd[...] = dot(tt[:, :N], one_hot(brows[...], 0, N)).astype(BF)
    line[pl.ds(me, 1)] = cot[...][None]

    pl.semaphore_wait(barrier, GX - 1 + GY - 1)

    there = (me > 0, me < GX - 1, my > 0, my < GY - 1)
    halo = (
        remote(bnd, hrecv.at[1], h_s.at[1], h_r.at[1], {"gx": lax.rem(me + GX - 1, GX)}),
        remote(bnd, hrecv.at[0], h_s.at[0], h_r.at[0], {"gx": lax.rem(me + 1, GX)}),
        remote(bnd, hrecv.at[3], h_s.at[3], h_r.at[3], {"gy": lax.rem(my + GY - 1, GY)}),
        remote(bnd, hrecv.at[2], h_s.at[2], h_r.at[2], {"gy": lax.rem(my + 1, GY)}),
    )
    for k in range(4):
        pl.when(there[k])(halo[k].start)
    cots = [
        remote(
            cot,
            line.at[me],
            c_s.at[d],
            c_r.at[d],
            {"gx": lax.rem(me + d, GX)},
        )
        for d in range(1, GX)
    ]
    for copy in cots:
        copy.start()
    for copy in loads[3:]:
        copy.wait()

    for i in range(2):
        for j in range(2):
            w1t[j * F : (j + 1) * F, i * F : (i + 1) * F] = dnt(
                unit, w1[i * F : (i + 1) * F, j * F : (j + 1) * F]
            ).astype(BF)
    bcol[...] = jnp.broadcast_to(
        jnp.transpose(jnp.broadcast_to(b1[...], (8, H)))[:, :1], (H, 128)
    )
    xt[2 * F :, :] = jnp.ones((16, E), BF)
    seg_ids = segs[...]
    seg_parts = jnp.concatenate(
        [
            jnp.bitwise_and(seg_ids, 255).astype(F32).astype(BF),
            jnp.right_shift(seg_ids, 8).astype(F32).astype(BF),
        ],
        axis=0,
    )

    def block(b, width=W):
        return pl.ds(pl.multiple_of(b * width, width), width)

    def gather(b, carry):
        targets = id_row(tgt, b * 8, 8)
        sources = id_row(src, b * 8, 8)
        live = id_row(mask, b * 8, 8)
        low = one_hot(jnp.bitwise_and(targets, 127), 0, 128)
        found = dot(seg_parts, low)
        found = found[:16] + 256.0 * found[16:]
        high = lax.broadcasted_iota(jnp.int32, (16, W), 0) == jnp.right_shift(targets, 7)
        segment = jnp.sum(jnp.where(high, found, 0.0), axis=0, keepdims=True)
        segment = jnp.where(live > 0, segment, -1.0).astype(jnp.int32)
        mseg[:, block(b)] = jnp.broadcast_to(segment, (8, W))
        xt[F : 2 * F, block(b)] = dot(tt[:, :N], one_hot(targets, 0, N)).astype(BF)
        xt[:F, block(b)] = dot(tt[:, :N], one_hot(sources, 0, N)).astype(BF)
        return carry

    lax.fori_loop(0, E // W, gather, 0)

    for k, coming in enumerate((halo[1], halo[0], halo[3], halo[2])):
        pl.when(there[k])(coming.wait_recv)

        @pl.when(jnp.logical_not(there[k]))
        def _(k=k):
            hrecv[k] = jnp.zeros((F, NB), BF)

        tt[:, N + k * NB : N + (k + 1) * NB] = hrecv[k]
    for copy in cots:
        copy.wait_recv()
    lines = jnp.concatenate([line[g] for g in range(GX)], axis=0)
    line_t[...] = dnt(unit, lines).astype(BF)

    def edges(b, carry):
        sources = id_row(src, b * 8, 8)
        xt[:F, block(b)] = (
            xt[:F, block(b)].astype(F32) + dot(tt[:, N:], one_hot(sources, N, HALO))
        ).astype(BF)
        chosen = one_hot(mseg[:1, block(b)], 0, SEG)
        gm = dot(line_t[...], chosen).astype(BF)
        bias = jnp.concatenate([bcol[...]] * (W // 128), axis=1)
        x = dot(w1t[...], xt[: 2 * F, block(b)]) + bias
        gh = dot(w2[...], gm)
        square = x * x
        t = jnp.tanh(x * (0.7978845608028654 + 0.035677408136300125 * square))
        half = 0.5 + 0.5 * t
        hid[:, block(b)] = (x * half).astype(BF)
        slope = half + (0.5 * x) * (1.0 - t * t) * (
            0.7978845608028654 + 0.10703222440890037 * square
        )
        gp[:, block(b)] = (gh * slope).astype(BF)
        return carry

    lax.fori_loop(0, E // W, edges, 0)

    firsts, counts = (0, 528), (528, 256)
    shares = (32, 16)
    arrived = (rsb_a, rsb_b)
    by_z = (zb_a, zb_b)

    def rows_of(part, member):
        return pl.ds(pl.multiple_of(firsts[part] + member * shares[part], 16), shares[part])

    def whole(part):
        return pl.ds(firsts[part], counts[part])

    peers = [lax.rem(me + d, GX) for d in range(GX)]
    pair, scatter, over_z, gathers, forwards = [], [], [], [], []
    for part in range(2):
        pair.append(
            remote(
                pws.at[1 - core, whole(part)],
                cbuf.at[whole(part)],
                core_s.at[part],
                core_r.at[part],
                {"gy": sib},
            )
        )
        scatter.append(
            [
                remote(
                    csum.at[rows_of(part, peers[d])],
                    arrived[part].at[d],
                    rs_s.at[part, d],
                    rs_r.at[part, d],
                    {"gx": peers[d]},
                )
                for d in range(1, GX)
            ]
        )
        over_z.append(
            [
                remote(
                    by_z[part].at[z],
                    by_z[part].at[z],
                    z_s.at[part, d],
                    z_r.at[part, d],
                    {"gy": lax.rem(my + 2 * d, GY)},
                )
                for d in range(1, 4)
            ]
        )
        place = ag.at[core, rows_of(part, me)]
        gathers.append(
            [
                remote(place, place, ag_s.at[part, d], ag_r.at[part, d], {"gx": peers[d]})
                for d in range(1, GX)
            ]
        )
        ways = []
        for d in range(GX):
            place = ag.at[core, rows_of(part, lax.rem(me + GX - d, GX))]
            ways.append(remote(place, place, fw_s.at[part, d], fw_r.at[part, d], {"gy": sib}))
        forwards.append(ways)
    bias_rows = csum.at[pl.ds(512, 16)]
    bias_scatter = [
        remote(bias_rows, rsbias.at[d], rb_s.at[d], rb_r.at[d], {"gx": peers[d]})
        for d in range(1, GX)
    ]
    bias_z = [
        remote(zbias.at[z], zbias.at[z], zb_s.at[d], zb_r.at[d], {"gy": lax.rem(my + 2 * d, GY)})
        for d in range(1, 4)
    ]
    bias_place = ag.at[core, pl.ds(512, 16)]
    bias_gathers = [
        remote(bias_place, bias_place, agb_s.at[d], agb_r.at[d], {"gx": peers[d]})
        for d in range(1, GX)
    ]
    bias_forward = remote(bias_place, bias_place, fw_s.at[0, GX], fw_r.at[0, GX], {"gy": sib})

    def to_pair(part):
        pws[:, whole(part), :] = pwf[:, whole(part), :].astype(BF)
        pair[part].start()

    def to_members(part):
        pair[part].wait_recv()
        csum[whole(part), :] = (
            pwf[core, whole(part), :] + cbuf[whole(part), :].astype(F32)
        ).astype(BF)
        for copy in scatter[part]:
            copy.start()
        if part == 0:
            for d in range(1, GX):
                pl.when(me + d == GX)(bias_scatter[d - 1].start)

    def to_z(part):
        for copy in scatter[part]:
            copy.wait_recv()
        total = csum[rows_of(part, me), :].astype(F32)
        for d in range(1, GX):
            total = total + arrived[part][d].astype(F32)
        by_z[part][pl.ds(z, 1)] = total[None]
        for copy in over_z[part]:
            copy.start()
        if part == 0:

            @pl.when(me == 0)
            def _():
                for copy in bias_scatter:
                    copy.wait_recv()
                sums = csum[512:528, :].astype(F32)
                for d in range(1, GX):
                    sums = sums + rsbias[d].astype(F32)
                zbias[pl.ds(z, 1)] = sums[None]
                for copy in bias_z:
                    copy.start()

    def to_all(part):
        for copy in over_z[part]:
            copy.wait_recv()
        sums = by_z[part]
        total = (sums[0] + sums[1]) + (sums[2] + sums[3])
        ag[pl.ds(core, 1), rows_of(part, me), :] = total.astype(BF)[None]
        for copy in gathers[part]:
            copy.start()
        forwards[part][0].start()
        if part == 0:

            @pl.when(me == 0)
            def _():
                for copy in bias_z:
                    copy.wait_recv()
                sums = (zbias[0] + zbias[1]) + (zbias[2] + zbias[3])
                ag[pl.ds(core, 1), 512:528, :] = sums.astype(BF)[None]
                for copy in bias_gathers:
                    copy.start()

    def to_other_core(part):
        for d in range(1, GX):
            gathers[part][d - 1].wait_recv()
            forwards[part][d].start()
        if part == 0:
            for d in range(1, GX):
                pl.when(me == d)(bias_gathers[d - 1].wait_recv)
            bias_forward.start()

    grads = dnt(xt[...], gp[...])
    for c in range(2):
        pwf[c, 0:528, :] = grads[:, c * HW : (c + 1) * HW]
    to_pair(0)

    w2v = w2[...]

    def segment_sums(b, carry):
        first = b * 256
        edge_hot = one_hot(mseg[:1, :], first, 256)
        high, low = split(dnt(edge_hot, hid[...]))
        node_hot = one_hot(id_row(segs, 0, N // 128), first, 256)
        part = dot(high, w2v) + dot(low, w2v) + dot(node_hot, nodes[...])
        for i in range(8):
            psend[b * 8 + i] = part[i * SR : (i + 1) * SR]
        lines_t = line_t[:, block(b, 256)]
        add = dot(lines_t, high) + dot(lines_t, low)
        for c in range(2):
            pwf[c, 528:784, :] = pwf[c, 528:784, :] + add[:, c * HW : (c + 1) * HW]
        pl.when(b == 0)(functools.partial(to_members, 0))
        return carry

    pwf[:, 528:784, :] = jnp.zeros((2, 256, HW), F32)
    lax.fori_loop(0, SEG // 256, segment_sums, 0)
    to_pair(1)
    pools = [
        remote(
            psend.at[peers[d]],
            precv.at[d],
            p_s.at[d],
            p_r.at[d],
            {"gx": peers[d]},
        )
        for d in range(1, GX)
    ]
    for copy in pools:
        copy.start()

    def input_grads(b, carry):
        gi[:, block(b)] = dot(w1[...], gp[:, block(b)]).astype(BF)
        return carry

    lax.fori_loop(0, E // W, input_grads, 0)
    to_members(1)
    to_z(0)

    all_src = id_row(src, 0, 32)
    slots = dnt(one_hot(all_src, N, HALO), gi[:F, :])
    for k in range(4):
        gslot[k] = slots[k * NB : (k + 1) * NB].astype(BF)
    back = (
        remote(gslot.at[0], gret.at[0], g_s.at[0], g_r.at[0], {"gx": lax.rem(me + GX - 1, GX)}),
        remote(gslot.at[1], gret.at[1], g_s.at[1], g_r.at[1], {"gx": lax.rem(me + 1, GX)}),
        remote(gslot.at[2], gret.at[2], g_s.at[2], g_r.at[2], {"gy": lax.rem(my + GY - 1, GY)}),
        remote(gslot.at[3], gret.at[3], g_s.at[3], g_r.at[3], {"gy": lax.rem(my + 1, GY)}),
    )
    for k in range(4):
        pl.when(there[k])(back[k].start)

    def own(b, carry):
        first = b * 512
        s = dnt(one_hot(id_row(src, 0, 32), first, 512), gi[:F, :])
        t = dnt(one_hot(id_row(tgt, 0, 32), first, 512), gi[F:, :])
        acc[block(b, 512), :] = s + t

        @pl.when(b == 0)
        def _():
            to_z(1)
            to_all(0)

        pl.when(b == 1)(functools.partial(to_all, 1))
        pl.when(b == 2)(functools.partial(to_other_core, 0))
        pl.when(b == 3)(functools.partial(to_other_core, 1))
        return carry

    lax.fori_loop(0, N // 512, own, 0)

    ret = jnp.zeros((NB, F), F32)
    for k, here in enumerate((there[1], there[0], there[3], there[2])):
        pl.when(here)(back[k].wait_recv)

        @pl.when(jnp.logical_not(here))
        def _(k=k):
            gret[k] = jnp.zeros((NB, F), BF)

        ret = ret + gret[k].astype(F32)
    ret_parts = jnp.concatenate(split(ret), axis=0)
    lines = jnp.concatenate([line[g] for g in range(GX)], axis=0)
    seg_cols = jnp.transpose(segs[...].astype(F32)).astype(jnp.int32)
    stores = []
    for r in range(N // 128):
        rows = slice(r * 128, (r + 1) * 128)
        seg_hot = jnp.where(
            lax.broadcasted_iota(jnp.int32, (128, SEG), 1) == seg_cols[:, r : r + 1], 1.0, 0.0
        ).astype(BF)
        place_hot = one_hot(brows[...], r * 128, 128)
        place_hot = jnp.concatenate([place_hot, place_hot], axis=1)
        gnodes[rows, :] = (acc[rows, :] + dot(seg_hot, lines) + dot(place_hot, ret_parts)).astype(
            BF
        )
        if r % 4 == 3:
            done = pl.ds((r - 3) * 128, 512)
            stores.append(
                pltpu.make_async_copy(gnodes.at[done], gnodes_h.at[done], out_s.at[r // 4])
            )
            stores[-1].start()

    for copy in pools:
        copy.wait_recv()
    sums = psend[me]
    for d in range(1, GX):
        sums = sums + precv[d]
    pooled[...] = sums.astype(BF)
    stores.append(pltpu.make_async_copy(pooled, pooled_h, out_s.at[4]))
    stores[-1].start()

    for part in range(2):
        for copy in forwards[part]:
            copy.wait_recv()
    bias_forward.wait_recv()
    stores.append(pltpu.make_async_copy(ag, gw_h, out_s.at[5]))
    stores[-1].start()

    for k in range(4):
        pl.when(there[k])(halo[k].wait_send)
        pl.when(there[k])(back[k].wait_send)
    for group in (cots, pools, pair, [bias_forward], *scatter, *over_z, *gathers, *forwards):
        for copy in group:
            copy.wait_send()
    for d in range(1, GX):
        pl.when(me + d == GX)(bias_scatter[d - 1].wait_send)

    @pl.when(me == 0)
    def _():
        for copy in bias_z:
            copy.wait_send()
        for copy in bias_gathers:
            copy.wait_send()

    for copy in stores:
        copy.wait()


def finish(
    scale,
    pooled,
    gnodes,
    gw,
    pooled_o,
    gnodes_o,
    first_o,
    bias_o,
    second_o,
    pooled_v,
    gnodes_v,
    gw_v,
    first_v,
    bias_v,
    second_v,
    sems,
):
    def move(source, target, number):
        copy = pltpu.make_async_copy(source, target, sems.at[number])
        copy.start()
        return copy

    coming = [move(gw.at[c], gw_v.at[c], c) for c in range(2)]
    parts = [pl.ds(i * (N // 2), N // 2) for i in range(2)]
    rows = [move(gnodes.at[part], gnodes_v.at[part], 2 + i) for i, part in enumerate(parts)]
    small = move(pooled, pooled_v, 4)
    unit = eye(HW)
    going = []
    for c in range(2):
        half = slice(c * HW, (c + 1) * HW)
        coming[c].wait()
        first_v[:, half] = gw_v[c, 0:512, :].astype(F32) * scale
        bias_v[:, half] = gw_v[c, 512:528, :].astype(F32)[:1] * scale
        second_v[half, :] = dnt(unit, gw_v[c, 528:784, :]) * scale
        place = pl.ds(c * HW, HW)
        going.append(move(second_v.at[place], second_o.at[place], 5 + c))
    going.append(move(first_v, first_o, 7))
    going.append(move(bias_v, bias_o, 8))
    for i, part in enumerate(parts):
        rows[i].wait()
        going.append(move(gnodes_v.at[part], gnodes_o.at[part], 9 + i))
    small.wait()
    going.append(move(pooled_v, pooled_o, 11))
    for copy in going:
        copy.wait()


def local(nodes, brows, src, tgt, mask, segs, w1, b1, w2, cot):
    dma = pltpu.SemaphoreType.DMA
    int32 = jnp.int32
    arguments = (
        nodes,
        brows.reshape(1, NB),
        src,
        tgt,
        mask,
        segs.reshape(N // 128, 128),
        w1,
        b1.reshape(1, H),
        w2,
        cot,
    )
    scratch = [pltpu.VMEM(a.shape, a.dtype) for a in arguments]
    scratch += [
        pltpu.VMEM((SR, F), BF),
        pltpu.VMEM((N, F), BF),
        pltpu.VMEM((F, N + HALO), BF),
        pltpu.VMEM((H, 2 * F), BF),
        pltpu.VMEM((H, 128), F32),
        pltpu.VMEM((F, NB), BF),
        pltpu.VMEM((4, F, NB), BF),
        pltpu.VMEM((GX, SR, F), BF),
        pltpu.VMEM((F, SEG), BF),
        pltpu.VMEM((2 * F + 16, E), BF),
        pltpu.VMEM((8, E), int32),
        pltpu.VMEM((H, E), BF),
        pltpu.VMEM((H, E), BF),
        pltpu.VMEM((2 * F, E), BF),
        pltpu.VMEM((2, PW, HW), F32),
        pltpu.VMEM((2, PW, HW), BF),
        pltpu.VMEM((PW, HW), BF),
        pltpu.VMEM((PW, HW), BF),
        pltpu.VMEM((GX, 32, HW), BF),
        pltpu.VMEM((GX, 16, HW), BF),
        pltpu.VMEM((GX, 16, HW), BF),
        pltpu.VMEM((4, 32, HW), F32),
        pltpu.VMEM((4, 16, HW), F32),
        pltpu.VMEM((4, 16, HW), F32),
        pltpu.VMEM((2, PW, HW), BF),
        pltpu.VMEM((GX, SR, F), F32),
        pltpu.VMEM((GX, SR, F), F32),
        pltpu.VMEM((4, NB, F), BF),
        pltpu.VMEM((4, NB, F), BF),
        pltpu.VMEM((N, F), F32),
        dma((10,)),
        dma((6,)),
    ]
    for shape in (
        (4,),
        (GX,),
        (GX,),
        (4,),
        (2,),
        (2, GX),
        (GX,),
        (2, 4),
        (4,),
        (2, GX),
        (GX,),
        (2, GX + 1),
    ):
        scratch += [dma(shape), dma(shape)]
    anywhere = pl.BlockSpec(memory_space=pl.ANY)
    outs = (
        jax.ShapeDtypeStruct((SR, F), BF),
        jax.ShapeDtypeStruct((N, F), BF),
    )
    pooled, gnodes, gw = pl.pallas_call(
        kernel,
        out_shape=(*outs, jax.ShapeDtypeStruct((2, PW, HW), BF)),
        in_specs=[anywhere] * 10,
        out_specs=(anywhere,) * 3,
        scratch_shapes=scratch,
        compiler_params=pltpu.CompilerParams(
            collective_id=0, has_side_effects=True, vmem_limit_bytes=60 * 2**20
        ),
    )(*arguments)
    pooled, gnodes, first, bias, second = pl.pallas_call(
        functools.partial(finish, float((E * GX * GY) ** -0.5)),
        out_shape=(
            *outs,
            jax.ShapeDtypeStruct((H, H), F32),
            jax.ShapeDtypeStruct((1, H), F32),
            jax.ShapeDtypeStruct((H, F), F32),
        ),
        in_specs=[anywhere] * 3,
        out_specs=(anywhere,) * 5,
        scratch_shapes=[
            pltpu.VMEM((SR, F), BF),
            pltpu.VMEM((N, F), BF),
            pltpu.VMEM((2, PW, HW), BF),
            pltpu.VMEM((H, H), F32),
            pltpu.VMEM((1, H), F32),
            pltpu.VMEM((H, F), F32),
            dma((12,)),
        ],
        compiler_params=pltpu.CompilerParams(vmem_limit_bytes=60 * 2**20),
    )(pooled, gnodes, gw)
    return pooled, gnodes, first, bias.reshape(H), second


def solution(mesh):
    in_specs = (
        P(("gx", "gy"), None),
        P(("gx", "gy")),
        P(("gx", "gy"), None),
        P(("gx", "gy"), None),
        P(("gx", "gy"), None),
        P(("gx", "gy")),
        P(),
        P(),
        P(),
        P(("gx", "gy"), None),
    )
    out_specs = (P(("gx", "gy"), None), P(("gx", "gy"), None), P(), P(), P())
    return jax.shard_map(local, mesh=mesh, in_specs=in_specs, out_specs=out_specs, check_vma=False)
```

```python
import functools

import jax
import jax.numpy as jnp
from jax import lax
from jax.experimental import pallas as pl
from jax.experimental.pallas import tpu as pltpu
from jax.sharding import PartitionSpec as P

MESH = pl.DeviceIdType.MESH
BF = jnp.bfloat16
F32 = jnp.float32
N = 2048
NB = 128
HALO = 4 * NB
F = 256
H = 512
E = 4096
SEG = 512
SR = 32
GX = 16
GY = 8
W = 1024
T = 256
TILES = (N + HALO) // T
RUNS = E // T
STEPS = TILES + RUNS - 1
KINDS = 12
PW = 784
HW = H // 2
NT = (((1,), (1,)), ((), ()))


def dot(a, b):
    return jnp.dot(a, b, preferred_element_type=F32)


def dnt(a, b):
    return lax.dot_general(a, b, NT, preferred_element_type=F32)


def one_hot(row, first, count):
    rows = lax.broadcasted_iota(jnp.int32, (count, row.shape[1]), 0)
    return jnp.where(rows == row - first, 1.0, 0.0).astype(BF)


def id_row(ref, first, count):
    return jnp.concatenate([ref[pl.ds(first + i, 1), :] for i in range(count)], axis=1)


def eye(size):
    a = lax.broadcasted_iota(jnp.int32, (size, size), 0)
    b = lax.broadcasted_iota(jnp.int32, (size, size), 1)
    return jnp.where(a == b, 1.0, 0.0).astype(BF)


def ordered(size, earlier_row):
    a = lax.broadcasted_iota(jnp.int32, (size, size), 0)
    b = lax.broadcasted_iota(jnp.int32, (size, size), 1)
    return jnp.where(a < b if earlier_row else b < a, 1.0, 0.0).astype(BF)


def sort_edges(src, tgt, mask, spot, plan):
    tile = jnp.right_shift(src[...], 8)
    inside = jnp.concatenate(
        [jnp.where(tile == j, 1.0, 0.0).astype(BF) for j in range(KINDS)], axis=0
    )
    before = dot(inside, ordered(128, True))
    counts = dot(inside, jnp.ones((128, 128), BF)).astype(BF)
    base = dot(ordered(32 * KINDS, False), counts)
    places = jnp.zeros((32, 128), F32)
    for j in range(TILES):
        rows = slice(32 * j, 32 * j + 32)
        places = places + jnp.where(tile == j, before[rows] + base[rows], 0.0)
    spot[...] = places.astype(jnp.int32)

    place = id_row(spot, 0, 32)
    sources = id_row(src, 0, 32)
    targets = id_row(tgt, 0, 32)
    live = id_row(mask, 0, 32)
    here = lax.broadcasted_iota(jnp.int32, (32, E), 0) == jnp.right_shift(place, 7)
    parts = (
        jnp.bitwise_and(sources, 255),
        jnp.bitwise_and(targets, 255),
        jnp.right_shift(sources, 8) * 16 + jnp.right_shift(targets, 8),
        live,
    )
    parts = [jnp.where(here, part.astype(F32), 0.0).astype(BF) for part in parts]
    moved = dnt(
        jnp.concatenate(parts, axis=0), one_hot(jnp.bitwise_and(place, 127), 0, 128)
    ).astype(jnp.int32)
    upper = moved[64:96]
    src[...] = moved[0:32] + 256 * jnp.right_shift(upper, 4)
    tgt[...] = moved[32:64] + 256 * jnp.bitwise_and(upper, 15)
    mask[...] = moved[96:128]

    lane = lax.broadcasted_iota(jnp.int32, (1, 128), 1)
    border = jnp.zeros((1, 128), F32)
    for j in range(1, TILES):
        border = jnp.where(lane == j, base[32 * j : 32 * j + 1], border)
    passed = jnp.minimum(jnp.right_shift(border.astype(jnp.int32), 8), RUNS - 1)
    rank = jnp.where((lane >= 1) & (lane < TILES), lane - 1 + passed, 1000)
    step = lax.broadcasted_iota(jnp.int32, (32, 128), 0)
    wide = lax.broadcasted_iota(jnp.int32, (32, 128), 1)
    table_tile = jnp.sum(jnp.where(rank < step, 1.0, 0.0), axis=1, keepdims=True).astype(
        jnp.int32
    )
    table_tile = jnp.broadcast_to(table_tile, (32, 128))
    edge_tile = step - table_tile
    plan[0:32, :] = jnp.where(wide == 0, edge_tile, table_tile)
    for row, which in ((32, edge_tile), (33, table_tile)):
        upto = jnp.where((which <= wide) & (step < STEPS), 1.0, 0.0)
        plan[row : row + 1, :] = jnp.sum(upto, axis=0, keepdims=True).astype(jnp.int32) - 1


def split(value):
    high = value.astype(BF)
    return high, (value - high.astype(F32)).astype(BF)


def kernel(
    nodes_h,
    brows_h,
    src_h,
    tgt_h,
    mask_h,
    segs_h,
    w1_h,
    b1_h,
    w2_h,
    cot_h,
    pooled_h,
    gnodes_h,
    gw_h,
    nodes,
    brows,
    src,
    tgt,
    mask,
    segs,
    w1,
    b1,
    w2,
    cot,
    pooled,
    gnodes,
    tt,
    tiles,
    spot,
    plan_v,
    plan,
    xs,
    gis,
    sums_s,
    run,
    w1t,
    bcol,
    bnd,
    hrecv,
    line,
    line_t,
    xt,
    mseg,
    hid,
    gp,
    gi,
    pwf,
    pws,
    cbuf,
    csum,
    rsb_a,
    rsb_b,
    rsbias,
    zb_a,
    zb_b,
    zbias,
    ag,
    psend,
    precv,
    gslot,
    gret,
    acc,
    in_s,
    out_s,
    plan_s,
    h_s,
    h_r,
    c_s,
    c_r,
    p_s,
    p_r,
    g_s,
    g_r,
    core_s,
    core_r,
    rs_s,
    rs_r,
    rb_s,
    rb_r,
    z_s,
    z_r,
    zb_s,
    zb_r,
    ag_s,
    ag_r,
    agb_s,
    agb_r,
    fw_s,
    fw_r,
):
    me = lax.axis_index("gx")
    my = lax.axis_index("gy")
    core = lax.rem(my, 2)
    z = lax.div(my, 2)
    sib = my + 1 - 2 * core

    barrier = pltpu.get_barrier_semaphore()
    for d in range(1, GX):
        pl.semaphore_signal(
            barrier, inc=1, device_id={"gx": lax.rem(me + d, GX)}, device_id_type=MESH
        )
    for d in range(1, GY):
        pl.semaphore_signal(
            barrier, inc=1, device_id={"gy": lax.rem(my + d, GY)}, device_id_type=MESH
        )

    def remote(source, target, send, receive, device):
        return pltpu.make_async_remote_copy(
            src_ref=source,
            dst_ref=target,
            send_sem=send,
            recv_sem=receive,
            device_id=device,
            device_id_type=MESH,
        )

    pairs = (
        (nodes_h, nodes),
        (brows_h, brows),
        (cot_h, cot),
        (w1_h, w1),
        (b1_h, b1),
        (segs_h, segs),
        (tgt_h, tgt),
        (src_h, src),
        (mask_h, mask),
        (w2_h, w2),
    )
    loads = [pltpu.make_async_copy(a, b, in_s.at[i]) for i, (a, b) in enumerate(pairs)]
    for copy in loads:
        copy.start()

    unit = eye(F)
    for copy in loads[:3]:
        copy.wait()
    tt[...] = dnt(unit, nodes[...]).astype(BF)
    bnd[...] = dot(tt[...], one_hot(brows[...], 0, N)).astype(BF)
    line[pl.ds(me, 1)] = cot[...][None]

    pl.semaphore_wait(barrier, GX - 1 + GY - 1)

    there = (me > 0, me < GX - 1, my > 0, my < GY - 1)
    halo = (
        remote(bnd, hrecv.at[1], h_s.at[1], h_r.at[1], {"gx": lax.rem(me + GX - 1, GX)}),
        remote(bnd, hrecv.at[0], h_s.at[0], h_r.at[0], {"gx": lax.rem(me + 1, GX)}),
        remote(bnd, hrecv.at[3], h_s.at[3], h_r.at[3], {"gy": lax.rem(my + GY - 1, GY)}),
        remote(bnd, hrecv.at[2], h_s.at[2], h_r.at[2], {"gy": lax.rem(my + 1, GY)}),
    )
    for k in range(4):
        pl.when(there[k])(halo[k].start)
    cots = [
        remote(
            cot,
            line.at[me],
            c_s.at[d],
            c_r.at[d],
            {"gx": lax.rem(me + d, GX)},
        )
        for d in range(1, GX)
    ]
    for copy in cots:
        copy.start()
    for copy in loads[3:]:
        copy.wait()

    sort_edges(src, tgt, mask, spot, plan_v)
    to_plan = pltpu.make_async_copy(plan_v, plan, plan_s)
    to_plan.start()
    for j in range(N // T):
        tiles[j] = tt[:, j * T : (j + 1) * T]

    for i in range(2):
        for j in range(2):
            w1t[j * F : (j + 1) * F, i * F : (i + 1) * F] = dnt(
                unit, w1[i * F : (i + 1) * F, j * F : (j + 1) * F]
            ).astype(BF)
    bcol[...] = jnp.broadcast_to(
        jnp.transpose(jnp.broadcast_to(b1[...], (8, H)))[:, :1], (H, 128)
    )
    xt[2 * F :, :] = jnp.ones((16, E), BF)
    seg_ids = segs[...]
    seg_parts = jnp.concatenate(
        [
            jnp.bitwise_and(seg_ids, 255).astype(F32).astype(BF),
            jnp.right_shift(seg_ids, 8).astype(F32).astype(BF),
        ],
        axis=0,
    )

    def block(b, width=W):
        return pl.ds(pl.multiple_of(b * width, width), width)

    def gather(b, carry):
        targets = id_row(tgt, b * 8, 8)
        live = id_row(mask, b * 8, 8)
        low = one_hot(jnp.bitwise_and(targets, 127), 0, 128)
        found = dot(seg_parts, low)
        found = found[:16] + 256.0 * found[16:]
        high = lax.broadcasted_iota(jnp.int32, (16, W), 0) == jnp.right_shift(targets, 7)
        segment = jnp.sum(jnp.where(high, found, 0.0), axis=0, keepdims=True)
        segment = jnp.where(live > 0, segment, -1.0).astype(jnp.int32)
        mseg[:, block(b)] = jnp.broadcast_to(segment, (8, W))
        xt[F : 2 * F, block(b)] = dot(tt[...], one_hot(targets, 0, N)).astype(BF)
        return carry

    lax.fori_loop(0, E // W, gather, 0)

    for k, coming in enumerate((halo[1], halo[0], halo[3], halo[2])):
        pl.when(there[k])(coming.wait_recv)

        @pl.when(jnp.logical_not(there[k]))
        def _(k=k):
            hrecv[k] = jnp.zeros((F, NB), BF)

    for j in range(2):
        tiles[N // T + j] = jnp.concatenate([hrecv[2 * j], hrecv[2 * j + 1]], axis=1)
    for copy in cots:
        copy.wait_recv()
    lines = jnp.concatenate([line[g] for g in range(GX)], axis=0)
    line_t[...] = dnt(unit, lines).astype(BF)

    to_plan.wait()

    def planned(row, column, count):
        return jnp.clip(plan[row, column], 0, count - 1)

    def meeting(p):
        run_of, tile_of = planned(p, 0, RUNS), planned(p, 1, TILES)
        earlier = jnp.maximum(p - 1, 0)
        hot = one_hot(id_row(src, run_of * (T // 128), T // 128), tile_of * T, T)
        return run_of, tile_of, earlier, hot

    def source_rows(g, carry):
        total = run[...]
        for k in range(5):
            p = g * 5 + k
            run_of, tile_of, earlier, hot = meeting(p)
            same = planned(earlier, 0, RUNS) == run_of
            total = jnp.where(same, total, 0.0) + dot(tiles[tile_of], hot)
            xs[p] = total.astype(BF)
        run[...] = total
        return carry

    run[...] = jnp.zeros_like(run)
    lax.fori_loop(0, STEPS // 5, source_rows, 0)

    def edges(b, carry):
        for k in range(W // T):
            xt[:F, block(b * (W // T) + k, T)] = xs[planned(32, b * (W // T) + k, STEPS)]
        chosen = one_hot(mseg[:1, block(b)], 0, SEG)
        gm = dot(line_t[...], chosen).astype(BF)
        bias = jnp.concatenate([bcol[...]] * (W // 128), axis=1)
        x = dot(w1t[...], xt[: 2 * F, block(b)]) + bias
        gh = dot(w2[...], gm)
        square = x * x
        t = jnp.tanh(x * (0.7978845608028654 + 0.035677408136300125 * square))
        half = 0.5 + 0.5 * t
        hid[:, block(b)] = (x * half).astype(BF)
        slope = half + (0.5 * x) * (1.0 - t * t) * (
            0.7978845608028654 + 0.10703222440890037 * square
        )
        gp[:, block(b)] = (gh * slope).astype(BF)
        return carry

    lax.fori_loop(0, E // W, edges, 0)

    firsts, counts = (0, 528), (528, 256)
    shares = (32, 16)
    arrived = (rsb_a, rsb_b)
    by_z = (zb_a, zb_b)

    def rows_of(part, member):
        return pl.ds(pl.multiple_of(firsts[part] + member * shares[part], 16), shares[part])

    def whole(part):
        return pl.ds(firsts[part], counts[part])

    peers = [lax.rem(me + d, GX) for d in range(GX)]
    pair, scatter, over_z, gathers, forwards = [], [], [], [], []
    for part in range(2):
        pair.append(
            remote(
                pws.at[1 - core, whole(part)],
                cbuf.at[whole(part)],
                core_s.at[part],
                core_r.at[part],
                {"gy": sib},
            )
        )
        scatter.append(
            [
                remote(
                    csum.at[rows_of(part, peers[d])],
                    arrived[part].at[d],
                    rs_s.at[part, d],
                    rs_r.at[part, d],
                    {"gx": peers[d]},
                )
                for d in range(1, GX)
            ]
        )
        over_z.append(
            [
                remote(
                    by_z[part].at[z],
                    by_z[part].at[z],
                    z_s.at[part, d],
                    z_r.at[part, d],
                    {"gy": lax.rem(my + 2 * d, GY)},
                )
                for d in range(1, 4)
            ]
        )
        place = ag.at[core, rows_of(part, me)]
        gathers.append(
            [
                remote(place, place, ag_s.at[part, d], ag_r.at[part, d], {"gx": peers[d]})
                for d in range(1, GX)
            ]
        )
        ways = []
        for d in range(GX):
            place = ag.at[core, rows_of(part, lax.rem(me + GX - d, GX))]
            ways.append(remote(place, place, fw_s.at[part, d], fw_r.at[part, d], {"gy": sib}))
        forwards.append(ways)
    bias_rows = csum.at[pl.ds(512, 16)]
    bias_scatter = [
        remote(bias_rows, rsbias.at[d], rb_s.at[d], rb_r.at[d], {"gx": peers[d]})
        for d in range(1, GX)
    ]
    bias_z = [
        remote(zbias.at[z], zbias.at[z], zb_s.at[d], zb_r.at[d], {"gy": lax.rem(my + 2 * d, GY)})
        for d in range(1, 4)
    ]
    bias_place = ag.at[core, pl.ds(512, 16)]
    bias_gathers = [
        remote(bias_place, bias_place, agb_s.at[d], agb_r.at[d], {"gx": peers[d]})
        for d in range(1, GX)
    ]
    bias_forward = remote(bias_place, bias_place, fw_s.at[0, GX], fw_r.at[0, GX], {"gy": sib})

    def to_pair(part):
        pws[:, whole(part), :] = pwf[:, whole(part), :].astype(BF)
        pair[part].start()

    def to_members(part):
        pair[part].wait_recv()
        csum[whole(part), :] = (
            pwf[core, whole(part), :] + cbuf[whole(part), :].astype(F32)
        ).astype(BF)
        for copy in scatter[part]:
            copy.start()
        if part == 0:
            for d in range(1, GX):
                pl.when(me + d == GX)(bias_scatter[d - 1].start)

    def to_z(part):
        for copy in scatter[part]:
            copy.wait_recv()
        total = csum[rows_of(part, me), :].astype(F32)
        for d in range(1, GX):
            total = total + arrived[part][d].astype(F32)
        by_z[part][pl.ds(z, 1)] = total[None]
        for copy in over_z[part]:
            copy.start()
        if part == 0:

            @pl.when(me == 0)
            def _():
                for copy in bias_scatter:
                    copy.wait_recv()
                sums = csum[512:528, :].astype(F32)
                for d in range(1, GX):
                    sums = sums + rsbias[d].astype(F32)
                zbias[pl.ds(z, 1)] = sums[None]
                for copy in bias_z:
                    copy.start()

    def to_all(part):
        for copy in over_z[part]:
            copy.wait_recv()
        sums = by_z[part]
        total = (sums[0] + sums[1]) + (sums[2] + sums[3])
        ag[pl.ds(core, 1), rows_of(part, me), :] = total.astype(BF)[None]
        for copy in gathers[part]:
            copy.start()
        forwards[part][0].start()
        if part == 0:

            @pl.when(me == 0)
            def _():
                for copy in bias_z:
                    copy.wait_recv()
                sums = (zbias[0] + zbias[1]) + (zbias[2] + zbias[3])
                ag[pl.ds(core, 1), 512:528, :] = sums.astype(BF)[None]
                for copy in bias_gathers:
                    copy.start()

    def to_other_core(part):
        for d in range(1, GX):
            gathers[part][d - 1].wait_recv()
            forwards[part][d].start()
        if part == 0:
            for d in range(1, GX):
                pl.when(me == d)(bias_gathers[d - 1].wait_recv)
            bias_forward.start()

    grads = dnt(xt[...], gp[...])
    for c in range(2):
        pwf[c, 0:528, :] = grads[:, c * HW : (c + 1) * HW]
    to_pair(0)

    w2v = w2[...]

    def segment_sums(b, carry):
        first = b * 256
        edge_hot = one_hot(mseg[:1, :], first, 256)
        high, low = split(dnt(edge_hot, hid[...]))
        node_hot = one_hot(id_row(segs, 0, N // 128), first, 256)
        part = dot(high, w2v) + dot(low, w2v) + dot(node_hot, nodes[...])
        for i in range(8):
            psend[b * 8 + i] = part[i * SR : (i + 1) * SR]
        lines_t = line_t[:, block(b, 256)]
        add = dot(lines_t, high) + dot(lines_t, low)
        for c in range(2):
            pwf[c, 528:784, :] = pwf[c, 528:784, :] + add[:, c * HW : (c + 1) * HW]
        pl.when(b == 0)(functools.partial(to_members, 0))
        return carry

    pwf[:, 528:784, :] = jnp.zeros((2, 256, HW), F32)
    lax.fori_loop(0, SEG // 256, segment_sums, 0)
    to_pair(1)
    pools = [
        remote(
            psend.at[peers[d]],
            precv.at[d],
            p_s.at[d],
            p_r.at[d],
            {"gx": peers[d]},
        )
        for d in range(1, GX)
    ]
    for copy in pools:
        copy.start()

    def input_grads(b, carry):
        grads = dot(w1[...], gp[:, block(b)]).astype(BF)
        gi[:, block(b)] = grads[F:]
        for k in range(W // T):
            gis[b * (W // T) + k] = grads[:F, k * T : (k + 1) * T]
        return carry

    lax.fori_loop(0, E // W, input_grads, 0)
    to_members(1)
    to_z(0)

    def source_sums(g, carry):
        total = run[...]
        for k in range(5):
            p = g * 5 + k
            run_of, tile_of, earlier, hot = meeting(p)
            same = planned(earlier, 1, TILES) == tile_of
            total = jnp.where(same, total, 0.0) + dnt(hot, gis[run_of])
            sums_s[p] = total
        run[...] = total
        return carry

    run[...] = jnp.zeros_like(run)
    lax.fori_loop(0, STEPS // 5, source_sums, 0)

    for j in range(2):
        slots = sums_s[planned(33, N // T + j, STEPS)].astype(BF)
        gslot[2 * j] = slots[:NB]
        gslot[2 * j + 1] = slots[NB:]
    back = (
        remote(gslot.at[0], gret.at[0], g_s.at[0], g_r.at[0], {"gx": lax.rem(me + GX - 1, GX)}),
        remote(gslot.at[1], gret.at[1], g_s.at[1], g_r.at[1], {"gx": lax.rem(me + 1, GX)}),
        remote(gslot.at[2], gret.at[2], g_s.at[2], g_r.at[2], {"gy": lax.rem(my + GY - 1, GY)}),
        remote(gslot.at[3], gret.at[3], g_s.at[3], g_r.at[3], {"gy": lax.rem(my + 1, GY)}),
    )
    for k in range(4):
        pl.when(there[k])(back[k].start)

    def own(b, carry):
        first = b * 512
        s = jnp.concatenate(
            [sums_s[planned(33, b * 2 + k, STEPS)] for k in range(2)], axis=0
        )
        t = dnt(one_hot(id_row(tgt, 0, 32), first, 512), gi[...])
        acc[block(b, 512), :] = s + t

        @pl.when(b == 0)
        def _():
            to_z(1)
            to_all(0)

        pl.when(b == 1)(functools.partial(to_all, 1))
        pl.when(b == 3)(functools.partial(to_other_core, 0))
        return carry

    lax.fori_loop(0, N // 512, own, 0)

    ret = jnp.zeros((NB, F), F32)
    for k, here in enumerate((there[1], there[0], there[3], there[2])):
        pl.when(here)(back[k].wait_recv)

        @pl.when(jnp.logical_not(here))
        def _(k=k):
            gret[k] = jnp.zeros((NB, F), BF)

        ret = ret + gret[k].astype(F32)
    ret_parts = jnp.concatenate(split(ret), axis=0)
    lines = jnp.concatenate([line[g] for g in range(GX)], axis=0)
    seg_cols = jnp.transpose(segs[...].astype(F32)).astype(jnp.int32)
    stores = []
    for r in range(N // 128):
        rows = slice(r * 128, (r + 1) * 128)
        seg_hot = jnp.where(
            lax.broadcasted_iota(jnp.int32, (128, SEG), 1) == seg_cols[:, r : r + 1], 1.0, 0.0
        ).astype(BF)
        place_hot = one_hot(brows[...], r * 128, 128)
        place_hot = jnp.concatenate([place_hot, place_hot], axis=1)
        gnodes[rows, :] = (acc[rows, :] + dot(seg_hot, lines) + dot(place_hot, ret_parts)).astype(
            BF
        )
        if r % 4 == 3:
            done = pl.ds((r - 3) * 128, 512)
            stores.append(
                pltpu.make_async_copy(gnodes.at[done], gnodes_h.at[done], out_s.at[r // 4])
            )
            stores[-1].start()

    for copy in pools:
        copy.wait_recv()
    sums = psend[me]
    for d in range(1, GX):
        sums = sums + precv[d]
    pooled[...] = sums.astype(BF)
    stores.append(pltpu.make_async_copy(pooled, pooled_h, out_s.at[4]))
    stores[-1].start()

    to_other_core(1)
    for part in range(2):
        for copy in forwards[part]:
            copy.wait_recv()
    bias_forward.wait_recv()
    stores.append(pltpu.make_async_copy(ag, gw_h, out_s.at[5]))
    stores[-1].start()

    for k in range(4):
        pl.when(there[k])(halo[k].wait_send)
        pl.when(there[k])(back[k].wait_send)
    for group in (cots, pools, pair, [bias_forward], *scatter, *over_z, *gathers, *forwards):
        for copy in group:
            copy.wait_send()
    for d in range(1, GX):
        pl.when(me + d == GX)(bias_scatter[d - 1].wait_send)

    @pl.when(me == 0)
    def _():
        for copy in bias_z:
            copy.wait_send()
        for copy in bias_gathers:
            copy.wait_send()

    for copy in stores:
        copy.wait()


def finish(
    scale,
    pooled,
    gnodes,
    gw,
    pooled_o,
    gnodes_o,
    first_o,
    bias_o,
    second_o,
    pooled_v,
    gnodes_v,
    gw_v,
    first_v,
    bias_v,
    second_v,
    sems,
):
    def move(source, target, number):
        copy = pltpu.make_async_copy(source, target, sems.at[number])
        copy.start()
        return copy

    coming = [move(gw.at[c], gw_v.at[c], c) for c in range(2)]
    parts = [pl.ds(i * (N // 2), N // 2) for i in range(2)]
    rows = [move(gnodes.at[part], gnodes_v.at[part], 2 + i) for i, part in enumerate(parts)]
    small = move(pooled, pooled_v, 4)
    unit = eye(HW)
    going = []
    for c in range(2):
        half = slice(c * HW, (c + 1) * HW)
        coming[c].wait()
        first_v[:, half] = gw_v[c, 0:512, :].astype(F32) * scale
        bias_v[:, half] = gw_v[c, 512:528, :].astype(F32)[:1] * scale
        second_v[half, :] = dnt(unit, gw_v[c, 528:784, :]) * scale
        place = pl.ds(c * HW, HW)
        going.append(move(second_v.at[place], second_o.at[place], 5 + c))
    going.append(move(first_v, first_o, 7))
    going.append(move(bias_v, bias_o, 8))
    for i, part in enumerate(parts):
        rows[i].wait()
        going.append(move(gnodes_v.at[part], gnodes_o.at[part], 9 + i))
    small.wait()
    going.append(move(pooled_v, pooled_o, 11))
    for copy in going:
        copy.wait()


def local(nodes, brows, src, tgt, mask, segs, w1, b1, w2, cot):
    dma = pltpu.SemaphoreType.DMA
    int32 = jnp.int32
    arguments = (
        nodes,
        brows.reshape(1, NB),
        src,
        tgt,
        mask,
        segs.reshape(N // 128, 128),
        w1,
        b1.reshape(1, H),
        w2,
        cot,
    )
    scratch = [pltpu.VMEM(a.shape, a.dtype) for a in arguments]
    scratch += [
        pltpu.VMEM((SR, F), BF),
        pltpu.VMEM((N, F), BF),
        pltpu.VMEM((F, N), BF),
        pltpu.VMEM((TILES, F, T), BF),
        pltpu.VMEM((32, 128), int32),
        pltpu.VMEM((40, 128), int32),
        pltpu.SMEM((40, 128), int32),
        pltpu.VMEM((STEPS, F, T), BF),
        pltpu.VMEM((RUNS, F, T), BF),
        pltpu.VMEM((STEPS, T, F), F32),
        pltpu.VMEM((T, F), F32),
        pltpu.VMEM((H, 2 * F), BF),
        pltpu.VMEM((H, 128), F32),
        pltpu.VMEM((F, NB), BF),
        pltpu.VMEM((4, F, NB), BF),
        pltpu.VMEM((GX, SR, F), BF),
        pltpu.VMEM((F, SEG), BF),
        pltpu.VMEM((2 * F + 16, E), BF),
        pltpu.VMEM((8, E), int32),
        pltpu.VMEM((H, E), BF),
        pltpu.VMEM((H, E), BF),
        pltpu.VMEM((F, E), BF),
        pltpu.VMEM((2, PW, HW), F32),
        pltpu.VMEM((2, PW, HW), BF),
        pltpu.VMEM((PW, HW), BF),
        pltpu.VMEM((PW, HW), BF),
        pltpu.VMEM((GX, 32, HW), BF),
        pltpu.VMEM((GX, 16, HW), BF),
        pltpu.VMEM((GX, 16, HW), BF),
        pltpu.VMEM((4, 32, HW), F32),
        pltpu.VMEM((4, 16, HW), F32),
        pltpu.VMEM((4, 16, HW), F32),
        pltpu.VMEM((2, PW, HW), BF),
        pltpu.VMEM((GX, SR, F), F32),
        pltpu.VMEM((GX, SR, F), F32),
        pltpu.VMEM((4, NB, F), BF),
        pltpu.VMEM((4, NB, F), BF),
        pltpu.VMEM((N, F), F32),
        dma((10,)),
        dma((6,)),
        dma,
    ]
    for shape in (
        (4,),
        (GX,),
        (GX,),
        (4,),
        (2,),
        (2, GX),
        (GX,),
        (2, 4),
        (4,),
        (2, GX),
        (GX,),
        (2, GX + 1),
    ):
        scratch += [dma(shape), dma(shape)]
    anywhere = pl.BlockSpec(memory_space=pl.ANY)
    outs = (
        jax.ShapeDtypeStruct((SR, F), BF),
        jax.ShapeDtypeStruct((N, F), BF),
    )
    pooled, gnodes, gw = pl.pallas_call(
        kernel,
        out_shape=(*outs, jax.ShapeDtypeStruct((2, PW, HW), BF)),
        in_specs=[anywhere] * 10,
        out_specs=(anywhere,) * 3,
        scratch_shapes=scratch,
        compiler_params=pltpu.CompilerParams(
            collective_id=0, has_side_effects=True, vmem_limit_bytes=60 * 2**20
        ),
    )(*arguments)
    pooled, gnodes, first, bias, second = pl.pallas_call(
        functools.partial(finish, float((E * GX * GY) ** -0.5)),
        out_shape=(
            *outs,
            jax.ShapeDtypeStruct((H, H), F32),
            jax.ShapeDtypeStruct((1, H), F32),
            jax.ShapeDtypeStruct((H, F), F32),
        ),
        in_specs=[anywhere] * 3,
        out_specs=(anywhere,) * 5,
        scratch_shapes=[
            pltpu.VMEM((SR, F), BF),
            pltpu.VMEM((N, F), BF),
            pltpu.VMEM((2, PW, HW), BF),
            pltpu.VMEM((H, H), F32),
            pltpu.VMEM((1, H), F32),
            pltpu.VMEM((H, F), F32),
            dma((12,)),
        ],
        compiler_params=pltpu.CompilerParams(vmem_limit_bytes=60 * 2**20),
    )(pooled, gnodes, gw)
    return pooled, gnodes, first, bias.reshape(H), second


def solution(mesh):
    in_specs = (
        P(("gx", "gy"), None),
        P(("gx", "gy")),
        P(("gx", "gy"), None),
        P(("gx", "gy"), None),
        P(("gx", "gy"), None),
        P(("gx", "gy")),
        P(),
        P(),
        P(),
        P(("gx", "gy"), None),
    )
    out_specs = (P(("gx", "gy"), None), P(("gx", "gy"), None), P(), P(), P())
    return jax.shard_map(local, mesh=mesh, in_specs=in_specs, out_specs=out_specs, check_vma=False)
```

```python
import functools

import jax
import jax.numpy as jnp
from jax import lax
from jax.experimental import pallas as pl
from jax.experimental.pallas import tpu as pltpu
from jax.sharding import PartitionSpec as P

MESH = pl.DeviceIdType.MESH
BF = jnp.bfloat16
F32 = jnp.float32
N = 2048
NB = 128
HALO = 4 * NB
F = 256
H = 512
E = 4096
SEG = 512
SR = 32
GX = 16
GY = 8
W = 1024
T = 256
TILES = (N + HALO) // T
RUNS = E // T
STEPS = TILES + RUNS - 1
KINDS = 12
PW = 784
HW = H // 2
NT = (((1,), (1,)), ((), ()))


def dot(a, b):
    return jnp.dot(a, b, preferred_element_type=F32)


def dnt(a, b):
    return lax.dot_general(a, b, NT, preferred_element_type=F32)


def one_hot(row, first, count):
    rows = lax.broadcasted_iota(jnp.int32, (count, row.shape[1]), 0)
    return jnp.where(rows == row - first, 1.0, 0.0).astype(BF)


def id_row(ref, first, count):
    return jnp.concatenate([ref[pl.ds(first + i, 1), :] for i in range(count)], axis=1)


def eye(size):
    a = lax.broadcasted_iota(jnp.int32, (size, size), 0)
    b = lax.broadcasted_iota(jnp.int32, (size, size), 1)
    return jnp.where(a == b, 1.0, 0.0).astype(BF)


def ordered(size, earlier_row):
    a = lax.broadcasted_iota(jnp.int32, (size, size), 0)
    b = lax.broadcasted_iota(jnp.int32, (size, size), 1)
    return jnp.where(a < b if earlier_row else b < a, 1.0, 0.0).astype(BF)


def sort_edges(src, tgt, mask, spot, plan):
    tile = jnp.right_shift(src[...], 8)
    inside = jnp.concatenate(
        [jnp.where(tile == j, 1.0, 0.0).astype(BF) for j in range(KINDS)], axis=0
    )
    before = dot(inside, ordered(128, True))
    counts = dot(inside, jnp.ones((128, 128), BF)).astype(BF)
    base = dot(ordered(32 * KINDS, False), counts)
    places = jnp.zeros((32, 128), F32)
    for j in range(TILES):
        rows = slice(32 * j, 32 * j + 32)
        places = places + jnp.where(tile == j, before[rows] + base[rows], 0.0)
    spot[...] = places.astype(jnp.int32)

    place = id_row(spot, 0, 32)
    sources = id_row(src, 0, 32)
    targets = id_row(tgt, 0, 32)
    live = id_row(mask, 0, 32)
    here = lax.broadcasted_iota(jnp.int32, (32, E), 0) == jnp.right_shift(place, 7)
    parts = (
        jnp.bitwise_and(sources, 255),
        jnp.bitwise_and(targets, 255),
        jnp.right_shift(sources, 8) * 16 + jnp.right_shift(targets, 8),
        live,
    )
    parts = [jnp.where(here, part.astype(F32), 0.0).astype(BF) for part in parts]
    moved = dnt(
        jnp.concatenate(parts, axis=0), one_hot(jnp.bitwise_and(place, 127), 0, 128)
    ).astype(jnp.int32)
    upper = moved[64:96]
    src[...] = moved[0:32] + 256 * jnp.right_shift(upper, 4)
    tgt[...] = moved[32:64] + 256 * jnp.bitwise_and(upper, 15)
    mask[...] = moved[96:128]

    lane = lax.broadcasted_iota(jnp.int32, (1, 128), 1)
    border = jnp.zeros((1, 128), F32)
    for j in range(1, TILES):
        border = jnp.where(lane == j, base[32 * j : 32 * j + 1], border)
    passed = jnp.minimum(jnp.right_shift(border.astype(jnp.int32), 8), RUNS - 1)
    rank = jnp.where((lane >= 1) & (lane < TILES), lane - 1 + passed, 1000)
    step = lax.broadcasted_iota(jnp.int32, (32, 128), 0)
    wide = lax.broadcasted_iota(jnp.int32, (32, 128), 1)
    table_tile = jnp.sum(jnp.where(rank < step, 1.0, 0.0), axis=1, keepdims=True).astype(
        jnp.int32
    )
    table_tile = jnp.broadcast_to(table_tile, (32, 128))
    edge_tile = step - table_tile
    plan[0:32, :] = jnp.where(wide == 0, edge_tile, table_tile)
    for row, which in ((32, edge_tile), (33, table_tile)):
        upto = jnp.where((which <= wide) & (step < STEPS), 1.0, 0.0)
        plan[row : row + 1, :] = jnp.sum(upto, axis=0, keepdims=True).astype(jnp.int32) - 1


def split(value):
    high = value.astype(BF)
    return high, (value - high.astype(F32)).astype(BF)


def kernel(
    nodes_h,
    brows_h,
    src_h,
    tgt_h,
    mask_h,
    segs_h,
    w1_h,
    b1_h,
    w2_h,
    cot_h,
    pooled_h,
    gnodes_h,
    gw_h,
    nodes,
    brows,
    src,
    tgt,
    mask,
    segs,
    w1,
    b1,
    w2,
    cot,
    pooled,
    gnodes,
    tt,
    tiles,
    spot,
    plan_v,
    plan,
    xs,
    gis,
    sums_s,
    run,
    w1t,
    bcol,
    bnd,
    hrecv,
    line,
    line_t,
    xt,
    mseg,
    hid,
    gp,
    gi,
    pwf,
    pws,
    cbuf,
    csum,
    rsb_a,
    rsb_b,
    rsbias,
    zb_a,
    zb_b,
    zbias,
    ag,
    psum,
    psend,
    precv,
    gslot,
    gret,
    acc,
    in_s,
    out_s,
    plan_s,
    h_s,
    h_r,
    c_s,
    c_r,
    p_s,
    p_r,
    g_s,
    g_r,
    core_s,
    core_r,
    rs_s,
    rs_r,
    rb_s,
    rb_r,
    z_s,
    z_r,
    zb_s,
    zb_r,
    ag_s,
    ag_r,
    agb_s,
    agb_r,
    fw_s,
    fw_r,
):
    me = lax.axis_index("gx")
    my = lax.axis_index("gy")
    core = lax.rem(my, 2)
    z = lax.div(my, 2)
    sib = my + 1 - 2 * core

    barrier = pltpu.get_barrier_semaphore()
    for d in range(1, GX):
        pl.semaphore_signal(
            barrier, inc=1, device_id={"gx": lax.rem(me + d, GX)}, device_id_type=MESH
        )
    for d in range(1, GY):
        pl.semaphore_signal(
            barrier, inc=1, device_id={"gy": lax.rem(my + d, GY)}, device_id_type=MESH
        )

    def remote(source, target, send, receive, device):
        return pltpu.make_async_remote_copy(
            src_ref=source,
            dst_ref=target,
            send_sem=send,
            recv_sem=receive,
            device_id=device,
            device_id_type=MESH,
        )

    pairs = (
        (nodes_h, nodes),
        (brows_h, brows),
        (cot_h, cot),
        (w1_h, w1),
        (b1_h, b1),
        (segs_h, segs),
        (tgt_h, tgt),
        (src_h, src),
        (mask_h, mask),
        (w2_h, w2),
    )
    loads = [pltpu.make_async_copy(a, b, in_s.at[i]) for i, (a, b) in enumerate(pairs)]
    for copy in loads:
        copy.start()

    unit = eye(F)
    for copy in loads[:3]:
        copy.wait()
    tt[...] = dnt(unit, nodes[...]).astype(BF)
    bnd[...] = dot(tt[...], one_hot(brows[...], 0, N)).astype(BF)
    line[pl.ds(me, 1)] = cot[...][None]

    pl.semaphore_wait(barrier, GX - 1 + GY - 1)

    there = (me > 0, me < GX - 1, my > 0, my < GY - 1)
    halo = (
        remote(bnd, hrecv.at[1], h_s.at[1], h_r.at[1], {"gx": lax.rem(me + GX - 1, GX)}),
        remote(bnd, hrecv.at[0], h_s.at[0], h_r.at[0], {"gx": lax.rem(me + 1, GX)}),
        remote(bnd, hrecv.at[3], h_s.at[3], h_r.at[3], {"gy": lax.rem(my + GY - 1, GY)}),
        remote(bnd, hrecv.at[2], h_s.at[2], h_r.at[2], {"gy": lax.rem(my + 1, GY)}),
    )
    for k in range(4):
        pl.when(there[k])(halo[k].start)
    cots = [
        remote(
            cot,
            line.at[me],
            c_s.at[d],
            c_r.at[d],
            {"gx": lax.rem(me + d, GX)},
        )
        for d in range(1, GX)
    ]
    for copy in cots:
        copy.start()
    for copy in loads[3:]:
        copy.wait()

    sort_edges(src, tgt, mask, spot, plan_v)
    to_plan = pltpu.make_async_copy(plan_v, plan, plan_s)
    to_plan.start()
    for j in range(N // T):
        tiles[j] = tt[:, j * T : (j + 1) * T]

    for i in range(2):
        for j in range(2):
            w1t[j * F : (j + 1) * F, i * F : (i + 1) * F] = dnt(
                unit, w1[i * F : (i + 1) * F, j * F : (j + 1) * F]
            ).astype(BF)
    bcol[...] = jnp.broadcast_to(
        jnp.transpose(jnp.broadcast_to(b1[...], (8, H)))[:, :1], (H, 128)
    )
    xt[2 * F :, :] = jnp.ones((16, E), BF)
    seg_ids = segs[...]
    seg_parts = jnp.concatenate(
        [
            jnp.bitwise_and(seg_ids, 255).astype(F32).astype(BF),
            jnp.right_shift(seg_ids, 8).astype(F32).astype(BF),
        ],
        axis=0,
    )

    def block(b, width=W):
        return pl.ds(pl.multiple_of(b * width, width), width)

    def gather(b, carry):
        targets = id_row(tgt, b * 8, 8)
        live = id_row(mask, b * 8, 8)
        low = one_hot(jnp.bitwise_and(targets, 127), 0, 128)
        found = dot(seg_parts, low)
        found = found[:16] + 256.0 * found[16:]
        high = lax.broadcasted_iota(jnp.int32, (16, W), 0) == jnp.right_shift(targets, 7)
        segment = jnp.sum(jnp.where(high, found, 0.0), axis=0, keepdims=True)
        segment = jnp.where(live > 0, segment, -1.0).astype(jnp.int32)
        mseg[:, block(b)] = jnp.broadcast_to(segment, (8, W))
        xt[F : 2 * F, block(b)] = dot(tt[...], one_hot(targets, 0, N)).astype(BF)
        return carry

    lax.fori_loop(0, E // W, gather, 0)

    for k, coming in enumerate((halo[1], halo[0], halo[3], halo[2])):
        pl.when(there[k])(coming.wait_recv)

        @pl.when(jnp.logical_not(there[k]))
        def _(k=k):
            hrecv[k] = jnp.zeros((F, NB), BF)

    for j in range(2):
        tiles[N // T + j] = jnp.concatenate([hrecv[2 * j], hrecv[2 * j + 1]], axis=1)
    for copy in cots:
        copy.wait_recv()
    lines = jnp.concatenate([line[g] for g in range(GX)], axis=0)
    line_t[...] = dnt(unit, lines).astype(BF)

    to_plan.wait()

    def planned(row, column, count):
        return jnp.clip(plan[row, column], 0, count - 1)

    def meeting(p):
        run_of, tile_of = planned(p, 0, RUNS), planned(p, 1, TILES)
        earlier = jnp.maximum(p - 1, 0)
        hot = one_hot(id_row(src, run_of * (T // 128), T // 128), tile_of * T, T)
        return run_of, tile_of, earlier, hot

    def source_rows(g, carry):
        total = run[...]
        for k in range(5):
            p = g * 5 + k
            run_of, tile_of, earlier, hot = meeting(p)
            same = planned(earlier, 0, RUNS) == run_of
            total = jnp.where(same, total, 0.0) + dot(tiles[tile_of], hot)
            xs[p] = total.astype(BF)
        run[...] = total
        return carry

    run[...] = jnp.zeros_like(run)
    lax.fori_loop(0, STEPS // 5, source_rows, 0)

    def edges(b, carry):
        for k in range(W // T):
            xt[:F, block(b * (W // T) + k, T)] = xs[planned(32, b * (W // T) + k, STEPS)]
        chosen = one_hot(mseg[:1, block(b)], 0, SEG)
        gm = dot(line_t[...], chosen).astype(BF)
        bias = jnp.concatenate([bcol[...]] * (W // 128), axis=1)
        x = dot(w1t[...], xt[: 2 * F, block(b)]) + bias
        gh = dot(w2[...], gm)
        square = x * x
        t = jnp.tanh(x * (0.7978845608028654 + 0.035677408136300125 * square))
        half = 0.5 + 0.5 * t
        hid[:, block(b)] = (x * half).astype(BF)
        slope = half + (0.5 * x) * (1.0 - t * t) * (
            0.7978845608028654 + 0.10703222440890037 * square
        )
        gp[:, block(b)] = (gh * slope).astype(BF)
        return carry

    lax.fori_loop(0, E // W, edges, 0)

    firsts, counts = (0, 528), (528, 256)
    shares = (32, 16)
    arrived = (rsb_a, rsb_b)
    by_z = (zb_a, zb_b)

    def rows_of(part, member):
        return pl.ds(pl.multiple_of(firsts[part] + member * shares[part], 16), shares[part])

    def whole(part):
        return pl.ds(firsts[part], counts[part])

    peers = [lax.rem(me + d, GX) for d in range(GX)]
    pair, scatter, over_z, gathers, forwards = [], [], [], [], []
    for part in range(2):
        pair.append(
            remote(
                pws.at[1 - core, whole(part)],
                cbuf.at[whole(part)],
                core_s.at[part],
                core_r.at[part],
                {"gy": sib},
            )
        )
        scatter.append(
            [
                remote(
                    csum.at[rows_of(part, peers[d])],
                    arrived[part].at[d],
                    rs_s.at[part, d],
                    rs_r.at[part, d],
                    {"gx": peers[d]},
                )
                for d in range(1, GX)
            ]
        )
        over_z.append(
            [
                remote(
                    by_z[part].at[z],
                    by_z[part].at[z],
                    z_s.at[part, d],
                    z_r.at[part, d],
                    {"gy": lax.rem(my + 2 * d, GY)},
                )
                for d in range(1, 4)
            ]
        )
        place = ag.at[core, rows_of(part, me)]
        gathers.append(
            [
                remote(place, place, ag_s.at[part, d], ag_r.at[part, d], {"gx": peers[d]})
                for d in range(1, GX)
            ]
        )
        ways = []
        for d in range(GX):
            place = ag.at[core, rows_of(part, lax.rem(me + GX - d, GX))]
            ways.append(remote(place, place, fw_s.at[part, d], fw_r.at[part, d], {"gy": sib}))
        forwards.append(ways)
    bias_rows = csum.at[pl.ds(512, 16)]
    bias_scatter = [
        remote(bias_rows, rsbias.at[d], rb_s.at[d], rb_r.at[d], {"gx": peers[d]})
        for d in range(1, GX)
    ]
    bias_z = [
        remote(zbias.at[z], zbias.at[z], zb_s.at[d], zb_r.at[d], {"gy": lax.rem(my + 2 * d, GY)})
        for d in range(1, 4)
    ]
    bias_place = ag.at[core, pl.ds(512, 16)]
    bias_gathers = [
        remote(bias_place, bias_place, agb_s.at[d], agb_r.at[d], {"gx": peers[d]})
        for d in range(1, GX)
    ]
    bias_forward = remote(bias_place, bias_place, fw_s.at[0, GX], fw_r.at[0, GX], {"gy": sib})

    def to_pair(part):
        pws[:, whole(part), :] = pwf[:, whole(part), :].astype(BF)
        pair[part].start()

    def to_members(part):
        pair[part].wait_recv()
        csum[whole(part), :] = (
            pwf[core, whole(part), :] + cbuf[whole(part), :].astype(F32)
        ).astype(BF)
        for copy in scatter[part]:
            copy.start()
        if part == 0:
            for d in range(1, GX):
                pl.when(me + d == GX)(bias_scatter[d - 1].start)

    def to_z(part):
        for copy in scatter[part]:
            copy.wait_recv()
        total = csum[rows_of(part, me), :].astype(F32)
        for d in range(1, GX):
            total = total + arrived[part][d].astype(F32)
        by_z[part][pl.ds(z, 1)] = total[None]
        for copy in over_z[part]:
            copy.start()
        if part == 0:

            @pl.when(me == 0)
            def _():
                for copy in bias_scatter:
                    copy.wait_recv()
                sums = csum[512:528, :].astype(F32)
                for d in range(1, GX):
                    sums = sums + rsbias[d].astype(F32)
                zbias[pl.ds(z, 1)] = sums[None]
                for copy in bias_z:
                    copy.start()

    def to_all(part):
        for copy in over_z[part]:
            copy.wait_recv()
        sums = by_z[part]
        total = (sums[0] + sums[1]) + (sums[2] + sums[3])
        ag[pl.ds(core, 1), rows_of(part, me), :] = total.astype(BF)[None]
        for copy in gathers[part]:
            copy.start()
        forwards[part][0].start()
        if part == 0:

            @pl.when(me == 0)
            def _():
                for copy in bias_z:
                    copy.wait_recv()
                sums = (zbias[0] + zbias[1]) + (zbias[2] + zbias[3])
                ag[pl.ds(core, 1), 512:528, :] = sums.astype(BF)[None]
                for copy in bias_gathers:
                    copy.start()

    def to_other_core(part):
        for d in range(1, GX):
            gathers[part][d - 1].wait_recv()
            forwards[part][d].start()
        if part == 0:
            for d in range(1, GX):
                pl.when(me == d)(bias_gathers[d - 1].wait_recv)
            bias_forward.start()

    grads = dnt(xt[...], gp[...])
    for c in range(2):
        pwf[c, 0:528, :] = grads[:, c * HW : (c + 1) * HW]
    to_pair(0)

    w2v = w2[...]

    def segment_sums(b, carry):
        first = b * 256
        edge_hot = one_hot(mseg[:1, :], first, 256)
        high, low = split(dnt(edge_hot, hid[...]))
        node_hot = one_hot(id_row(segs, 0, N // 128), first, 256)
        part = dot(high, w2v) + dot(low, w2v) + dot(node_hot, nodes[...])
        for i in range(8):
            psum[b * 8 + i] = part[i * SR : (i + 1) * SR]
            psend[b * 8 + i] = part[i * SR : (i + 1) * SR].astype(BF)
        lines_t = line_t[:, block(b, 256)]
        add = dot(lines_t, high) + dot(lines_t, low)
        for c in range(2):
            pwf[c, 528:784, :] = pwf[c, 528:784, :] + add[:, c * HW : (c + 1) * HW]
        pl.when(b == 0)(functools.partial(to_members, 0))
        return carry

    pwf[:, 528:784, :] = jnp.zeros((2, 256, HW), F32)
    lax.fori_loop(0, SEG // 256, segment_sums, 0)
    to_pair(1)
    pools = [
        remote(
            psend.at[peers[d]],
            precv.at[d],
            p_s.at[d],
            p_r.at[d],
            {"gx": peers[d]},
        )
        for d in range(1, GX)
    ]
    def input_grads(b, carry):
        grads = dot(w1[...], gp[:, block(b)]).astype(BF)
        gi[:, block(b)] = grads[F:]
        for k in range(W // T):
            gis[b * (W // T) + k] = grads[:F, k * T : (k + 1) * T]
        return carry

    lax.fori_loop(0, E // W, input_grads, 0)
    to_members(1)
    to_z(0)
    for copy in pools:
        copy.start()

    def source_sums(g, carry):
        total = run[...]
        for k in range(5):
            p = g * 5 + k
            run_of, tile_of, earlier, hot = meeting(p)
            same = planned(earlier, 1, TILES) == tile_of
            total = jnp.where(same, total, 0.0) + dnt(hot, gis[run_of])
            sums_s[p] = total
        run[...] = total
        return carry

    run[...] = jnp.zeros_like(run)
    lax.fori_loop(0, STEPS // 5, source_sums, 0)

    for j in range(2):
        slots = sums_s[planned(33, N // T + j, STEPS)].astype(BF)
        gslot[2 * j] = slots[:NB]
        gslot[2 * j + 1] = slots[NB:]
    back = (
        remote(gslot.at[0], gret.at[0], g_s.at[0], g_r.at[0], {"gx": lax.rem(me + GX - 1, GX)}),
        remote(gslot.at[1], gret.at[1], g_s.at[1], g_r.at[1], {"gx": lax.rem(me + 1, GX)}),
        remote(gslot.at[2], gret.at[2], g_s.at[2], g_r.at[2], {"gy": lax.rem(my + GY - 1, GY)}),
        remote(gslot.at[3], gret.at[3], g_s.at[3], g_r.at[3], {"gy": lax.rem(my + 1, GY)}),
    )
    for k in range(4):
        pl.when(there[k])(back[k].start)

    def own(b, carry):
        first = b * 512
        s = jnp.concatenate(
            [sums_s[planned(33, b * 2 + k, STEPS)] for k in range(2)], axis=0
        )
        t = dnt(one_hot(id_row(tgt, 0, 32), first, 512), gi[...])
        acc[block(b, 512), :] = s + t

        @pl.when(b == 0)
        def _():
            to_z(1)
            to_all(0)

        pl.when(b == 1)(functools.partial(to_all, 1))
        return carry

    lax.fori_loop(0, N // 512, own, 0)

    ret = jnp.zeros((NB, F), F32)
    for k, here in enumerate((there[1], there[0], there[3], there[2])):
        pl.when(here)(back[k].wait_recv)

        @pl.when(jnp.logical_not(here))
        def _(k=k):
            gret[k] = jnp.zeros((NB, F), BF)

        ret = ret + gret[k].astype(F32)
    ret_parts = jnp.concatenate(split(ret), axis=0)
    lines = jnp.concatenate([line[g] for g in range(GX)], axis=0)
    seg_cols = jnp.transpose(segs[...].astype(F32)).astype(jnp.int32)
    stores = []
    for r in range(N // 128):
        rows = slice(r * 128, (r + 1) * 128)
        seg_hot = jnp.where(
            lax.broadcasted_iota(jnp.int32, (128, SEG), 1) == seg_cols[:, r : r + 1], 1.0, 0.0
        ).astype(BF)
        place_hot = one_hot(brows[...], r * 128, 128)
        place_hot = jnp.concatenate([place_hot, place_hot], axis=1)
        gnodes[rows, :] = (acc[rows, :] + dot(seg_hot, lines) + dot(place_hot, ret_parts)).astype(
            BF
        )
        if r % 4 == 3:
            done = pl.ds((r - 3) * 128, 512)
            stores.append(
                pltpu.make_async_copy(gnodes.at[done], gnodes_h.at[done], out_s.at[r // 4])
            )
            stores[-1].start()

    to_other_core(0)

    for copy in pools:
        copy.wait_recv()
    sums = psum[me]
    for d in range(1, GX):
        sums = sums + precv[d].astype(F32)
    pooled[...] = sums.astype(BF)
    stores.append(pltpu.make_async_copy(pooled, pooled_h, out_s.at[4]))
    stores[-1].start()

    to_other_core(1)
    for part in range(2):
        for copy in forwards[part]:
            copy.wait_recv()
    bias_forward.wait_recv()
    stores.append(pltpu.make_async_copy(ag, gw_h, out_s.at[5]))
    stores[-1].start()

    for k in range(4):
        pl.when(there[k])(halo[k].wait_send)
        pl.when(there[k])(back[k].wait_send)
    for group in (cots, pools, pair, [bias_forward], *scatter, *over_z, *gathers, *forwards):
        for copy in group:
            copy.wait_send()
    for d in range(1, GX):
        pl.when(me + d == GX)(bias_scatter[d - 1].wait_send)

    @pl.when(me == 0)
    def _():
        for copy in bias_z:
            copy.wait_send()
        for copy in bias_gathers:
            copy.wait_send()

    for copy in stores:
        copy.wait()


def finish(
    scale,
    pooled,
    gnodes,
    gw,
    pooled_o,
    gnodes_o,
    first_o,
    bias_o,
    second_o,
    pooled_v,
    gnodes_v,
    gw_v,
    first_v,
    bias_v,
    second_v,
    sems,
):
    def move(source, target, number):
        copy = pltpu.make_async_copy(source, target, sems.at[number])
        copy.start()
        return copy

    coming = [move(gw.at[c], gw_v.at[c], c) for c in range(2)]
    parts = [pl.ds(i * (N // 2), N // 2) for i in range(2)]
    rows = [move(gnodes.at[part], gnodes_v.at[part], 2 + i) for i, part in enumerate(parts)]
    small = move(pooled, pooled_v, 4)
    unit = eye(HW)
    going = []
    for c in range(2):
        half = slice(c * HW, (c + 1) * HW)
        coming[c].wait()
        first_v[:, half] = gw_v[c, 0:512, :].astype(F32) * scale
        bias_v[:, half] = gw_v[c, 512:528, :].astype(F32)[:1] * scale
        second_v[half, :] = dnt(unit, gw_v[c, 528:784, :]) * scale
        place = pl.ds(c * HW, HW)
        going.append(move(second_v.at[place], second_o.at[place], 5 + c))
    going.append(move(first_v, first_o, 7))
    going.append(move(bias_v, bias_o, 8))
    for i, part in enumerate(parts):
        rows[i].wait()
        going.append(move(gnodes_v.at[part], gnodes_o.at[part], 9 + i))
    small.wait()
    going.append(move(pooled_v, pooled_o, 11))
    for copy in going:
        copy.wait()


def local(nodes, brows, src, tgt, mask, segs, w1, b1, w2, cot):
    dma = pltpu.SemaphoreType.DMA
    int32 = jnp.int32
    arguments = (
        nodes,
        brows.reshape(1, NB),
        src,
        tgt,
        mask,
        segs.reshape(N // 128, 128),
        w1,
        b1.reshape(1, H),
        w2,
        cot,
    )
    scratch = [pltpu.VMEM(a.shape, a.dtype) for a in arguments]
    scratch += [
        pltpu.VMEM((SR, F), BF),
        pltpu.VMEM((N, F), BF),
        pltpu.VMEM((F, N), BF),
        pltpu.VMEM((TILES, F, T), BF),
        pltpu.VMEM((32, 128), int32),
        pltpu.VMEM((40, 128), int32),
        pltpu.SMEM((40, 128), int32),
        pltpu.VMEM((STEPS, F, T), BF),
        pltpu.VMEM((RUNS, F, T), BF),
        pltpu.VMEM((STEPS, T, F), F32),
        pltpu.VMEM((T, F), F32),
        pltpu.VMEM((H, 2 * F), BF),
        pltpu.VMEM((H, 128), F32),
        pltpu.VMEM((F, NB), BF),
        pltpu.VMEM((4, F, NB), BF),
        pltpu.VMEM((GX, SR, F), BF),
        pltpu.VMEM((F, SEG), BF),
        pltpu.VMEM((2 * F + 16, E), BF),
        pltpu.VMEM((8, E), int32),
        pltpu.VMEM((H, E), BF),
        pltpu.VMEM((H, E), BF),
        pltpu.VMEM((F, E), BF),
        pltpu.VMEM((2, PW, HW), F32),
        pltpu.VMEM((2, PW, HW), BF),
        pltpu.VMEM((PW, HW), BF),
        pltpu.VMEM((PW, HW), BF),
        pltpu.VMEM((GX, 32, HW), BF),
        pltpu.VMEM((GX, 16, HW), BF),
        pltpu.VMEM((GX, 16, HW), BF),
        pltpu.VMEM((4, 32, HW), F32),
        pltpu.VMEM((4, 16, HW), F32),
        pltpu.VMEM((4, 16, HW), F32),
        pltpu.VMEM((2, PW, HW), BF),
        pltpu.VMEM((GX, SR, F), F32),
        pltpu.VMEM((GX, SR, F), BF),
        pltpu.VMEM((GX, SR, F), BF),
        pltpu.VMEM((4, NB, F), BF),
        pltpu.VMEM((4, NB, F), BF),
        pltpu.VMEM((N, F), F32),
        dma((10,)),
        dma((6,)),
        dma,
    ]
    for shape in (
        (4,),
        (GX,),
        (GX,),
        (4,),
        (2,),
        (2, GX),
        (GX,),
        (2, 4),
        (4,),
        (2, GX),
        (GX,),
        (2, GX + 1),
    ):
        scratch += [dma(shape), dma(shape)]
    anywhere = pl.BlockSpec(memory_space=pl.ANY)
    outs = (
        jax.ShapeDtypeStruct((SR, F), BF),
        jax.ShapeDtypeStruct((N, F), BF),
    )
    pooled, gnodes, gw = pl.pallas_call(
        kernel,
        out_shape=(*outs, jax.ShapeDtypeStruct((2, PW, HW), BF)),
        in_specs=[anywhere] * 10,
        out_specs=(anywhere,) * 3,
        scratch_shapes=scratch,
        compiler_params=pltpu.CompilerParams(
            collective_id=0, has_side_effects=True, vmem_limit_bytes=60 * 2**20
        ),
    )(*arguments)
    pooled, gnodes, first, bias, second = pl.pallas_call(
        functools.partial(finish, float((E * GX * GY) ** -0.5)),
        out_shape=(
            *outs,
            jax.ShapeDtypeStruct((H, H), F32),
            jax.ShapeDtypeStruct((1, H), F32),
            jax.ShapeDtypeStruct((H, F), F32),
        ),
        in_specs=[anywhere] * 3,
        out_specs=(anywhere,) * 5,
        scratch_shapes=[
            pltpu.VMEM((SR, F), BF),
            pltpu.VMEM((N, F), BF),
            pltpu.VMEM((2, PW, HW), BF),
            pltpu.VMEM((H, H), F32),
            pltpu.VMEM((1, H), F32),
            pltpu.VMEM((H, F), F32),
            dma((12,)),
        ],
        compiler_params=pltpu.CompilerParams(vmem_limit_bytes=60 * 2**20),
    )(pooled, gnodes, gw)
    return pooled, gnodes, first, bias.reshape(H), second


def solution(mesh):
    in_specs = (
        P(("gx", "gy"), None),
        P(("gx", "gy")),
        P(("gx", "gy"), None),
        P(("gx", "gy"), None),
        P(("gx", "gy"), None),
        P(("gx", "gy")),
        P(),
        P(),
        P(),
        P(("gx", "gy"), None),
    )
    out_specs = (P(("gx", "gy"), None), P(("gx", "gy"), None), P(), P(), P())
    return jax.shard_map(local, mesh=mesh, in_specs=in_specs, out_specs=out_specs, check_vma=False)
```

```python
import functools

import jax
import jax.numpy as jnp
from jax import lax
from jax.experimental import pallas as pl
from jax.experimental.pallas import tpu as pltpu
from jax.sharding import PartitionSpec as P

MESH = pl.DeviceIdType.MESH
BF = jnp.bfloat16
F32 = jnp.float32
N = 2048
NB = 128
HALO = 4 * NB
F = 256
H = 512
E = 4096
SEG = 512
SR = 32
GX = 16
GY = 8
W = 1024
T = 256
TILES = (N + HALO) // T
RUNS = E // T
STEPS = TILES + RUNS - 1
KINDS = 12
PW = 784
HW = H // 2
NT = (((1,), (1,)), ((), ()))


def dot(a, b):
    return jnp.dot(a, b, preferred_element_type=F32)


def dnt(a, b):
    return lax.dot_general(a, b, NT, preferred_element_type=F32)


def one_hot(row, first, count):
    rows = lax.broadcasted_iota(jnp.int32, (count, row.shape[1]), 0)
    return jnp.where(rows == row - first, 1.0, 0.0).astype(BF)


def id_row(ref, first, count):
    return jnp.concatenate([ref[pl.ds(first + i, 1), :] for i in range(count)], axis=1)


def eye(size):
    a = lax.broadcasted_iota(jnp.int32, (size, size), 0)
    b = lax.broadcasted_iota(jnp.int32, (size, size), 1)
    return jnp.where(a == b, 1.0, 0.0).astype(BF)


def ordered(size, earlier_row):
    a = lax.broadcasted_iota(jnp.int32, (size, size), 0)
    b = lax.broadcasted_iota(jnp.int32, (size, size), 1)
    return jnp.where(a < b if earlier_row else b < a, 1.0, 0.0).astype(BF)


def sort_edges(src, tgt, mask, spot, plan):
    tile = jnp.right_shift(src[...], 8)
    inside = jnp.concatenate(
        [jnp.where(tile == j, 1.0, 0.0).astype(BF) for j in range(KINDS)], axis=0
    )
    before = dot(inside, ordered(128, True))
    counts = dot(inside, jnp.ones((128, 128), BF)).astype(BF)
    base = dot(ordered(32 * KINDS, False), counts)
    places = jnp.zeros((32, 128), F32)
    for j in range(TILES):
        rows = slice(32 * j, 32 * j + 32)
        places = places + jnp.where(tile == j, before[rows] + base[rows], 0.0)
    spot[...] = places.astype(jnp.int32)

    place = id_row(spot, 0, 32)
    sources = id_row(src, 0, 32)
    targets = id_row(tgt, 0, 32)
    live = id_row(mask, 0, 32)
    here = lax.broadcasted_iota(jnp.int32, (32, E), 0) == jnp.right_shift(place, 7)
    parts = (
        jnp.bitwise_and(sources, 255),
        jnp.bitwise_and(targets, 255),
        jnp.right_shift(sources, 8) * 16 + jnp.right_shift(targets, 8),
        live,
    )
    parts = [jnp.where(here, part.astype(F32), 0.0).astype(BF) for part in parts]
    moved = dnt(
        jnp.concatenate(parts, axis=0), one_hot(jnp.bitwise_and(place, 127), 0, 128)
    ).astype(jnp.int32)
    upper = moved[64:96]
    src[...] = moved[0:32] + 256 * jnp.right_shift(upper, 4)
    tgt[...] = moved[32:64] + 256 * jnp.bitwise_and(upper, 15)
    mask[...] = moved[96:128]

    lane = lax.broadcasted_iota(jnp.int32, (1, 128), 1)
    border = jnp.zeros((1, 128), F32)
    for j in range(1, TILES):
        border = jnp.where(lane == j, base[32 * j : 32 * j + 1], border)
    passed = jnp.minimum(jnp.right_shift(border.astype(jnp.int32), 8), RUNS - 1)
    rank = jnp.where((lane >= 1) & (lane < TILES), lane - 1 + passed, 1000)
    step = lax.broadcasted_iota(jnp.int32, (32, 128), 0)
    wide = lax.broadcasted_iota(jnp.int32, (32, 128), 1)
    table_tile = jnp.sum(jnp.where(rank < step, 1.0, 0.0), axis=1, keepdims=True).astype(
        jnp.int32
    )
    table_tile = jnp.broadcast_to(table_tile, (32, 128))
    edge_tile = step - table_tile
    plan[0:32, :] = jnp.where(wide == 0, edge_tile, table_tile)
    for row, which in ((32, edge_tile), (33, table_tile)):
        upto = jnp.where((which <= wide) & (step < STEPS), 1.0, 0.0)
        plan[row : row + 1, :] = jnp.sum(upto, axis=0, keepdims=True).astype(jnp.int32) - 1


def split(value):
    high = value.astype(BF)
    return high, (value - high.astype(F32)).astype(BF)


def kernel(
    nodes_h,
    brows_h,
    src_h,
    tgt_h,
    mask_h,
    segs_h,
    w1_h,
    b1_h,
    w2_h,
    cot_h,
    pooled_h,
    gnodes_h,
    gw_h,
    nodes,
    brows,
    src,
    tgt,
    mask,
    segs,
    w1,
    b1,
    w2,
    cot,
    pooled,
    gnodes,
    tt,
    tiles,
    spot,
    plan_v,
    plan,
    xs,
    gis,
    sums_s,
    run,
    w1t,
    bcol,
    bnd,
    hrecv,
    line,
    line_t,
    xt,
    mseg,
    hid,
    gp,
    gi,
    pwf,
    pws,
    cbuf,
    csum,
    rsb_a,
    rsb_b,
    rsbias,
    zb_a,
    zb_b,
    zbias,
    ag,
    psum,
    psend,
    precv,
    gslot,
    gret,
    acc,
    in_s,
    out_s,
    plan_s,
    h_s,
    h_r,
    c_s,
    c_r,
    p_s,
    p_r,
    g_s,
    g_r,
    core_s,
    core_r,
    rs_s,
    rs_r,
    rb_s,
    rb_r,
    z_s,
    z_r,
    zb_s,
    zb_r,
    ag_s,
    ag_r,
    agb_s,
    agb_r,
    fw_s,
    fw_r,
):
    me = lax.axis_index("gx")
    my = lax.axis_index("gy")
    core = lax.rem(my, 2)
    z = lax.div(my, 2)
    sib = my + 1 - 2 * core

    barrier = pltpu.get_barrier_semaphore()
    for d in range(1, GX):
        pl.semaphore_signal(
            barrier, inc=1, device_id={"gx": lax.rem(me + d, GX)}, device_id_type=MESH
        )
    for d in range(1, GY):
        pl.semaphore_signal(
            barrier, inc=1, device_id={"gy": lax.rem(my + d, GY)}, device_id_type=MESH
        )

    def remote(source, target, send, receive, device):
        return pltpu.make_async_remote_copy(
            src_ref=source,
            dst_ref=target,
            send_sem=send,
            recv_sem=receive,
            device_id=device,
            device_id_type=MESH,
        )

    pairs = (
        (src_h, src),
        (tgt_h, tgt),
        (mask_h, mask),
        (nodes_h, nodes),
        (brows_h, brows),
        (cot_h, cot),
        (segs_h, segs),
        (w1_h, w1),
        (b1_h, b1),
        (w2_h, w2),
    )
    loads = [pltpu.make_async_copy(a, b, in_s.at[i]) for i, (a, b) in enumerate(pairs)]
    for copy in loads:
        copy.start()

    for copy in loads[:3]:
        copy.wait()
    sort_edges(src, tgt, mask, spot, plan_v)
    to_plan = pltpu.make_async_copy(plan_v, plan, plan_s)
    to_plan.start()

    unit = eye(F)
    for copy in loads[3:6]:
        copy.wait()
    tt[...] = dnt(unit, nodes[...]).astype(BF)
    bnd[...] = dot(tt[...], one_hot(brows[...], 0, N)).astype(BF)
    line[pl.ds(me, 1)] = cot[...][None]

    pl.semaphore_wait(barrier, GX - 1 + GY - 1)

    there = (me > 0, me < GX - 1, my > 0, my < GY - 1)
    halo = (
        remote(bnd, hrecv.at[1], h_s.at[1], h_r.at[1], {"gx": lax.rem(me + GX - 1, GX)}),
        remote(bnd, hrecv.at[0], h_s.at[0], h_r.at[0], {"gx": lax.rem(me + 1, GX)}),
        remote(bnd, hrecv.at[3], h_s.at[3], h_r.at[3], {"gy": lax.rem(my + GY - 1, GY)}),
        remote(bnd, hrecv.at[2], h_s.at[2], h_r.at[2], {"gy": lax.rem(my + 1, GY)}),
    )
    for k in range(4):
        pl.when(there[k])(halo[k].start)
    cots = [
        remote(
            cot,
            line.at[me],
            c_s,
            c_r,
            {"gx": lax.rem(me + d, GX)},
        )
        for d in range(1, GX)
    ]
    for copy in cots:
        copy.start()
    for copy in loads[6:]:
        copy.wait()

    for j in range(N // T):
        tiles[j] = tt[:, j * T : (j + 1) * T]

    for i in range(2):
        for j in range(2):
            w1t[j * F : (j + 1) * F, i * F : (i + 1) * F] = dnt(
                unit, w1[i * F : (i + 1) * F, j * F : (j + 1) * F]
            ).astype(BF)
    bcol[...] = jnp.broadcast_to(
        jnp.transpose(jnp.broadcast_to(b1[...], (8, H)))[:, :1], (H, 128)
    )
    xt[2 * F :, :] = jnp.ones((16, E), BF)
    seg_ids = segs[...]
    seg_parts = jnp.concatenate(
        [
            jnp.bitwise_and(seg_ids, 255).astype(F32).astype(BF),
            jnp.right_shift(seg_ids, 8).astype(F32).astype(BF),
        ],
        axis=0,
    )

    def block(b, width=W):
        return pl.ds(pl.multiple_of(b * width, width), width)

    def gather(b, carry):
        targets = id_row(tgt, b * 8, 8)
        live = id_row(mask, b * 8, 8)
        low = one_hot(jnp.bitwise_and(targets, 127), 0, 128)
        found = dot(seg_parts, low)
        found = found[:16] + 256.0 * found[16:]
        high = lax.broadcasted_iota(jnp.int32, (16, W), 0) == jnp.right_shift(targets, 7)
        segment = jnp.sum(jnp.where(high, found, 0.0), axis=0, keepdims=True)
        segment = jnp.where(live > 0, segment, -1.0).astype(jnp.int32)
        mseg[:, block(b)] = jnp.broadcast_to(segment, (8, W))
        xt[F : 2 * F, block(b)] = dot(tt[...], one_hot(targets, 0, N)).astype(BF)
        return carry

    lax.fori_loop(0, E // W, gather, 0)

    for k, coming in enumerate((halo[1], halo[0], halo[3], halo[2])):
        pl.when(there[k])(coming.wait_recv)

        @pl.when(jnp.logical_not(there[k]))
        def _(k=k):
            hrecv[k] = jnp.zeros((F, NB), BF)

    for j in range(2):
        tiles[N // T + j] = jnp.concatenate([hrecv[2 * j], hrecv[2 * j + 1]], axis=1)
    others = line.at[pl.ds(1, GX - 1)]
    all_cots = remote(others, others, c_s, c_r, {"gx": me})
    all_cots.wait_recv()
    lines = jnp.concatenate([line[g] for g in range(GX)], axis=0)
    line_t[...] = dnt(unit, lines).astype(BF)

    to_plan.wait()

    def planned(row, column, count):
        return jnp.clip(plan[row, column], 0, count - 1)

    def meeting(p):
        run_of, tile_of = planned(p, 0, RUNS), planned(p, 1, TILES)
        earlier = jnp.maximum(p - 1, 0)
        hot = one_hot(id_row(src, run_of * (T // 128), T // 128), tile_of * T, T)
        return run_of, tile_of, earlier, hot

    def source_rows(g, carry):
        total = run[...]
        for k in range(5):
            p = g * 5 + k
            run_of, tile_of, earlier, hot = meeting(p)
            same = planned(earlier, 0, RUNS) == run_of
            total = jnp.where(same, total, 0.0) + dot(tiles[tile_of], hot)
            xs[p] = total.astype(BF)
        run[...] = total
        return carry

    run[...] = jnp.zeros_like(run)
    lax.fori_loop(0, STEPS // 5, source_rows, 0)

    def edges(b, carry):
        for k in range(W // T):
            xt[:F, block(b * (W // T) + k, T)] = xs[planned(32, b * (W // T) + k, STEPS)]
        chosen = one_hot(mseg[:1, block(b)], 0, SEG)
        gm = dot(line_t[...], chosen).astype(BF)
        bias = jnp.concatenate([bcol[...]] * (W // 128), axis=1)
        x = dot(w1t[...], xt[: 2 * F, block(b)]) + bias
        gh = dot(w2[...], gm)
        square = x * x
        t = 0.5 * jnp.tanh(x * (0.7978845608028654 + 0.035677408136300125 * square))
        half = 0.5 + t
        h = x * half
        hid[:, block(b)] = h.astype(BF)
        slope = half + (h * (0.5 - t)) * (1.5957691216057308 + 0.21406444881780074 * square)
        gp[:, block(b)] = (gh * slope).astype(BF)
        return carry

    lax.fori_loop(0, E // W, edges, 0)

    firsts, counts = (0, 528), (528, 256)
    shares = (32, 16)
    arrived = (rsb_a, rsb_b)
    by_z = (zb_a, zb_b)

    def rows_of(part, member):
        return pl.ds(pl.multiple_of(firsts[part] + member * shares[part], 16), shares[part])

    def whole(part):
        return pl.ds(firsts[part], counts[part])

    peers = [lax.rem(me + d, GX) for d in range(GX)]
    pair, scatter, over_z, gathers, forwards = [], [], [], [], []
    all_scatter, all_z, all_gathers = [], [], []
    for part in range(2):
        pair.append(
            remote(
                pws.at[1 - core, whole(part)],
                cbuf.at[whole(part)],
                core_s.at[part],
                core_r.at[part],
                {"gy": sib},
            )
        )
        scatter.append(
            [
                remote(
                    csum.at[rows_of(part, peers[d])],
                    arrived[part].at[d],
                    rs_s.at[part],
                    rs_r.at[part],
                    {"gx": peers[d]},
                )
                for d in range(1, GX)
            ]
        )
        over_z.append(
            [
                remote(
                    by_z[part].at[z],
                    by_z[part].at[z],
                    z_s.at[part],
                    z_r.at[part],
                    {"gy": lax.rem(my + 2 * d, GY)},
                )
                for d in range(1, 4)
            ]
        )
        place = ag.at[core, rows_of(part, me)]
        gathers.append(
            [
                remote(place, place, ag_s.at[part], ag_r.at[part], {"gx": peers[d]})
                for d in range(1, GX)
            ]
        )
        place = ag.at[core, whole(part)]
        forwards.append(remote(place, place, fw_s.at[part], fw_r.at[part], {"gy": sib}))
        others = arrived[part].at[pl.ds(1, GX - 1)]
        all_scatter.append(remote(others, others, rs_s.at[part], rs_r.at[part], {"gx": me}))
        others = by_z[part].at[pl.ds(0, 3)]
        all_z.append(remote(others, others, z_s.at[part], z_r.at[part], {"gy": my}))
        others = ag.at[core, pl.ds(firsts[part], (GX - 1) * shares[part])]
        all_gathers.append(remote(others, others, ag_s.at[part], ag_r.at[part], {"gx": me}))
    bias_rows = csum.at[pl.ds(512, 16)]
    bias_scatter = [
        remote(bias_rows, rsbias.at[d], rb_s, rb_r, {"gx": peers[d]})
        for d in range(1, GX)
    ]
    bias_z = [
        remote(zbias.at[z], zbias.at[z], zb_s, zb_r, {"gy": lax.rem(my + 2 * d, GY)})
        for d in range(1, 4)
    ]
    bias_place = ag.at[core, pl.ds(512, 16)]
    bias_gathers = [
        remote(bias_place, bias_place, agb_s, agb_r, {"gx": peers[d]})
        for d in range(1, GX)
    ]
    others = rsbias.at[pl.ds(1, GX - 1)]
    all_bias_scatter = remote(others, others, rb_s, rb_r, {"gx": me})
    others = zbias.at[pl.ds(0, 3)]
    all_bias_z = remote(others, others, zb_s, zb_r, {"gy": my})
    others = ag.at[core, pl.ds(0, (GX - 1) * 16)]
    all_bias_gathers = remote(others, others, agb_s, agb_r, {"gx": me})

    def to_pair(part):
        pws[:, whole(part), :] = pwf[:, whole(part), :].astype(BF)
        pair[part].start()

    def to_members(part):
        pair[part].wait_recv()
        csum[whole(part), :] = (
            pwf[core, whole(part), :] + cbuf[whole(part), :].astype(F32)
        ).astype(BF)
        for copy in scatter[part]:
            copy.start()
        if part == 0:
            for d in range(1, GX):
                pl.when(me + d == GX)(bias_scatter[d - 1].start)

    def to_z(part):
        all_scatter[part].wait_recv()
        total = csum[rows_of(part, me), :].astype(F32)
        for d in range(1, GX):
            total = total + arrived[part][d].astype(F32)
        by_z[part][pl.ds(z, 1)] = total[None]
        for copy in over_z[part]:
            copy.start()
        if part == 0:

            @pl.when(me == 0)
            def _():
                all_bias_scatter.wait_recv()
                sums = csum[512:528, :].astype(F32)
                for d in range(1, GX):
                    sums = sums + rsbias[d].astype(F32)
                zbias[pl.ds(z, 1)] = sums[None]
                for copy in bias_z:
                    copy.start()

    def to_all(part):
        all_z[part].wait_recv()
        sums = by_z[part]
        total = (sums[0] + sums[1]) + (sums[2] + sums[3])
        ag[pl.ds(core, 1), rows_of(part, me), :] = total.astype(BF)[None]
        for copy in gathers[part]:
            copy.start()
        if part == 0:

            @pl.when(me == 0)
            def _():
                all_bias_z.wait_recv()
                sums = (zbias[0] + zbias[1]) + (zbias[2] + zbias[3])
                ag[pl.ds(core, 1), 512:528, :] = sums.astype(BF)[None]
                for copy in bias_gathers:
                    copy.start()

    def to_other_core(part):
        all_gathers[part].wait_recv()
        if part == 0:
            pl.when(me > 0)(bias_gathers[0].wait_recv)
        forwards[part].start()

    grads = dnt(xt[...], gp[...])
    for c in range(2):
        pwf[c, 0:528, :] = grads[:, c * HW : (c + 1) * HW]
    to_pair(0)

    w2v = w2[...]

    def segment_sums(b, carry):
        first = b * 256
        edge_hot = one_hot(mseg[:1, :], first, 256)
        high, low = split(dnt(edge_hot, hid[...]))
        node_hot = one_hot(id_row(segs, 0, N // 128), first, 256)
        part = dot(high, w2v) + dot(low, w2v) + dot(node_hot, nodes[...])
        for i in range(8):
            psum[b * 8 + i] = part[i * SR : (i + 1) * SR]
            psend[b * 8 + i] = part[i * SR : (i + 1) * SR].astype(BF)
        lines_t = line_t[:, block(b, 256)]
        add = dot(lines_t, high) + dot(lines_t, low)
        for c in range(2):
            pwf[c, 528:784, :] = pwf[c, 528:784, :] + add[:, c * HW : (c + 1) * HW]
        pl.when(b == 0)(functools.partial(to_members, 0))
        return carry

    pwf[:, 528:784, :] = jnp.zeros((2, 256, HW), F32)
    lax.fori_loop(0, SEG // 256, segment_sums, 0)
    to_pair(1)
    pools = [
        remote(
            psend.at[peers[d]],
            precv.at[d],
            p_s,
            p_r,
            {"gx": peers[d]},
        )
        for d in range(1, GX)
    ]
    def input_grads(b, carry):
        grads = dot(w1[...], gp[:, block(b)]).astype(BF)
        gi[:, block(b)] = grads[F:]
        for k in range(W // T):
            gis[b * (W // T) + k] = grads[:F, k * T : (k + 1) * T]
        return carry

    lax.fori_loop(0, E // W, input_grads, 0)
    to_members(1)
    to_z(0)
    for copy in pools:
        copy.start()

    def source_sums(g, carry):
        total = run[...]
        for k in range(5):
            p = g * 5 + k
            run_of, tile_of, earlier, hot = meeting(p)
            same = planned(earlier, 1, TILES) == tile_of
            total = jnp.where(same, total, 0.0) + dnt(hot, gis[run_of])
            sums_s[p] = total
        run[...] = total
        return carry

    run[...] = jnp.zeros_like(run)
    lax.fori_loop(0, STEPS // 5, source_sums, 0)

    for j in range(2):
        slots = sums_s[planned(33, N // T + j, STEPS)].astype(BF)
        gslot[2 * j] = slots[:NB]
        gslot[2 * j + 1] = slots[NB:]
    back = (
        remote(gslot.at[0], gret.at[0], g_s.at[0], g_r.at[0], {"gx": lax.rem(me + GX - 1, GX)}),
        remote(gslot.at[1], gret.at[1], g_s.at[1], g_r.at[1], {"gx": lax.rem(me + 1, GX)}),
        remote(gslot.at[2], gret.at[2], g_s.at[2], g_r.at[2], {"gy": lax.rem(my + GY - 1, GY)}),
        remote(gslot.at[3], gret.at[3], g_s.at[3], g_r.at[3], {"gy": lax.rem(my + 1, GY)}),
    )
    for k in range(4):
        pl.when(there[k])(back[k].start)

    def own(b, carry):
        first = b * 512
        s = jnp.concatenate(
            [sums_s[planned(33, b * 2 + k, STEPS)] for k in range(2)], axis=0
        )
        t = dnt(one_hot(id_row(tgt, 0, 32), first, 512), gi[...])
        acc[block(b, 512), :] = s + t

        @pl.when(b == 0)
        def _():
            to_z(1)
            to_all(0)

        pl.when(b == 1)(functools.partial(to_all, 1))
        return carry

    lax.fori_loop(0, N // 512, own, 0)

    ret = jnp.zeros((NB, F), F32)
    for k, here in enumerate((there[1], there[0], there[3], there[2])):
        pl.when(here)(back[k].wait_recv)

        @pl.when(jnp.logical_not(here))
        def _(k=k):
            gret[k] = jnp.zeros((NB, F), BF)

        ret = ret + gret[k].astype(F32)
    ret_parts = jnp.concatenate(split(ret), axis=0)
    lines = jnp.concatenate([line[g] for g in range(GX)], axis=0)
    seg_cols = jnp.transpose(segs[...].astype(F32)).astype(jnp.int32)
    stores = []
    for r in range(N // 128):
        rows = slice(r * 128, (r + 1) * 128)
        seg_hot = jnp.where(
            lax.broadcasted_iota(jnp.int32, (128, SEG), 1) == seg_cols[:, r : r + 1], 1.0, 0.0
        ).astype(BF)
        place_hot = one_hot(brows[...], r * 128, 128)
        place_hot = jnp.concatenate([place_hot, place_hot], axis=1)
        gnodes[rows, :] = (acc[rows, :] + dot(seg_hot, lines) + dot(place_hot, ret_parts)).astype(
            BF
        )
        if r % 4 == 3:
            done = pl.ds((r - 3) * 128, 512)
            stores.append(
                pltpu.make_async_copy(gnodes.at[done], gnodes_h.at[done], out_s.at[r // 4])
            )
            stores[-1].start()

    to_other_core(0)

    others = precv.at[pl.ds(1, GX - 1)]
    all_pools = remote(others, others, p_s, p_r, {"gx": me})
    all_pools.wait_recv()
    sums = psum[me]
    for d in range(1, GX):
        sums = sums + precv[d].astype(F32)
    pooled[...] = sums.astype(BF)
    stores.append(pltpu.make_async_copy(pooled, pooled_h, out_s.at[4]))
    stores[-1].start()

    to_other_core(1)
    for copy in forwards:
        copy.wait_recv()
    stores.append(pltpu.make_async_copy(ag, gw_h, out_s.at[5]))
    stores[-1].start()

    for k in range(4):
        pl.when(there[k])(halo[k].wait_send)
        pl.when(there[k])(back[k].wait_send)
    for group in ([all_cots, all_pools], pair, all_scatter, all_z, all_gathers, forwards):
        for copy in group:
            copy.wait_send()
    pl.when(me > 0)(bias_scatter[0].wait_send)

    @pl.when(me == 0)
    def _():
        all_bias_z.wait_send()
        all_bias_gathers.wait_send()

    for copy in stores:
        copy.wait()


def finish(
    scale,
    pooled,
    gnodes,
    gw,
    pooled_o,
    gnodes_o,
    first_o,
    bias_o,
    second_o,
    pooled_v,
    gnodes_v,
    gw_v,
    first_v,
    bias_v,
    second_v,
    sems,
):
    def move(source, target, number):
        copy = pltpu.make_async_copy(source, target, sems.at[number])
        copy.start()
        return copy

    coming = [move(gw.at[c], gw_v.at[c], c) for c in range(2)]
    parts = [pl.ds(i * (N // 2), N // 2) for i in range(2)]
    rows = [move(gnodes.at[part], gnodes_v.at[part], 2 + i) for i, part in enumerate(parts)]
    small = move(pooled, pooled_v, 4)
    unit = eye(HW)
    going = []
    for c in range(2):
        half = slice(c * HW, (c + 1) * HW)
        coming[c].wait()
        first_v[:, half] = gw_v[c, 0:512, :].astype(F32) * scale
        bias_v[:, half] = gw_v[c, 512:528, :].astype(F32)[:1] * scale
        second_v[half, :] = dnt(unit, gw_v[c, 528:784, :]) * scale
        place = pl.ds(c * HW, HW)
        going.append(move(second_v.at[place], second_o.at[place], 5 + c))
    going.append(move(first_v, first_o, 7))
    going.append(move(bias_v, bias_o, 8))
    for i, part in enumerate(parts):
        rows[i].wait()
        going.append(move(gnodes_v.at[part], gnodes_o.at[part], 9 + i))
    small.wait()
    going.append(move(pooled_v, pooled_o, 11))
    for copy in going:
        copy.wait()


def local(nodes, brows, src, tgt, mask, segs, w1, b1, w2, cot):
    dma = pltpu.SemaphoreType.DMA
    int32 = jnp.int32
    arguments = (
        nodes,
        brows.reshape(1, NB),
        src,
        tgt,
        mask,
        segs.reshape(N // 128, 128),
        w1,
        b1.reshape(1, H),
        w2,
        cot,
    )
    scratch = [pltpu.VMEM(a.shape, a.dtype) for a in arguments]
    scratch += [
        pltpu.VMEM((SR, F), BF),
        pltpu.VMEM((N, F), BF),
        pltpu.VMEM((F, N), BF),
        pltpu.VMEM((TILES, F, T), BF),
        pltpu.VMEM((32, 128), int32),
        pltpu.VMEM((40, 128), int32),
        pltpu.SMEM((40, 128), int32),
        pltpu.VMEM((STEPS, F, T), BF),
        pltpu.VMEM((RUNS, F, T), BF),
        pltpu.VMEM((STEPS, T, F), F32),
        pltpu.VMEM((T, F), F32),
        pltpu.VMEM((H, 2 * F), BF),
        pltpu.VMEM((H, 128), F32),
        pltpu.VMEM((F, NB), BF),
        pltpu.VMEM((4, F, NB), BF),
        pltpu.VMEM((GX, SR, F), BF),
        pltpu.VMEM((F, SEG), BF),
        pltpu.VMEM((2 * F + 16, E), BF),
        pltpu.VMEM((8, E), int32),
        pltpu.VMEM((H, E), BF),
        pltpu.VMEM((H, E), BF),
        pltpu.VMEM((F, E), BF),
        pltpu.VMEM((2, PW, HW), F32),
        pltpu.VMEM((2, PW, HW), BF),
        pltpu.VMEM((PW, HW), BF),
        pltpu.VMEM((PW, HW), BF),
        pltpu.VMEM((GX, 32, HW), BF),
        pltpu.VMEM((GX, 16, HW), BF),
        pltpu.VMEM((GX, 16, HW), BF),
        pltpu.VMEM((4, 32, HW), F32),
        pltpu.VMEM((4, 16, HW), F32),
        pltpu.VMEM((4, 16, HW), F32),
        pltpu.VMEM((2, PW, HW), BF),
        pltpu.VMEM((GX, SR, F), F32),
        pltpu.VMEM((GX, SR, F), BF),
        pltpu.VMEM((GX, SR, F), BF),
        pltpu.VMEM((4, NB, F), BF),
        pltpu.VMEM((4, NB, F), BF),
        pltpu.VMEM((N, F), F32),
        dma((10,)),
        dma((6,)),
        dma,
    ]
    scratch += [
        dma((4,)),
        dma((4,)),
        dma,
        dma,
        dma,
        dma,
        dma((4,)),
        dma((4,)),
        dma((2,)),
        dma((2,)),
        dma((2,)),
        dma((2,)),
        dma,
        dma,
        dma((2,)),
        dma((2,)),
        dma,
        dma,
        dma((2,)),
        dma((2,)),
        dma,
        dma,
        dma((2,)),
        dma((2,)),
    ]
    anywhere = pl.BlockSpec(memory_space=pl.ANY)
    outs = (
        jax.ShapeDtypeStruct((SR, F), BF),
        jax.ShapeDtypeStruct((N, F), BF),
    )
    pooled, gnodes, gw = pl.pallas_call(
        kernel,
        out_shape=(*outs, jax.ShapeDtypeStruct((2, PW, HW), BF)),
        in_specs=[anywhere] * 10,
        out_specs=(anywhere,) * 3,
        scratch_shapes=scratch,
        compiler_params=pltpu.CompilerParams(
            collective_id=0, has_side_effects=True, vmem_limit_bytes=60 * 2**20
        ),
    )(*arguments)
    pooled, gnodes, first, bias, second = pl.pallas_call(
        functools.partial(finish, float((E * GX * GY) ** -0.5)),
        out_shape=(
            *outs,
            jax.ShapeDtypeStruct((H, H), F32),
            jax.ShapeDtypeStruct((1, H), F32),
            jax.ShapeDtypeStruct((H, F), F32),
        ),
        in_specs=[anywhere] * 3,
        out_specs=(anywhere,) * 5,
        scratch_shapes=[
            pltpu.VMEM((SR, F), BF),
            pltpu.VMEM((N, F), BF),
            pltpu.VMEM((2, PW, HW), BF),
            pltpu.VMEM((H, H), F32),
            pltpu.VMEM((1, H), F32),
            pltpu.VMEM((H, F), F32),
            dma((12,)),
        ],
        compiler_params=pltpu.CompilerParams(vmem_limit_bytes=60 * 2**20),
    )(pooled, gnodes, gw)
    return pooled, gnodes, first, bias.reshape(H), second


def solution(mesh):
    in_specs = (
        P(("gx", "gy"), None),
        P(("gx", "gy")),
        P(("gx", "gy"), None),
        P(("gx", "gy"), None),
        P(("gx", "gy"), None),
        P(("gx", "gy")),
        P(),
        P(),
        P(),
        P(("gx", "gy"), None),
    )
    out_specs = (P(("gx", "gy"), None), P(("gx", "gy"), None), P(), P(), P())
    return jax.shard_map(local, mesh=mesh, in_specs=in_specs, out_specs=out_specs, check_vma=False)
```

```python
import functools

import jax
import jax.numpy as jnp
from jax import lax
from jax.experimental import pallas as pl
from jax.experimental.pallas import tpu as pltpu
from jax.sharding import PartitionSpec as P

MESH = pl.DeviceIdType.MESH
BF = jnp.bfloat16
F32 = jnp.float32
N = 2048
NB = 128
HALO = 4 * NB
F = 256
H = 512
E = 4096
SEG = 512
SR = 32
GX = 16
GY = 8
W = 2048
T = 256
TILES = (N + HALO) // T
RUNS = E // T
STEPS = TILES + RUNS - 1
KINDS = 12
PW = 784
HW = H // 2
NT = (((1,), (1,)), ((), ()))


def dot(a, b):
    return jnp.dot(a, b, preferred_element_type=F32)


def dnt(a, b):
    return lax.dot_general(a, b, NT, preferred_element_type=F32)


def one_hot(row, first, count):
    rows = lax.broadcasted_iota(jnp.int32, (count, row.shape[1]), 0)
    return jnp.where(rows == row - first, 1.0, 0.0).astype(BF)


def id_row(ref, first, count):
    return jnp.concatenate([ref[pl.ds(first + i, 1), :] for i in range(count)], axis=1)


def eye(size):
    a = lax.broadcasted_iota(jnp.int32, (size, size), 0)
    b = lax.broadcasted_iota(jnp.int32, (size, size), 1)
    return jnp.where(a == b, 1.0, 0.0).astype(BF)


def ordered(size, earlier_row):
    a = lax.broadcasted_iota(jnp.int32, (size, size), 0)
    b = lax.broadcasted_iota(jnp.int32, (size, size), 1)
    return jnp.where(a < b if earlier_row else b < a, 1.0, 0.0).astype(BF)


def sort_edges(src, tgt, mask, spot, plan):
    tile = jnp.right_shift(src[...], 8)
    inside = jnp.concatenate(
        [jnp.where(tile == j, 1.0, 0.0).astype(BF) for j in range(KINDS)], axis=0
    )
    before = dot(inside, ordered(128, True))
    counts = dot(inside, jnp.ones((128, 128), BF)).astype(BF)
    base = dot(ordered(32 * KINDS, False), counts)
    places = jnp.zeros((32, 128), F32)
    for j in range(TILES):
        rows = slice(32 * j, 32 * j + 32)
        places = places + jnp.where(tile == j, before[rows] + base[rows], 0.0)
    spot[...] = places.astype(jnp.int32)

    place = id_row(spot, 0, 32)
    sources = id_row(src, 0, 32)
    targets = id_row(tgt, 0, 32)
    live = id_row(mask, 0, 32)
    here = lax.broadcasted_iota(jnp.int32, (32, E), 0) == jnp.right_shift(place, 7)
    parts = (
        jnp.bitwise_and(sources, 255),
        jnp.bitwise_and(targets, 255),
        jnp.right_shift(sources, 8) * 16 + jnp.right_shift(targets, 8),
        live,
    )
    parts = [jnp.where(here, part.astype(F32), 0.0).astype(BF) for part in parts]
    moved = dnt(
        jnp.concatenate(parts, axis=0), one_hot(jnp.bitwise_and(place, 127), 0, 128)
    ).astype(jnp.int32)
    upper = moved[64:96]
    src[...] = moved[0:32] + 256 * jnp.right_shift(upper, 4)
    tgt[...] = moved[32:64] + 256 * jnp.bitwise_and(upper, 15)
    mask[...] = moved[96:128]

    lane = lax.broadcasted_iota(jnp.int32, (1, 128), 1)
    border = jnp.zeros((1, 128), F32)
    for j in range(1, TILES):
        border = jnp.where(lane == j, base[32 * j : 32 * j + 1], border)
    passed = jnp.minimum(jnp.right_shift(border.astype(jnp.int32), 8), RUNS - 1)
    rank = jnp.where((lane >= 1) & (lane < TILES), lane - 1 + passed, 1000)
    step = lax.broadcasted_iota(jnp.int32, (32, 128), 0)
    wide = lax.broadcasted_iota(jnp.int32, (32, 128), 1)
    table_tile = jnp.sum(jnp.where(rank < step, 1.0, 0.0), axis=1, keepdims=True).astype(
        jnp.int32
    )
    table_tile = jnp.broadcast_to(table_tile, (32, 128))
    edge_tile = step - table_tile
    plan[0:32, :] = jnp.where(wide == 0, edge_tile, table_tile)
    for row, which in ((32, edge_tile), (33, table_tile)):
        upto = jnp.where((which <= wide) & (step < STEPS), 1.0, 0.0)
        plan[row : row + 1, :] = jnp.sum(upto, axis=0, keepdims=True).astype(jnp.int32) - 1


def split(value):
    high = value.astype(BF)
    return high, (value - high.astype(F32)).astype(BF)


def kernel(
    nodes_h,
    brows_h,
    src_h,
    tgt_h,
    mask_h,
    segs_h,
    w1_h,
    b1_h,
    w2_h,
    cot_h,
    pooled_h,
    gnodes_h,
    gw_h,
    nodes,
    brows,
    src,
    tgt,
    mask,
    segs,
    w1,
    b1,
    w2,
    cot,
    pooled,
    gnodes,
    tt,
    tiles,
    spot,
    plan_v,
    plan,
    xs,
    gis,
    sums_s,
    run,
    w1t,
    bcol,
    bnd,
    hrecv,
    line,
    line_t,
    xt,
    mseg,
    hid,
    gp,
    gi,
    pwf,
    pws,
    cbuf,
    csum,
    rsb_a,
    rsb_b,
    rsbias,
    zb_a,
    zb_b,
    zbias,
    ag,
    psum,
    psend,
    precv,
    gslot,
    gret,
    acc,
    in_s,
    out_s,
    plan_s,
    h_s,
    h_r,
    c_s,
    c_r,
    p_s,
    p_r,
    g_s,
    g_r,
    core_s,
    core_r,
    rs_s,
    rs_r,
    rb_s,
    rb_r,
    z_s,
    z_r,
    zb_s,
    zb_r,
    ag_s,
    ag_r,
    agb_s,
    agb_r,
    fw_s,
    fw_r,
):
    me = lax.axis_index("gx")
    my = lax.axis_index("gy")
    core = lax.rem(my, 2)
    z = lax.div(my, 2)
    sib = my + 1 - 2 * core

    barrier = pltpu.get_barrier_semaphore()
    for d in range(1, GX):
        pl.semaphore_signal(
            barrier, inc=1, device_id={"gx": lax.rem(me + d, GX)}, device_id_type=MESH
        )
    for d in range(1, GY):
        pl.semaphore_signal(
            barrier, inc=1, device_id={"gy": lax.rem(my + d, GY)}, device_id_type=MESH
        )

    def remote(source, target, send, receive, device):
        return pltpu.make_async_remote_copy(
            src_ref=source,
            dst_ref=target,
            send_sem=send,
            recv_sem=receive,
            device_id=device,
            device_id_type=MESH,
        )

    pairs = (
        (src_h, src),
        (tgt_h, tgt),
        (mask_h, mask),
        (nodes_h, nodes),
        (brows_h, brows),
        (cot_h, cot),
        (segs_h, segs),
        (w1_h, w1),
        (b1_h, b1),
        (w2_h, w2),
    )
    loads = [pltpu.make_async_copy(a, b, in_s.at[i]) for i, (a, b) in enumerate(pairs)]
    for copy in loads:
        copy.start()

    for copy in loads[:3]:
        copy.wait()
    sort_edges(src, tgt, mask, spot, plan_v)
    to_plan = pltpu.make_async_copy(plan_v, plan, plan_s)
    to_plan.start()

    unit = eye(F)
    for copy in loads[3:6]:
        copy.wait()
    tt[...] = dnt(unit, nodes[...]).astype(BF)
    bnd[...] = dot(tt[...], one_hot(brows[...], 0, N)).astype(BF)
    line[pl.ds(me, 1)] = cot[...][None]

    pl.semaphore_wait(barrier, GX - 1 + GY - 1)

    there = (me > 0, me < GX - 1, my > 0, my < GY - 1)
    halo = (
        remote(bnd, hrecv.at[1], h_s.at[1], h_r.at[1], {"gx": lax.rem(me + GX - 1, GX)}),
        remote(bnd, hrecv.at[0], h_s.at[0], h_r.at[0], {"gx": lax.rem(me + 1, GX)}),
        remote(bnd, hrecv.at[3], h_s.at[3], h_r.at[3], {"gy": lax.rem(my + GY - 1, GY)}),
        remote(bnd, hrecv.at[2], h_s.at[2], h_r.at[2], {"gy": lax.rem(my + 1, GY)}),
    )
    for k in range(4):
        pl.when(there[k])(halo[k].start)
    cots = [
        remote(
            cot,
            line.at[me],
            c_s,
            c_r,
            {"gx": lax.rem(me + d, GX)},
        )
        for d in range(1, GX)
    ]
    for copy in cots:
        copy.start()
    for copy in loads[6:]:
        copy.wait()

    for j in range(N // T):
        tiles[j] = tt[:, j * T : (j + 1) * T]

    for i in range(2):
        for j in range(2):
            w1t[j * F : (j + 1) * F, i * F : (i + 1) * F] = dnt(
                unit, w1[i * F : (i + 1) * F, j * F : (j + 1) * F]
            ).astype(BF)
    bcol[...] = jnp.broadcast_to(
        jnp.transpose(jnp.broadcast_to(b1[...], (8, H)))[:, :1], (H, 128)
    )
    xt[2 * F :, :] = jnp.ones((16, E), BF)
    seg_ids = segs[...]
    seg_parts = jnp.concatenate(
        [
            jnp.bitwise_and(seg_ids, 255).astype(F32).astype(BF),
            jnp.right_shift(seg_ids, 8).astype(F32).astype(BF),
        ],
        axis=0,
    )

    def block(b, width=W):
        return pl.ds(pl.multiple_of(b * width, width), width)

    def gather(b, carry):
        targets = id_row(tgt, b * 16, 16)
        live = id_row(mask, b * 16, 16)
        low = one_hot(jnp.bitwise_and(targets, 127), 0, 128)
        found = dot(seg_parts, low)
        found = found[:16] + 256.0 * found[16:]
        high = lax.broadcasted_iota(jnp.int32, (16, W), 0) == jnp.right_shift(targets, 7)
        segment = jnp.sum(jnp.where(high, found, 0.0), axis=0, keepdims=True)
        segment = jnp.where(live > 0, segment, -1.0).astype(jnp.int32)
        mseg[:, block(b)] = jnp.broadcast_to(segment, (8, W))
        xt[F : 2 * F, block(b)] = dot(tt[...], one_hot(targets, 0, N)).astype(BF)
        return carry

    lax.fori_loop(0, E // W, gather, 0)

    for k, coming in enumerate((halo[1], halo[0], halo[3], halo[2])):
        pl.when(there[k])(coming.wait_recv)

        @pl.when(jnp.logical_not(there[k]))
        def _(k=k):
            hrecv[k] = jnp.zeros((F, NB), BF)

    for j in range(2):
        tiles[N // T + j] = jnp.concatenate([hrecv[2 * j], hrecv[2 * j + 1]], axis=1)
    others = line.at[pl.ds(1, GX - 1)]
    all_cots = remote(others, others, c_s, c_r, {"gx": me})
    all_cots.wait_recv()
    lines = jnp.concatenate([line[g] for g in range(GX)], axis=0)
    line_t[...] = dnt(unit, lines).astype(BF)

    to_plan.wait()

    def planned(row, column, count):
        return jnp.clip(plan[row, column], 0, count - 1)

    def meeting(p):
        run_of, tile_of = planned(p, 0, RUNS), planned(p, 1, TILES)
        earlier = jnp.maximum(p - 1, 0)
        hot = one_hot(id_row(src, run_of * (T // 128), T // 128), tile_of * T, T)
        return run_of, tile_of, earlier, hot

    def source_rows(g, carry):
        total = run[...]
        for k in range(5):
            p = g * 5 + k
            run_of, tile_of, earlier, hot = meeting(p)
            same = planned(earlier, 0, RUNS) == run_of
            total = jnp.where(same, total, 0.0) + dot(tiles[tile_of], hot)
            xs[p] = total.astype(BF)
        run[...] = total
        return carry

    run[...] = jnp.zeros_like(run)
    lax.fori_loop(0, STEPS // 5, source_rows, 0)

    def edges(b, carry):
        for k in range(W // T):
            xt[:F, block(b * (W // T) + k, T)] = xs[planned(32, b * (W // T) + k, STEPS)]
        chosen = one_hot(mseg[:1, block(b)], 0, SEG)
        gm = dot(line_t[...], chosen).astype(BF)
        bias = jnp.concatenate([bcol[...]] * (W // 128), axis=1)
        x = dot(w1t[...], xt[: 2 * F, block(b)]) + bias
        gh = dot(w2[...], gm)
        square = x * x
        t = 0.5 * jnp.tanh(x * (0.7978845608028654 + 0.035677408136300125 * square))
        half = 0.5 + t
        h = x * half
        hid[:, block(b)] = h.astype(BF)
        slope = half + (h * (0.5 - t)) * (1.5957691216057308 + 0.21406444881780074 * square)
        gp[:, block(b)] = (gh * slope).astype(BF)
        return carry

    lax.fori_loop(0, E // W, edges, 0)

    firsts, counts = (0, 528), (528, 256)
    shares = (32, 16)
    arrived = (rsb_a, rsb_b)
    by_z = (zb_a, zb_b)

    def rows_of(part, member):
        return pl.ds(pl.multiple_of(firsts[part] + member * shares[part], 16), shares[part])

    def whole(part):
        return pl.ds(firsts[part], counts[part])

    peers = [lax.rem(me + d, GX) for d in range(GX)]
    pair, scatter, over_z, gathers, forwards = [], [], [], [], []
    all_scatter, all_z, all_gathers = [], [], []
    for part in range(2):
        pair.append(
            remote(
                pws.at[1 - core, whole(part)],
                cbuf.at[whole(part)],
                core_s.at[part],
                core_r.at[part],
                {"gy": sib},
            )
        )
        scatter.append(
            [
                remote(
                    csum.at[rows_of(part, peers[d])],
                    arrived[part].at[d],
                    rs_s.at[part],
                    rs_r.at[part],
                    {"gx": peers[d]},
                )
                for d in range(1, GX)
            ]
        )
        over_z.append(
            [
                remote(
                    by_z[part].at[z],
                    by_z[part].at[z],
                    z_s.at[part],
                    z_r.at[part],
                    {"gy": lax.rem(my + 2 * d, GY)},
                )
                for d in range(1, 4)
            ]
        )
        place = ag.at[core, rows_of(part, me)]
        gathers.append(
            [
                remote(place, place, ag_s.at[part], ag_r.at[part], {"gx": peers[d]})
                for d in range(1, GX)
            ]
        )
        place = ag.at[core, whole(part)]
        forwards.append(remote(place, place, fw_s.at[part], fw_r.at[part], {"gy": sib}))
        others = arrived[part].at[pl.ds(1, GX - 1)]
        all_scatter.append(remote(others, others, rs_s.at[part], rs_r.at[part], {"gx": me}))
        others = by_z[part].at[pl.ds(0, 3)]
        all_z.append(remote(others, others, z_s.at[part], z_r.at[part], {"gy": my}))
        others = ag.at[core, pl.ds(firsts[part], (GX - 1) * shares[part])]
        all_gathers.append(remote(others, others, ag_s.at[part], ag_r.at[part], {"gx": me}))
    bias_rows = csum.at[pl.ds(512, 16)]
    bias_scatter = [
        remote(bias_rows, rsbias.at[d], rb_s, rb_r, {"gx": peers[d]})
        for d in range(1, GX)
    ]
    bias_z = [
        remote(zbias.at[z], zbias.at[z], zb_s, zb_r, {"gy": lax.rem(my + 2 * d, GY)})
        for d in range(1, 4)
    ]
    bias_place = ag.at[core, pl.ds(512, 16)]
    bias_gathers = [
        remote(bias_place, bias_place, agb_s, agb_r, {"gx": peers[d]})
        for d in range(1, GX)
    ]
    others = rsbias.at[pl.ds(1, GX - 1)]
    all_bias_scatter = remote(others, others, rb_s, rb_r, {"gx": me})
    others = zbias.at[pl.ds(0, 3)]
    all_bias_z = remote(others, others, zb_s, zb_r, {"gy": my})
    others = ag.at[core, pl.ds(0, (GX - 1) * 16)]
    all_bias_gathers = remote(others, others, agb_s, agb_r, {"gx": me})

    def to_pair(part):
        pws[:, whole(part), :] = pwf[:, whole(part), :].astype(BF)
        pair[part].start()

    def to_members(part):
        pair[part].wait_recv()
        csum[whole(part), :] = (
            pwf[core, whole(part), :] + cbuf[whole(part), :].astype(F32)
        ).astype(BF)
        for copy in scatter[part]:
            copy.start()
        if part == 0:
            for d in range(1, GX):
                pl.when(me + d == GX)(bias_scatter[d - 1].start)

    def to_z(part):
        all_scatter[part].wait_recv()
        total = csum[rows_of(part, me), :].astype(F32)
        for d in range(1, GX):
            total = total + arrived[part][d].astype(F32)
        by_z[part][pl.ds(z, 1)] = total[None]
        for copy in over_z[part]:
            copy.start()
        if part == 0:

            @pl.when(me == 0)
            def _():
                all_bias_scatter.wait_recv()
                sums = csum[512:528, :].astype(F32)
                for d in range(1, GX):
                    sums = sums + rsbias[d].astype(F32)
                zbias[pl.ds(z, 1)] = sums[None]
                for copy in bias_z:
                    copy.start()

    def to_all(part):
        all_z[part].wait_recv()
        sums = by_z[part]
        total = (sums[0] + sums[1]) + (sums[2] + sums[3])
        ag[pl.ds(core, 1), rows_of(part, me), :] = total.astype(BF)[None]
        for copy in gathers[part]:
            copy.start()
        if part == 0:

            @pl.when(me == 0)
            def _():
                all_bias_z.wait_recv()
                sums = (zbias[0] + zbias[1]) + (zbias[2] + zbias[3])
                ag[pl.ds(core, 1), 512:528, :] = sums.astype(BF)[None]
                for copy in bias_gathers:
                    copy.start()

    def to_other_core(part):
        all_gathers[part].wait_recv()
        if part == 0:
            pl.when(me > 0)(bias_gathers[0].wait_recv)
        forwards[part].start()

    grads = dnt(xt[...], gp[...])
    for c in range(2):
        pwf[c, 0:528, :] = grads[:, c * HW : (c + 1) * HW]
    to_pair(0)

    w2v = w2[...]

    def segment_sums(b, carry):
        first = b * 256
        edge_hot = one_hot(mseg[:1, :], first, 256)
        high, low = split(dnt(edge_hot, hid[...]))
        node_hot = one_hot(id_row(segs, 0, N // 128), first, 256)
        part = dot(high, w2v) + dot(low, w2v) + dot(node_hot, nodes[...])
        for i in range(8):
            psum[b * 8 + i] = part[i * SR : (i + 1) * SR]
            psend[b * 8 + i] = part[i * SR : (i + 1) * SR].astype(BF)
        lines_t = line_t[:, block(b, 256)]
        add = dot(lines_t, high) + dot(lines_t, low)
        for c in range(2):
            pwf[c, 528:784, :] = pwf[c, 528:784, :] + add[:, c * HW : (c + 1) * HW]
        pl.when(b == 0)(functools.partial(to_members, 0))
        return carry

    pwf[:, 528:784, :] = jnp.zeros((2, 256, HW), F32)
    lax.fori_loop(0, SEG // 256, segment_sums, 0)
    to_pair(1)
    pools = [
        remote(
            psend.at[peers[d]],
            precv.at[d],
            p_s,
            p_r,
            {"gx": peers[d]},
        )
        for d in range(1, GX)
    ]
    def input_grads(b, carry):
        grads = dot(w1[...], gp[:, block(b)]).astype(BF)
        gi[:, block(b)] = grads[F:]
        for k in range(W // T):
            gis[b * (W // T) + k] = grads[:F, k * T : (k + 1) * T]
        return carry

    lax.fori_loop(0, E // W, input_grads, 0)
    to_members(1)
    to_z(0)
    for copy in pools:
        copy.start()

    def source_sums(g, carry):
        total = run[...]
        for k in range(5):
            p = g * 5 + k
            run_of, tile_of, earlier, hot = meeting(p)
            same = planned(earlier, 1, TILES) == tile_of
            total = jnp.where(same, total, 0.0) + dnt(hot, gis[run_of])
            sums_s[p] = total
        run[...] = total
        return carry

    run[...] = jnp.zeros_like(run)
    lax.fori_loop(0, STEPS // 5, source_sums, 0)

    for j in range(2):
        slots = sums_s[planned(33, N // T + j, STEPS)].astype(BF)
        gslot[2 * j] = slots[:NB]
        gslot[2 * j + 1] = slots[NB:]
    back = (
        remote(gslot.at[0], gret.at[0], g_s.at[0], g_r.at[0], {"gx": lax.rem(me + GX - 1, GX)}),
        remote(gslot.at[1], gret.at[1], g_s.at[1], g_r.at[1], {"gx": lax.rem(me + 1, GX)}),
        remote(gslot.at[2], gret.at[2], g_s.at[2], g_r.at[2], {"gy": lax.rem(my + GY - 1, GY)}),
        remote(gslot.at[3], gret.at[3], g_s.at[3], g_r.at[3], {"gy": lax.rem(my + 1, GY)}),
    )
    for k in range(4):
        pl.when(there[k])(back[k].start)

    def own(b, carry):
        first = b * 512
        s = jnp.concatenate(
            [sums_s[planned(33, b * 2 + k, STEPS)] for k in range(2)], axis=0
        )
        t = dnt(one_hot(id_row(tgt, 0, 32), first, 512), gi[...])
        acc[block(b, 512), :] = s + t

        @pl.when(b == 0)
        def _():
            to_z(1)
            to_all(0)

        pl.when(b == 1)(functools.partial(to_all, 1))
        return carry

    lax.fori_loop(0, N // 512, own, 0)

    ret = jnp.zeros((NB, F), F32)
    for k, here in enumerate((there[1], there[0], there[3], there[2])):
        pl.when(here)(back[k].wait_recv)

        @pl.when(jnp.logical_not(here))
        def _(k=k):
            gret[k] = jnp.zeros((NB, F), BF)

        ret = ret + gret[k].astype(F32)
    ret_parts = jnp.concatenate(split(ret), axis=0)
    lines = jnp.concatenate([line[g] for g in range(GX)], axis=0)
    seg_cols = jnp.transpose(segs[...].astype(F32)).astype(jnp.int32)
    stores = []
    for r in range(N // 128):
        rows = slice(r * 128, (r + 1) * 128)
        seg_hot = jnp.where(
            lax.broadcasted_iota(jnp.int32, (128, SEG), 1) == seg_cols[:, r : r + 1], 1.0, 0.0
        ).astype(BF)
        place_hot = one_hot(brows[...], r * 128, 128)
        place_hot = jnp.concatenate([place_hot, place_hot], axis=1)
        gnodes[rows, :] = (acc[rows, :] + dot(seg_hot, lines) + dot(place_hot, ret_parts)).astype(
            BF
        )
        if r % 4 == 3:
            done = pl.ds((r - 3) * 128, 512)
            stores.append(
                pltpu.make_async_copy(gnodes.at[done], gnodes_h.at[done], out_s.at[r // 4])
            )
            stores[-1].start()

    to_other_core(0)

    others = precv.at[pl.ds(1, GX - 1)]
    all_pools = remote(others, others, p_s, p_r, {"gx": me})
    all_pools.wait_recv()
    sums = psum[me]
    for d in range(1, GX):
        sums = sums + precv[d].astype(F32)
    pooled[...] = sums.astype(BF)
    stores.append(pltpu.make_async_copy(pooled, pooled_h, out_s.at[4]))
    stores[-1].start()

    to_other_core(1)
    for copy in forwards:
        copy.wait_recv()
    stores.append(pltpu.make_async_copy(ag, gw_h, out_s.at[5]))
    stores[-1].start()

    for k in range(4):
        pl.when(there[k])(halo[k].wait_send)
        pl.when(there[k])(back[k].wait_send)
    for group in ([all_cots, all_pools], pair, all_scatter, all_z, all_gathers, forwards):
        for copy in group:
            copy.wait_send()
    pl.when(me > 0)(bias_scatter[0].wait_send)

    @pl.when(me == 0)
    def _():
        all_bias_z.wait_send()
        all_bias_gathers.wait_send()

    for copy in stores:
        copy.wait()


def finish(
    scale,
    pooled,
    gnodes,
    gw,
    pooled_o,
    gnodes_o,
    first_o,
    bias_o,
    second_o,
    pooled_v,
    gnodes_v,
    gw_v,
    first_v,
    bias_v,
    second_v,
    sems,
):
    def move(source, target, number):
        copy = pltpu.make_async_copy(source, target, sems.at[number])
        copy.start()
        return copy

    coming = [move(gw.at[c], gw_v.at[c], c) for c in range(2)]
    parts = [pl.ds(i * (N // 2), N // 2) for i in range(2)]
    rows = [move(gnodes.at[part], gnodes_v.at[part], 2 + i) for i, part in enumerate(parts)]
    small = move(pooled, pooled_v, 4)
    unit = eye(HW)
    going = []
    for c in range(2):
        half = slice(c * HW, (c + 1) * HW)
        coming[c].wait()
        first_v[:, half] = gw_v[c, 0:512, :].astype(F32) * scale
        bias_v[:, half] = gw_v[c, 512:528, :].astype(F32)[:1] * scale
        second_v[half, :] = dnt(unit, gw_v[c, 528:784, :]) * scale
        place = pl.ds(c * HW, HW)
        going.append(move(second_v.at[place], second_o.at[place], 5 + c))
        going.append(move(first_v.at[:, place], first_o.at[:, place], 7 + c))
    going.append(move(bias_v, bias_o, 12))
    for i, part in enumerate(parts):
        rows[i].wait()
        going.append(move(gnodes_v.at[part], gnodes_o.at[part], 9 + i))
    small.wait()
    going.append(move(pooled_v, pooled_o, 11))
    for copy in going:
        copy.wait()


def local(nodes, brows, src, tgt, mask, segs, w1, b1, w2, cot):
    dma = pltpu.SemaphoreType.DMA
    int32 = jnp.int32
    arguments = (
        nodes,
        brows.reshape(1, NB),
        src,
        tgt,
        mask,
        segs.reshape(N // 128, 128),
        w1,
        b1.reshape(1, H),
        w2,
        cot,
    )
    scratch = [pltpu.VMEM(a.shape, a.dtype) for a in arguments]
    scratch += [
        pltpu.VMEM((SR, F), BF),
        pltpu.VMEM((N, F), BF),
        pltpu.VMEM((F, N), BF),
        pltpu.VMEM((TILES, F, T), BF),
        pltpu.VMEM((32, 128), int32),
        pltpu.VMEM((40, 128), int32),
        pltpu.SMEM((40, 128), int32),
        pltpu.VMEM((STEPS, F, T), BF),
        pltpu.VMEM((RUNS, F, T), BF),
        pltpu.VMEM((STEPS, T, F), F32),
        pltpu.VMEM((T, F), F32),
        pltpu.VMEM((H, 2 * F), BF),
        pltpu.VMEM((H, 128), F32),
        pltpu.VMEM((F, NB), BF),
        pltpu.VMEM((4, F, NB), BF),
        pltpu.VMEM((GX, SR, F), BF),
        pltpu.VMEM((F, SEG), BF),
        pltpu.VMEM((2 * F + 16, E), BF),
        pltpu.VMEM((8, E), int32),
        pltpu.VMEM((H, E), BF),
        pltpu.VMEM((H, E), BF),
        pltpu.VMEM((F, E), BF),
        pltpu.VMEM((2, PW, HW), F32),
        pltpu.VMEM((2, PW, HW), BF),
        pltpu.VMEM((PW, HW), BF),
        pltpu.VMEM((PW, HW), BF),
        pltpu.VMEM((GX, 32, HW), BF),
        pltpu.VMEM((GX, 16, HW), BF),
        pltpu.VMEM((GX, 16, HW), BF),
        pltpu.VMEM((4, 32, HW), F32),
        pltpu.VMEM((4, 16, HW), F32),
        pltpu.VMEM((4, 16, HW), F32),
        pltpu.VMEM((2, PW, HW), BF),
        pltpu.VMEM((GX, SR, F), F32),
        pltpu.VMEM((GX, SR, F), BF),
        pltpu.VMEM((GX, SR, F), BF),
        pltpu.VMEM((4, NB, F), BF),
        pltpu.VMEM((4, NB, F), BF),
        pltpu.VMEM((N, F), F32),
        dma((10,)),
        dma((6,)),
        dma,
    ]
    scratch += [
        dma((4,)),
        dma((4,)),
        dma,
        dma,
        dma,
        dma,
        dma((4,)),
        dma((4,)),
        dma((2,)),
        dma((2,)),
        dma((2,)),
        dma((2,)),
        dma,
        dma,
        dma((2,)),
        dma((2,)),
        dma,
        dma,
        dma((2,)),
        dma((2,)),
        dma,
        dma,
        dma((2,)),
        dma((2,)),
    ]
    anywhere = pl.BlockSpec(memory_space=pl.ANY)
    outs = (
        jax.ShapeDtypeStruct((SR, F), BF),
        jax.ShapeDtypeStruct((N, F), BF),
    )
    pooled, gnodes, gw = pl.pallas_call(
        kernel,
        out_shape=(*outs, jax.ShapeDtypeStruct((2, PW, HW), BF)),
        in_specs=[anywhere] * 10,
        out_specs=(anywhere,) * 3,
        scratch_shapes=scratch,
        compiler_params=pltpu.CompilerParams(
            collective_id=0, has_side_effects=True, vmem_limit_bytes=60 * 2**20
        ),
    )(*arguments)
    pooled, gnodes, first, bias, second = pl.pallas_call(
        functools.partial(finish, float((E * GX * GY) ** -0.5)),
        out_shape=(
            *outs,
            jax.ShapeDtypeStruct((H, H), F32),
            jax.ShapeDtypeStruct((1, H), F32),
            jax.ShapeDtypeStruct((H, F), F32),
        ),
        in_specs=[anywhere] * 3,
        out_specs=(anywhere,) * 5,
        scratch_shapes=[
            pltpu.VMEM((SR, F), BF),
            pltpu.VMEM((N, F), BF),
            pltpu.VMEM((2, PW, HW), BF),
            pltpu.VMEM((H, H), F32),
            pltpu.VMEM((1, H), F32),
            pltpu.VMEM((H, F), F32),
            dma((13,)),
        ],
        compiler_params=pltpu.CompilerParams(vmem_limit_bytes=60 * 2**20),
    )(pooled, gnodes, gw)
    return pooled, gnodes, first, bias.reshape(H), second


def solution(mesh):
    in_specs = (
        P(("gx", "gy"), None),
        P(("gx", "gy")),
        P(("gx", "gy"), None),
        P(("gx", "gy"), None),
        P(("gx", "gy"), None),
        P(("gx", "gy")),
        P(),
        P(),
        P(),
        P(("gx", "gy"), None),
    )
    out_specs = (P(("gx", "gy"), None), P(("gx", "gy"), None), P(), P(), P())
    return jax.shard_map(local, mesh=mesh, in_specs=in_specs, out_specs=out_specs, check_vma=False)
```
